256 devices in a mesh: rep: 8 (over x_hi, y), shard: 32 (over x_lo, z, core).
Axes of the slice: x: 4 (x_hi: 2, x_lo: 2; x = x_hi * 2 + x_lo), y: 4, z: 8, core: 2. Of those that a mesh axis runs over, the one named last changes fastest.
Arguments:
- grads: float32 [8, 4, 1024, 8192], P('rep', None, 'shard')
- owner_slot: int32 [32], replicated, may hold values from 0 to 31, each once
- left_stat: float32 [32, 1024, 1024], P('shard', 'rep')
- right_stat: float32 [32, 1024, 1024], P('shard', 'rep')
- left_root: float32 [32, 1024, 1024], P('shard', 'rep')
- right_root: float32 [32, 1024, 1024], P('shard', 'rep')
- second_moment: float32 [32, 1024, 1024], P('shard', 'rep')
Outputs:
- direction: float32 [4, 1024, 8192], P(None, 'shard')
- left_new: float32 [32, 1024, 1024], P('shard', 'rep')
- right_new: float32 [32, 1024, 1024], P('shard', 'rep')
- moment_new: float32 [32, 1024, 1024], P('shard', 'rep')
The draws below stay inside these ranges and needn't reach their ends.
Inputs may be any that keep to these rules, and one draw needn't show every extreme that they name: Block b's state lies at slot owner_slot[b]; every slot holds one block; slot s belongs to index s // 1 of shard.
All inputs are finite; a program needn't handle non-finite values.
Results may differ from the reference program's by a relative error of at most 0.000098.
Values sent between devices are 32-bit elements; how exact they have to be, the bound alone decides.
No kernel may reach another device: no remote copies, remote signals or barrier semaphores. Data moves between devices by JAX's collectives and lax.ppermute only.
A program may use at most 128 MiB of HBM per device.

```python
import math
import jax
import jax.numpy as jnp
from jax import lax

BS = 1024
BR = 4
REPS = 8
NB = 32
BC = 8
COLS = 8192
N_REP = 8


def log_scales(key, shape):
    return jnp.exp(jax.random.uniform(key, shape, jnp.float32) * math.log(10.0)) / math.sqrt(10.0)


def draw_grads(key, part):
    key = jax.random.fold_in(key, 11)
    keys = jax.random.split(key, 3)
    row_scale = log_scales(keys[0], (BR, BS))[None, :, :, None]
    col_scale = log_scales(keys[1], (COLS,))[None, None, None, :]
    noise = jax.random.normal(keys[2], (REPS, BR, BS, COLS), jnp.float32)
    return 0.3 * noise * row_scale * col_scale


def symmetric(key, lowest, highest, spread):
    diag_key, off_key = jax.random.split(key)
    noise = jax.random.normal(off_key, (NB, BS, BS), jnp.float32)
    off_part = (noise + jnp.swapaxes(noise, 1, 2)) * (spread / math.sqrt(BS))
    diagonal = jnp.exp(jax.random.uniform(diag_key, (NB, BS), jnp.float32, math.log(lowest), math.log(highest)))
    return off_part + diagonal[:, :, None] * jnp.eye(BS, dtype=jnp.float32)[None, :, :]


def draw_left_stat(key, part):
    key = jax.random.fold_in(key, 21)
    return symmetric(key, 0.5, 2.0, 0.4)


def draw_right_stat(key, part):
    key = jax.random.fold_in(key, 22)
    return symmetric(key, 0.5, 2.0, 0.4)


def draw_left_root(key, part):
    key = jax.random.fold_in(key, 23)
    return symmetric(key, 0.3, 1.5, 0.3)


def draw_right_root(key, part):
    key = jax.random.fold_in(key, 24)
    return symmetric(key, 0.3, 1.5, 0.3)


def draw_second_moment(key, part):
    key = jax.random.fold_in(key, 31)
    base = jnp.exp(jax.random.uniform(key, (NB, BS, BS), jnp.float32, math.log(0.003), math.log(0.3)))
    position = jnp.arange(BS, dtype=jnp.float32) / (BS - 1)
    rising = 1.0 + 2.0 * position
    return base / rising[None, :, None]


def setup_inputs(seed: int = 0) -> dict:
    streams_of = jax.random.split(jax.random.key(seed), 8)
    return {
        "grads": draw_grads(jax.random.fold_in(streams_of[7], 71), 0),
        "owner_slot": jax.random.permutation(streams_of[1], NB).astype(jnp.int32),
        "left_stat": draw_left_stat(jax.random.fold_in(streams_of[7], 71), 0),
        "right_stat": draw_right_stat(jax.random.fold_in(streams_of[7], 71), 0),
        "left_root": draw_left_root(jax.random.fold_in(streams_of[7], 71), 0),
        "right_root": draw_right_root(jax.random.fold_in(streams_of[7], 71), 0),
        "second_moment": draw_second_moment(jax.random.fold_in(streams_of[7], 71), 0),
    }


HIGHEST = lax.Precision.HIGHEST
beta_two = 0.99
adam_eps = 1e-08
norm_eps = 1e-06

def per_block(operands):
    gradient, left_old, right_old, left_inv, right_inv, moment_old = operands
    left_next = beta_two * left_old + (1.0 - beta_two) * jnp.dot(gradient, gradient.T, precision=HIGHEST, preferred_element_type=jnp.float32)
    right_next = beta_two * right_old + (1.0 - beta_two) * jnp.dot(gradient.T, gradient, precision=HIGHEST, preferred_element_type=jnp.float32)
    moment_next = beta_two * moment_old + (1.0 - beta_two) * gradient * gradient
    adam_dir = gradient / (jnp.sqrt(moment_next) + adam_eps)
    mixed = jnp.dot(left_inv, gradient, precision=HIGHEST, preferred_element_type=jnp.float32)
    shampoo = jnp.dot(mixed, right_inv, precision=HIGHEST, preferred_element_type=jnp.float32)
    factor = jnp.sqrt(jnp.sum(adam_dir * adam_dir)) / (jnp.sqrt(jnp.sum(shampoo * shampoo)) + norm_eps)
    return (left_next, right_next, moment_next, shampoo * factor)

def reference(grads, owner_slot, left_stat, right_stat, left_root, right_root, second_moment):
    summed = lax.optimization_barrier(jnp.sum(grads, axis=0)) / N_REP
    blocks = summed.reshape(BR, BS, BC, BS).transpose(0, 2, 1, 3).reshape(NB, BS, BS)
    slot_block = jnp.zeros((NB,), jnp.int32).at[owner_slot].set(jnp.arange(NB, dtype=jnp.int32))
    ordered = jnp.take(blocks, slot_block, axis=0)
    left_new, right_new, moment_new, grafted = lax.map(per_block, (ordered, left_stat, right_stat, left_root, right_root, second_moment))
    direction = jnp.take(grafted, owner_slot, axis=0).reshape(BR, BC, BS, BS).transpose(0, 2, 1, 3).reshape(BR, BS, BC * BS)
    return (direction, left_new, right_new, moment_new)
```

```python
import functools

import jax
import jax.numpy as jnp
from jax import lax
from jax.experimental import pallas as pl
from jax.experimental.pallas import tpu as pltpu
from jax.sharding import PartitionSpec as P

beta_two = 0.99
adam_eps = 1e-08
norm_eps = 1e-06

XS, YS = 2, 4
LANES = 128
VMEM = pltpu.VMEM
PARAMS = pltpu.CompilerParams(vmem_limit_bytes=48 * 1024 * 1024)


def shift(value, dx, dy):
    pairs = [
        (r, ((r // YS + dx) % XS) * YS + (r % YS + dy) % YS) for r in range(XS * YS)
    ]
    return lax.ppermute(value, "rep", pairs)


def whole(n):
    return [pl.BlockSpec(memory_space=VMEM)] * n


def smem(n):
    return [pl.BlockSpec(memory_space=pltpu.SMEM)] * n


def place(pos_ref, x_rel, t):
    x = lax.rem(pos_ref[0] + x_rel, XS)
    y = lax.rem(pos_ref[1] + t + YS, YS)
    return x * YS + y


def split3(value):
    high = value.astype(jnp.bfloat16)
    low = (value - high.astype(jnp.float32)).astype(jnp.bfloat16)
    return high, low


def dot3(a, b, dims):
    dot = functools.partial(
        lax.dot_general, dimension_numbers=(dims, ((), ())), preferred_element_type=jnp.float32
    )
    return dot(a[0], b[0]) + (dot(a[0], b[1]) + dot(a[1], b[0]))


def cut_kernel(pos_ref, owner_ref, g_ref, keep_a, send_a, keep_b, send_b1, send_b2, send_b3):
    i = pl.program_id(0)
    half = keep_a.shape[2]
    block_cols = g_ref.shape[2] // (XS * YS * LANES)
    for j in range(block_cols):
        slot = owner_ref[i * block_cols + j]
        for x_rel in range(XS):
            for t in range(YS):
                column = (j * XS * YS + place(pos_ref, x_rel, t)) * LANES
                piece = g_ref[0, :, pl.ds(pl.multiple_of(column, LANES), LANES)]
                (keep_a, send_a)[x_rel][t, slot] = piece[:half]
                (keep_b, send_b1, send_b2, send_b3)[t][x_rel, slot] = piece[half:]


def cut(pos, owner_slot, own_rows, slots):
    block_rows, stripe, columns = own_rows.shape
    a = jax.ShapeDtypeStruct((YS, slots, stripe // 2, LANES), jnp.float32)
    b = jax.ShapeDtypeStruct((XS, slots, stripe // 2, LANES), jnp.float32)
    fixed = lambda i, *_: (0, 0, 0, 0)
    return pl.pallas_call(
        cut_kernel,
        grid_spec=pltpu.PrefetchScalarGridSpec(
            num_scalar_prefetch=2,
            grid=(block_rows,),
            in_specs=[pl.BlockSpec((1, stripe, columns), lambda i, *_: (i, 0, 0))],
            out_specs=[pl.BlockSpec(s.shape, fixed) for s in (a, a, b, b, b, b)],
        ),
        out_shape=(a, a, b, b, b, b),
        compiler_params=PARAMS,
    )(pos, owner_slot, own_rows)


def reduce_scatter(parts):
    keep_a, send_a, keep_b, *send_b = parts
    got_a = shift(send_a, 1, 0)
    got_b = [shift(send_b[t - 1], 0, t) for t in (1, 3, 2)]
    sum_a = [keep_a[t] + got_a[t] for t in range(YS)]
    sum_b = [keep_b[x] + got_b[0][x] + got_b[1][x] + got_b[2][x] for x in range(XS)]
    last_a = [shift(sum_a[t], 0, t) for t in (1, 3, 2)]
    last_b = shift(sum_b[1], 1, 0)
    return jnp.concatenate(
        [sum_a[0] + last_a[0] + last_a[1] + last_a[2], sum_b[0] + last_b], axis=1
    )


def gather(part_a, part_b):
    a = [part_a] + [shift(part_a, 0, t) for t in (1, 2, 3)]
    b_x = shift(part_b, 1, 0)
    a = a + [shift(v, 1, 0) for v in a]
    b = [part_b] + [shift(part_b, 0, t) for t in (1, 2, 3)]
    b = b + [b_x] + [shift(b_x, 0, t) for t in (1, 2, 3)]
    return a, b


def roots_kernel(left_ref, right_ref, after_ref, left_a, left_b, right_cut):
    half = left_a.shape[0]
    left_a[...] = left_ref[:half]
    left_b[...] = left_ref[half:]
    for k in range(XS * YS):
        right_cut[k] = right_ref[:, k * LANES : (k + 1) * LANES]


def roots(left_rows, right_rows, after):
    rows, size = left_rows.shape
    half = jax.ShapeDtypeStruct((rows // 2, size), jnp.float32)
    return pl.pallas_call(
        roots_kernel,
        in_specs=whole(2) + [pl.BlockSpec(memory_space=pl.ANY)],
        out_specs=whole(3),
        out_shape=(half, half, jax.ShapeDtypeStruct((XS * YS, rows, LANES), jnp.float32)),
        compiler_params=PARAMS,
    )(left_rows, right_rows, after)


def assemble(pos_ref, a_refs, b_refs, g):
    half = a_refs[0].shape[0]
    for n in range(XS * YS):
        k = place(pos_ref, n // YS, -(n % YS))
        columns = pl.ds(pl.multiple_of(k * LANES, LANES), LANES)
        g[:half, columns] = a_refs[n][...]
        g[half:, columns] = b_refs[n][...]


def shampoo_kernel(pos_ref, *refs):
    n = XS * YS
    g_a, g_b, l_a, l_b = refs[:n], refs[n : 2 * n], refs[2 * n : 3 * n], refs[3 * n : 4 * n]
    right_ref, second_ref, out_ref, moment_ref, g, left = refs[4 * n :]
    assemble(pos_ref, g_a, g_b, g)
    rows = second_ref.shape[0]
    half = rows // 2
    for m in range(n):
        k = place(pos_ref, m // YS, -(m % YS))
        left[pl.ds(pl.multiple_of(k * rows, rows), half), :] = l_a[m][...]
        left[pl.ds(pl.multiple_of(k * rows + half, half), half), :] = l_b[m][...]

    own = g[pl.ds(pl.multiple_of(place(pos_ref, 0, 0) * rows, rows), rows), :]
    moment = beta_two * second_ref[...] + (1.0 - beta_two) * own * own
    moment_ref[...] = moment
    adam = own / (jnp.sqrt(moment) + adam_eps)
    adam_part = jnp.sum(adam * adam)

    mixed = dot3(split3(g[...]), split3(right_ref[...]), ((1,), (0,)))
    result = dot3(split3(left[...]), split3(mixed), ((1,), (0,)))
    shampoo_part = jnp.sum(result * result)

    shards, message, _ = out_ref.shape
    stripe = result.shape[0] // shards
    row = lax.broadcasted_iota(jnp.int32, (message - stripe, LANES), 0)
    lane = lax.broadcasted_iota(jnp.int32, (message - stripe, LANES), 1)
    norms = jnp.where(row == 0, adam_part, jnp.where(row == 1, shampoo_part, 0.0))
    norms = jnp.where(lane == pos_ref[2], norms, 0.0)
    for s in range(shards):
        out_ref[s, :stripe] = result[s * stripe : (s + 1) * stripe]
        out_ref[s, stripe:] = norms


def shampoo(pos, g_parts, left_parts, right_cols, second, shards):
    rows, size = second.shape
    return pl.pallas_call(
        shampoo_kernel,
        in_specs=smem(1) + whole(4 * XS * YS + 2),
        out_specs=whole(2),
        out_shape=(
            jax.ShapeDtypeStruct((shards, size // shards + 8, LANES), jnp.float32),
            jax.ShapeDtypeStruct(second.shape, jnp.float32),
        ),
        scratch_shapes=[VMEM((size, size), jnp.float32), VMEM((size, size), jnp.float32)],
        compiler_params=PARAMS,
    )(pos, *g_parts[0], *g_parts[1], *left_parts[0], *left_parts[1], right_cols, second)


def stats_kernel(pos_ref, *refs):
    n = XS * YS
    left_ref, right_ref, left_out, right_out, g = refs[2 * n :]
    assemble(pos_ref, refs[:n], refs[n : 2 * n], g)
    rows = left_ref.shape[0]
    first = pl.multiple_of(place(pos_ref, 0, 0) * rows, rows)
    every = split3(g[...])
    own_rows = split3(g[pl.ds(first, rows), :])
    own_cols = split3(g[:, pl.ds(first, rows)])
    left_out[...] = beta_two * left_ref[...] + (1.0 - beta_two) * dot3(
        own_rows, every, ((1,), (1,))
    )
    right_out[...] = beta_two * right_ref[...] + (1.0 - beta_two) * dot3(
        own_cols, every, ((0,), (0,))
    )


def statistics(pos, g_parts, left, right):
    size = left.shape[1]
    return pl.pallas_call(
        stats_kernel,
        in_specs=smem(1) + whole(2 * XS * YS + 2),
        out_specs=whole(2),
        out_shape=(
            jax.ShapeDtypeStruct(left.shape, jnp.float32),
            jax.ShapeDtypeStruct(right.shape, jnp.float32),
        ),
        scratch_shapes=[VMEM((size, size), jnp.float32)],
        compiler_params=PARAMS,
        cost_estimate=pl.CostEstimate(
            flops=12 * left.shape[0] * size * size, bytes_accessed=24 * left.size, transcendentals=0
        ),
    )(pos, *g_parts[0], *g_parts[1], left, right)


def order_kernel(pos_ref, owner_ref, *refs):
    n = XS * YS
    a_refs, b_refs, out_ref = refs[:n], refs[n : 2 * n], refs[2 * n]
    stripe, columns = out_ref.shape[1:]
    half = stripe // 2
    block_cols = columns // (n * LANES)
    body = b_refs[0].shape[0]
    norms = a_refs[0][body:]
    for m in range(1, n):
        norms = norms + a_refs[m][body:]
    root = jnp.sqrt(norms)
    factors = root[0:1] / (root[1:2] + norm_eps)
    lane = lax.broadcasted_iota(jnp.int32, (1, LANES), 1)
    for j in range(block_cols):
        slot = owner_ref[pl.program_id(0) * block_cols + j]
        factor = jnp.sum(jnp.where(lane == slot, factors, 0.0))
        rows = pl.ds(pl.multiple_of(slot * half, half), half)
        for m in range(n):
            column = (j * n + place(pos_ref, m // YS, -(m % YS))) * LANES
            columns_m = pl.ds(pl.multiple_of(column, LANES), LANES)
            out_ref[0, :half, columns_m] = a_refs[m][rows] * factor
            out_ref[0, half:, columns_m] = b_refs[m][rows] * factor


def order(pos, owner_slot, a, b, shape):
    block_rows, stripe, columns = shape
    fixed = lambda i, *_: (0, 0)
    return pl.pallas_call(
        order_kernel,
        grid_spec=pltpu.PrefetchScalarGridSpec(
            num_scalar_prefetch=2,
            grid=(block_rows,),
            in_specs=[pl.BlockSpec(v.shape, fixed) for v in (*a, *b)],
            out_specs=pl.BlockSpec((1, stripe, columns), lambda i, *_: (i, 0, 0)),
        ),
        out_shape=jax.ShapeDtypeStruct(shape, jnp.float32),
        compiler_params=PARAMS,
    )(pos, owner_slot, *a, *b)


def per_device(grads, owner_slot, left_stat, right_stat, left_root, right_root, second_moment):
    replicas = lax.axis_size("rep")
    shards = lax.axis_size("shard")
    own_rows = grads[0]
    stripe = own_rows.shape[1]
    size = stripe * shards
    rep = lax.axis_index("rep")
    pos = jnp.stack([rep // YS, rep % YS, lax.axis_index("shard")]).astype(jnp.int32)

    summed = reduce_scatter(cut(pos, owner_slot, own_rows, shards)) / replicas
    panel = lax.all_to_all(summed, "shard", 0, 0, tiled=True).reshape(size, LANES)

    left_a, left_b, right_cut = roots(left_root[0], right_root[0], summed)
    right_cols = lax.all_to_all(right_cut, "rep", 0, 0, tiled=True).reshape(size, LANES)
    left_parts = gather(left_a, left_b)

    g_parts = gather(panel[: size // 2], panel[size // 2 :])
    message, moment_new = shampoo(
        pos, g_parts, left_parts, right_cols, second_moment[0], shards
    )
    left_new, right_new = statistics(pos, g_parts, left_stat[0], right_stat[0])

    back = lax.all_to_all(message, "shard", 0, 0, tiled=True)
    half = stripe // 2
    first = jnp.concatenate(
        [back[:, :half].reshape(-1, LANES), jnp.sum(back[:, stripe:], axis=0)], axis=0
    )
    a, b = gather(first, back[:, half:stripe].reshape(-1, LANES))
    direction = order(pos, owner_slot, a, b, own_rows.shape)
    return (direction, left_new[None], right_new[None], moment_new[None])


def solution(mesh):
    return jax.shard_map(
        per_device,
        mesh=mesh,
        in_specs=(
            P("rep", None, "shard", None),
            P(),
            P("shard", "rep", None),
            P("shard", "rep", None),
            P("shard", "rep", None),
            P("shard", "rep", None),
            P("shard", "rep", None),
        ),
        out_specs=(
            P(None, "shard", None),
            P("shard", "rep", None),
            P("shard", "rep", None),
            P("shard", "rep", None),
        ),
        check_vma=False,
    )
```

```python
import functools

import jax
import jax.numpy as jnp
from jax import lax
from jax.experimental import pallas as pl
from jax.experimental.pallas import tpu as pltpu
from jax.sharding import PartitionSpec as P

beta_two = 0.99
adam_eps = 1e-08
norm_eps = 1e-06

XS, YS = 2, 4
LANES = 128
VMEM = pltpu.VMEM
PARAMS = pltpu.CompilerParams(vmem_limit_bytes=48 * 1024 * 1024)


def shift(value, dx, dy):
    pairs = [
        (r, ((r // YS + dx) % XS) * YS + (r % YS + dy) % YS) for r in range(XS * YS)
    ]
    return lax.ppermute(value, "rep", pairs)


def whole(n):
    return [pl.BlockSpec(memory_space=VMEM)] * n


def smem(n):
    return [pl.BlockSpec(memory_space=pltpu.SMEM)] * n


def place(pos_ref, x_rel, t):
    x = lax.rem(pos_ref[0] + x_rel, XS)
    y = lax.rem(pos_ref[1] + t + YS, YS)
    return x * YS + y


def split3(value):
    high = value.astype(jnp.bfloat16)
    low = (value - high.astype(jnp.float32)).astype(jnp.bfloat16)
    return high, low


def dot3(a, b, dims):
    dot = functools.partial(
        lax.dot_general, dimension_numbers=(dims, ((), ())), preferred_element_type=jnp.float32
    )
    return dot(a[0], b[0]) + (dot(a[0], b[1]) + dot(a[1], b[0]))


def cut_kernel(pos_ref, owner_ref, g_ref, *outs):
    keep_a, send_a, keep_b, send_b = outs[0], outs[1:5], outs[5], outs[6:9]
    i = pl.program_id(0)
    split = keep_a.shape[1]
    block_cols = g_ref.shape[2] // (XS * YS * LANES)

    def piece(j, x_rel, t):
        column = (j * XS * YS + place(pos_ref, x_rel, t)) * LANES
        return g_ref[0, :, pl.ds(pl.multiple_of(column, LANES), LANES)]

    for j in range(block_cols):
        slot = owner_ref[i * block_cols + j]

        @pl.when(slot < split)
        def _():
            for t in range(YS):
                keep_a[t, slot] = piece(j, 0, t)
                send_a[t][slot] = piece(j, 1, t)

        @pl.when(slot >= split)
        def _():
            for x_rel in range(XS):
                keep_b[x_rel, slot - split] = piece(j, x_rel, 0)
                for t in range(1, YS):
                    send_b[t - 1][x_rel, slot - split] = piece(j, x_rel, t)


def cut(pos, owner_slot, own_rows, slots):
    block_rows, stripe, columns = own_rows.shape
    split = (slots * 19) // 32
    shapes = [(YS, split, stripe, LANES)] + [(split, stripe, LANES)] * YS
    shapes += [(XS, slots - split, stripe, LANES)] * YS
    fixed = lambda n: lambda i, *_: (0,) * n
    return pl.pallas_call(
        cut_kernel,
        grid_spec=pltpu.PrefetchScalarGridSpec(
            num_scalar_prefetch=2,
            grid=(block_rows,),
            in_specs=[pl.BlockSpec((1, stripe, columns), lambda i, *_: (i, 0, 0))],
            out_specs=[pl.BlockSpec(s, fixed(len(s))) for s in shapes],
        ),
        out_shape=[jax.ShapeDtypeStruct(s, jnp.float32) for s in shapes],
        compiler_params=PARAMS,
    )(pos, owner_slot, own_rows)


def reduce_scatter(parts):
    keep_a, send_a, keep_b, send_b = parts[0], parts[1:5], parts[5], parts[6:9]
    got_b = [shift(send_b[t - 1], 0, t) for t in (1, 3, 2)]
    got_a = {t: shift(send_a[t], 1, 0) for t in (2, 1, 3, 0)}
    sum_a = {t: keep_a[t] + got_a[t] for t in (2, 1, 3, 0)}
    last_a = [shift(sum_a[t], 0, t) for t in (2, 1, 3)]
    sum_b = [keep_b[x] + got_b[0][x] + got_b[1][x] + got_b[2][x] for x in (1, 0)]
    last_b = shift(sum_b[0], 1, 0)
    total = jnp.concatenate(
        [sum_a[0] + last_a[0] + last_a[1] + last_a[2], sum_b[1] + last_b], axis=0
    )
    return total, sum_a[3]


def gather(part_a, part_b):
    a = [part_a] + [shift(part_a, 0, t) for t in (1, 2, 3)]
    b_x = shift(part_b, 1, 0)
    a = a + [shift(v, 1, 0) for v in a]
    b = [part_b] + [shift(part_b, 0, t) for t in (1, 2, 3)]
    b = b + [b_x] + [shift(b_x, 0, t) for t in (1, 2, 3)]
    return a, b


def roots_kernel(pos_ref, left_ref, right_ref, after_ref, left_own, right_own, right_other, *along_y):
    half = right_own.shape[1]
    rows = left_own.shape[0] // XS
    for x_rel, out in ((0, right_own), (1, right_other)):
        first = lax.rem(pos_ref[0] + x_rel, XS) * half
        out[...] = right_ref[:, pl.ds(pl.multiple_of(first, half), half)]
    stripes = left_ref.shape[0] // (YS * 8)
    for t in range(YS):
        y = lax.rem(pos_ref[1] + t, YS)
        out = left_own if t == 0 else along_y[t - 1]
        for n in range(stripes):
            first = pl.multiple_of((n * YS + y) * 8, 8)
            for x in range(XS):
                out[x * rows + n * 8 : x * rows + n * 8 + 8] = left_ref[
                    pl.ds(first, 8), x * half : (x + 1) * half
                ]
        if t:
            out[XS * rows :] = right_own[...]


def roots(pos, left_rows, right_rows, after):
    rows, size = left_rows.shape
    half = size // XS
    left = jax.ShapeDtypeStruct((rows // YS * XS, half), jnp.float32)
    right = jax.ShapeDtypeStruct((rows, half), jnp.float32)
    both = jax.ShapeDtypeStruct((rows // YS * XS + rows, half), jnp.float32)
    left_own, right_own, right_other, *along_y = pl.pallas_call(
        roots_kernel,
        in_specs=smem(1) + whole(2) + [pl.BlockSpec(memory_space=pl.ANY)],
        out_specs=whole(3 + YS - 1),
        out_shape=[left, right, right] + [both] * (YS - 1),
        compiler_params=PARAMS,
    )(pos, left_rows, right_rows, after)
    right_x = shift(right_other, 1, 0)
    got = [shift(along_y[t - 1], 0, t) for t in (1, 2, 3)]
    left_x = shift(jnp.concatenate([left_own] + [v[: left.shape[0]] for v in got]), 1, 0)
    forwarded = [shift(right_x, 0, t) for t in (1, 2, 3)]
    return (left_own, right_own, *got, left_x, right_x, *forwarded)


def blocks(arrays):
    return [pl.BlockSpec(v.shape, lambda i, n=v.ndim: (0,) * n) for v in arrays]


def assemble(pos_ref, a_refs, b_refs, store):
    split = a_refs[0].shape[0]
    for n in range(XS * YS):
        k = place(pos_ref, n // YS, -(n % YS))
        columns = pl.ds(pl.multiple_of(k * LANES, LANES), LANES)
        store(slice(0, split), columns, a_refs[n][...])
        store(slice(split, None), columns, b_refs[n][...])


def assemble_roots(pos_ref, refs, left, right):
    left_own, right_own, left_x, right_x = refs[0], refs[1], refs[5], refs[6]
    rows, half = left_own.shape[0] // XS, left_own.shape[1]
    for n in range(XS * YS):
        t = n % YS
        k = place(pos_ref, n // YS, -t)
        if n < YS:
            l_ref, l_first = (left_own if t == 0 else refs[1 + t]), 0
            r_ref, r_first = (right_own, 0) if t == 0 else (refs[1 + t], XS * rows)
        else:
            l_ref, l_first = left_x, t * XS * rows
            r_ref, r_first = (right_x if t == 0 else refs[6 + t]), 0
        for x in range(XS):
            left[pl.ds(pl.multiple_of(k * rows, rows), rows), x * half : (x + 1) * half] = l_ref[
                l_first + x * rows : l_first + (x + 1) * rows
            ]
        r_rows = right_own.shape[0]
        right[pl.ds(pl.multiple_of(k * r_rows, r_rows), r_rows), :] = r_ref[
            r_first : r_first + r_rows
        ]


def shampoo_kernel(pos_ref, *refs):
    n = XS * YS
    g_a, g_b, root_refs = refs[:n], refs[n : 2 * n], refs[2 * n : 3 * n + 2]
    second_ref, out_ref, moment_ref, high, low, left, right, own = refs[3 * n + 2 :]

    def store(rows, columns, value):
        high[rows, columns], low[rows, columns] = split3(value)

    assemble(pos_ref, g_a, g_b, store)
    assemble_roots(pos_ref, root_refs, left, right)

    rows = second_ref.shape[0]
    mine = place(pos_ref, 0, 0)
    parts_a = g_a[0].shape[0] // rows
    for refs_part, first, here in (
        (g_a, mine, mine < parts_a),
        (g_b, mine - parts_a, mine >= parts_a),
    ):

        @pl.when(here)
        def _():
            for m in range(n):
                k = place(pos_ref, m // YS, -(m % YS))
                own[:, pl.ds(pl.multiple_of(k * LANES, LANES), LANES)] = refs_part[m][
                    pl.ds(pl.multiple_of(first * rows, rows), rows), :
                ]

    moment = beta_two * second_ref[...] + (1.0 - beta_two) * own[...] * own[...]
    moment_ref[...] = moment
    adam = own[...] / (jnp.sqrt(moment) + adam_eps)
    adam_part = jnp.sum(adam * adam)

    mixed = dot3((high[...], low[...]), split3(right[...]), ((1,), (0,)))
    result = dot3(split3(left[...]), split3(mixed), ((1,), (0,)))
    shampoo_part = jnp.sum(result * result)

    shards, per, _ = out_ref.shape
    width = result.shape[1]
    row = lax.broadcasted_iota(jnp.int32, (per, LANES), 0)
    lane = lax.broadcasted_iota(jnp.int32, (per, LANES), 1)
    norms = jnp.where(row == 0, adam_part, jnp.where(row == 1, shampoo_part, 0.0))
    norms = jnp.where(lane == pos_ref[2], norms, 0.0)
    out_ref[:, :, :width] = result.reshape(shards, per, width)
    out_ref[:, :, width:] = jnp.broadcast_to(norms[None], (shards, per, LANES))


def shampoo(pos, g_parts, root_parts, second, shards):
    rows, size = second.shape
    half, per = size // XS, size // shards // YS
    outs = (
        jax.ShapeDtypeStruct((shards, per, half + LANES), jnp.float32),
        jax.ShapeDtypeStruct(second.shape, jnp.float32),
    )
    arrays = (*g_parts[0], *g_parts[1], *root_parts, second)
    return pl.pallas_call(
        shampoo_kernel,
        grid=(1,),
        in_specs=smem(1) + blocks(arrays),
        out_specs=blocks(outs),
        out_shape=outs,
        scratch_shapes=[
            VMEM((size, size), jnp.bfloat16),
            VMEM((size, size), jnp.bfloat16),
            VMEM((size // YS, size), jnp.float32),
            VMEM((size, half), jnp.float32),
            VMEM((rows, size), jnp.float32),
        ],
        compiler_params=PARAMS,
    )(pos, *arrays)


def stats_kernel(pos_ref, *refs):
    n = XS * YS
    left_ref, right_ref, left_out, right_out, g = refs[2 * n :]

    def store(rows, columns, value):
        g[rows, columns] = value

    assemble(pos_ref, refs[:n], refs[n : 2 * n], store)
    rows = left_ref.shape[0]
    first = pl.multiple_of(place(pos_ref, 0, 0) * rows, rows)
    every = split3(g[...])
    own_rows = split3(g[pl.ds(first, rows), :])
    own_cols = split3(g[:, pl.ds(first, rows)])
    left_out[...] = beta_two * left_ref[...] + (1.0 - beta_two) * dot3(
        own_rows, every, ((1,), (1,))
    )
    right_out[...] = beta_two * right_ref[...] + (1.0 - beta_two) * dot3(
        own_cols, every, ((0,), (0,))
    )


def statistics(pos, g_parts, left, right):
    size = left.shape[1]
    arrays = (*g_parts[0], *g_parts[1], left, right)
    outs = (
        jax.ShapeDtypeStruct(left.shape, jnp.float32),
        jax.ShapeDtypeStruct(right.shape, jnp.float32),
    )
    return pl.pallas_call(
        stats_kernel,
        grid=(1,),
        in_specs=smem(1) + blocks(arrays),
        out_specs=blocks(outs),
        out_shape=outs,
        scratch_shapes=[VMEM((size, size), jnp.float32)],
        compiler_params=PARAMS,
        cost_estimate=pl.CostEstimate(
            flops=12 * left.shape[0] * size * size, bytes_accessed=24 * left.size, transcendentals=0
        ),
    )(pos, *arrays)


def order_kernel(pos_ref, owner_ref, *refs):
    n = XS * YS
    a_refs, b_refs, out_ref = refs[:n], refs[n : 2 * n], refs[2 * n]
    stripe, columns = out_ref.shape[1:]
    body, width = a_refs[0].shape
    per = b_refs[0].shape[0] - body
    block_cols = columns // (2 * XS * width)
    norms = b_refs[0][body:, :LANES]
    for m in range(1, n):
        norms = norms + b_refs[m][body:, :LANES]
    root = jnp.sqrt(norms)
    factors = root[0:1] / (root[1:2] + norm_eps)
    lane = lax.broadcasted_iota(jnp.int32, (1, LANES), 1)
    for j in range(block_cols):
        slot = owner_ref[pl.program_id(0) * block_cols + j]
        factor = jnp.sum(jnp.where(lane == slot, factors, 0.0))
        for m in range(n):
            x = lax.rem(pos_ref[0] + m // YS, XS)
            y = lax.rem(pos_ref[1] + YS - m % YS, YS)
            rows = pl.ds(pl.multiple_of(y * per, per), per)
            first = pl.multiple_of((j * XS + x) * 2 * width, 2 * width)
            source = pl.ds(pl.multiple_of(slot * per, per), per)
            out_ref[0, rows, pl.ds(first, width)] = a_refs[m][source] * factor
            out_ref[0, rows, pl.ds(pl.multiple_of(first + width, width), width)] = (
                b_refs[m][source] * factor
            )


def order(pos, owner_slot, a, b, shape):
    block_rows, stripe, columns = shape
    fixed = lambda n: lambda i, *_: (0,) * n
    return pl.pallas_call(
        order_kernel,
        grid_spec=pltpu.PrefetchScalarGridSpec(
            num_scalar_prefetch=2,
            grid=(block_rows,),
            in_specs=[pl.BlockSpec(v.shape, fixed(v.ndim)) for v in (*a, *b)],
            out_specs=pl.BlockSpec((1, stripe, columns), lambda i, *_: (i, 0, 0)),
        ),
        out_shape=jax.ShapeDtypeStruct(shape, jnp.float32),
        compiler_params=PARAMS,
    )(pos, owner_slot, *a, *b)


def per_device(grads, owner_slot, left_stat, right_stat, left_root, right_root, second_moment):
    replicas = lax.axis_size("rep")
    shards = lax.axis_size("shard")
    own_rows = grads[0]
    size = own_rows.shape[1] * shards
    rep = lax.axis_index("rep")
    pos = jnp.stack([rep // YS, rep % YS, lax.axis_index("shard")]).astype(jnp.int32)

    summed, under_way = reduce_scatter(cut(pos, owner_slot, own_rows, shards))
    panel = lax.all_to_all(summed / replicas, "shard", 0, 0, tiled=True).reshape(size, LANES)
    root_parts = roots(pos, left_root[0], right_root[0], under_way)

    split = size * 5 // 8
    g_parts = gather(panel[:split], panel[split:])
    message, moment_new = shampoo(pos, g_parts, root_parts, second_moment[0], shards)
    back = lax.all_to_all(message, "shard", 0, 0, tiled=True)
    left_new, right_new = statistics(pos, g_parts, left_stat[0], right_stat[0])

    width = (message.shape[2] - LANES) // 2
    norms = jnp.tile(jnp.sum(back[:, :, 2 * width :], axis=0), (1, width // LANES))
    part_a = back[:, :, :width].reshape(-1, width)
    part_b = back[:, :, width : 2 * width].reshape(-1, width)
    a, b = gather(part_a, jnp.concatenate([part_b, norms]))
    direction = order(pos, owner_slot, a, b, own_rows.shape)
    return (direction, left_new[None], right_new[None], moment_new[None])


def solution(mesh):
    return jax.shard_map(
        per_device,
        mesh=mesh,
        in_specs=(
            P("rep", None, "shard", None),
            P(),
            P("shard", "rep", None),
            P("shard", "rep", None),
            P("shard", "rep", None),
            P("shard", "rep", None),
            P("shard", "rep", None),
        ),
        out_specs=(
            P(None, "shard", None),
            P("shard", "rep", None),
            P("shard", "rep", None),
            P("shard", "rep", None),
        ),
        check_vma=False,
    )
```

```python
import functools

import jax
import jax.numpy as jnp
from jax import lax
from jax.experimental import pallas as pl
from jax.experimental.pallas import tpu as pltpu
from jax.sharding import PartitionSpec as P

beta_two = 0.99
adam_eps = 1e-08
norm_eps = 1e-06

XS, YS = 2, 4
LANES = 128
VMEM = pltpu.VMEM
PARAMS = pltpu.CompilerParams(vmem_limit_bytes=48 * 1024 * 1024)


def shift(value, dx, dy):
    pairs = [
        (r, ((r // YS + dx) % XS) * YS + (r % YS + dy) % YS) for r in range(XS * YS)
    ]
    return lax.ppermute(value, "rep", pairs)


def whole(n):
    return [pl.BlockSpec(memory_space=VMEM)] * n


def smem(n):
    return [pl.BlockSpec(memory_space=pltpu.SMEM)] * n


def place(pos_ref, x_rel, t):
    x = lax.rem(pos_ref[0] + x_rel, XS)
    y = lax.rem(pos_ref[1] + t + YS, YS)
    return x * YS + y


def split3(value):
    high = value.astype(jnp.bfloat16)
    low = (value - high.astype(jnp.float32)).astype(jnp.bfloat16)
    return high, low


def dot3(a, b, dims):
    dot = functools.partial(
        lax.dot_general, dimension_numbers=(dims, ((), ())), preferred_element_type=jnp.float32
    )
    return dot(a[0], b[0]) + (dot(a[0], b[1]) + dot(a[1], b[0]))


def cut_kernel(pos_ref, owner_ref, g_ref, *outs):
    keep_a, send_a, keep_b, send_b = outs[:4], outs[4:8], outs[8], outs[9:12]
    i = pl.program_id(0)
    split = keep_a[0].shape[0]
    block_cols = g_ref.shape[2] // (XS * YS * LANES)

    def piece(j, x_rel, t):
        column = (j * XS * YS + place(pos_ref, x_rel, t)) * LANES
        return g_ref[0, :, pl.ds(pl.multiple_of(column, LANES), LANES)]

    for j in range(block_cols):
        slot = owner_ref[i * block_cols + j]

        @pl.when(slot < split)
        def _():
            for t in range(YS):
                keep_a[t][slot] = piece(j, 0, t)
                send_a[t][slot] = piece(j, 1, t)

        @pl.when(slot >= split)
        def _():
            for x_rel in range(XS):
                keep_b[x_rel, slot - split] = piece(j, x_rel, 0)
                for t in range(1, YS):
                    send_b[t - 1][x_rel, slot - split] = piece(j, x_rel, t)


def cut(pos, owner_slot, own_rows, slots):
    block_rows, stripe, columns = own_rows.shape
    split = (slots * 19) // 32
    shapes = [(split, stripe, LANES)] * (2 * YS)
    shapes += [(XS, slots - split, stripe, LANES)] * YS
    fixed = lambda n: lambda i, *_: (0,) * n
    return pl.pallas_call(
        cut_kernel,
        grid_spec=pltpu.PrefetchScalarGridSpec(
            num_scalar_prefetch=2,
            grid=(block_rows,),
            in_specs=[pl.BlockSpec((1, stripe, columns), lambda i, *_: (i, 0, 0))],
            out_specs=[pl.BlockSpec(s, fixed(len(s))) for s in shapes],
        ),
        out_shape=[jax.ShapeDtypeStruct(s, jnp.float32) for s in shapes],
        compiler_params=PARAMS,
    )(pos, owner_slot, own_rows)


def blocks(arrays):
    return [pl.BlockSpec(v.shape, lambda i, n=v.ndim: (0,) * n) for v in arrays]


def unread(n):
    return [pl.BlockSpec(memory_space=pl.ANY)] * n


def add_kernel(keep, first, second, third, *refs):
    away, own = refs[-2:]
    for x, out in ((1, away), (0, own)):
        out[...] = keep[x] + first[x] + second[x] + third[x]


def add(keep, got, after):
    out = jax.ShapeDtypeStruct(keep.shape[1:], jnp.float32)
    arrays = (keep, *got)
    return pl.pallas_call(
        add_kernel,
        grid=(1,),
        in_specs=blocks(arrays) + unread(len(after)),
        out_specs=blocks((out, out)),
        out_shape=(out, out),
        compiler_params=PARAMS,
    )(*arrays, *after)


def total_kernel(scale, a0, a1, a2, a3, b0, b1, *refs):
    out = refs[-1]
    split = a0.shape[0]
    out[:split] = (a0[...] + a1[...] + a2[...] + a3[...]) * scale
    out[split:] = (b0[...] + b1[...]) * scale


def total(scale, a, b, after):
    slots = a[0].shape[0] + b[0].shape[0]
    out = jax.ShapeDtypeStruct((slots, *a[0].shape[1:]), jnp.float32)
    arrays = (*a, *b)
    return pl.pallas_call(
        functools.partial(total_kernel, scale),
        grid=(1,),
        in_specs=blocks(arrays) + unread(len(after)),
        out_specs=blocks((out,))[0],
        out_shape=out,
        compiler_params=PARAMS,
    )(*arrays, *after)


def reduce_scatter(parts):
    keep_a, send_a, keep_b, send_b = parts[:4], parts[4:8], parts[8], parts[9:12]
    got_a = {t: shift(send_a[t], 1, 0) for t in (2, 1, 3, 0)}
    got_b = [shift(send_b[t - 1], 0, t) for t in (1, 3, 2)]
    sum_a = {t: keep_a[t] + got_a[t] for t in (2, 1, 3, 0)}
    last_a = {t: shift(sum_a[t], 0, t) for t in (2, 1, 3)}
    away, own = add(keep_b, got_b, (sum_a[2], sum_a[1]))
    last_b = shift(away, 1, 0)
    return (sum_a[0], last_a[2], last_a[1], last_a[3]), (own, last_b), sum_a[3]


def gather(part_a, part_b):
    got = {("a", 0, 0): part_a, ("b", 0, 0): part_b}
    for t in (1, 3, 2):
        got["a", 0, t] = shift(part_a, 0, t)
    got["b", 1, 0] = shift(part_b, 1, 0)
    got["a", 1, 0] = shift(part_a, 1, 0)
    for t in (1, 3, 2):
        got["b", 0, t] = shift(part_b, 0, t)
    for t in (1, 3, 2):
        got["a", 1, t] = shift(got["a", 0, t], 1, 0)
        got["b", 1, t] = shift(got["b", 1, 0], 0, t)
    return got


LATEST_FIRST = (
    [(n, 1, t) for t in (2, 3, 1) for n in ("b", "a")]
    + [("b", 0, t) for t in (2, 3, 1)]
    + [("a", 1, 0), ("b", 1, 0)]
    + [("a", 0, t) for t in (2, 3, 1)]
    + [("b", 0, 0), ("a", 0, 0)]
)
PARTS = len(LATEST_FIRST)


def listed(got):
    return [got[key] for key in LATEST_FIRST]


def named(refs):
    got = dict(zip(LATEST_FIRST, refs))
    return tuple([got[n, x, t] for x in range(XS) for t in range(YS)] for n in ("a", "b"))


def roots_kernel(pos_ref, left_ref, right_ref, after_ref, left_own, right_own, right_other, *along_y):
    half = right_own.shape[1]
    rows = left_own.shape[0] // XS
    for x_rel, out in ((0, right_own), (1, right_other)):
        first = lax.rem(pos_ref[0] + x_rel, XS) * half
        out[...] = right_ref[:, pl.ds(pl.multiple_of(first, half), half)]
    stripes = left_ref.shape[0] // (YS * 8)
    for t in range(YS):
        y = lax.rem(pos_ref[1] + t, YS)
        out = left_own if t == 0 else along_y[t - 1]
        for n in range(stripes):
            first = pl.multiple_of((n * YS + y) * 8, 8)
            for x in range(XS):
                out[x * rows + n * 8 : x * rows + n * 8 + 8] = left_ref[
                    pl.ds(first, 8), x * half : (x + 1) * half
                ]
        if t:
            out[XS * rows :] = right_own[...]


def roots(pos, left_rows, right_rows, after):
    rows, size = left_rows.shape
    half = size // XS
    left = jax.ShapeDtypeStruct((rows // YS * XS, half), jnp.float32)
    right = jax.ShapeDtypeStruct((rows, half), jnp.float32)
    both = jax.ShapeDtypeStruct((rows // YS * XS + rows, half), jnp.float32)
    left_own, right_own, right_other, *along_y = pl.pallas_call(
        roots_kernel,
        in_specs=smem(1) + whole(2) + [pl.BlockSpec(memory_space=pl.ANY)],
        out_specs=whole(3 + YS - 1),
        out_shape=[left, right, right] + [both] * (YS - 1),
        compiler_params=PARAMS,
    )(pos, left_rows, right_rows, after)
    right_x = shift(right_other, 1, 0)
    got = [shift(along_y[t - 1], 0, t) for t in (1, 2, 3)]
    forwarded = [shift(right_x, 0, t) for t in (1, 2, 3)]
    left_x = shift(jnp.concatenate([left_own] + [v[: left.shape[0]] for v in got]), 1, 0)
    return (left_x, *forwarded, *got, right_x, left_own, right_own), right_x


def assemble(pos_ref, a_refs, b_refs, store):
    split = a_refs[0].shape[0]
    for n in range(XS * YS):
        k = place(pos_ref, n // YS, -(n % YS))
        columns = pl.ds(pl.multiple_of(k * LANES, LANES), LANES)
        store(slice(0, split), columns, a_refs[n][...])
        store(slice(split, None), columns, b_refs[n][...])


def assemble_roots(pos_ref, refs, left, right):
    left_x, forwarded, got, right_x, left_own, right_own = refs[0], refs[1:4], refs[4:7], *refs[7:]
    rows, half = left_own.shape[0] // XS, left_own.shape[1]
    for n in range(XS * YS):
        t = n % YS
        k = place(pos_ref, n // YS, -t)
        if n < YS:
            l_ref, l_first = (left_own if t == 0 else got[t - 1]), 0
            r_ref, r_first = (right_own, 0) if t == 0 else (got[t - 1], XS * rows)
        else:
            l_ref, l_first = left_x, t * XS * rows
            r_ref, r_first = (right_x if t == 0 else forwarded[t - 1]), 0
        for x in range(XS):
            left[pl.ds(pl.multiple_of(k * rows, rows), rows), x * half : (x + 1) * half] = l_ref[
                l_first + x * rows : l_first + (x + 1) * rows
            ]
        r_rows = right_own.shape[0]
        right[pl.ds(pl.multiple_of(k * r_rows, r_rows), r_rows), :] = r_ref[
            r_first : r_first + r_rows
        ]


def shampoo_kernel(pos_ref, *refs):
    n = XS * YS
    (g_a, g_b), root_refs = named(refs[:PARTS]), refs[PARTS : PARTS + n + 2]
    second_ref, out_ref, moment_ref, high, low, left, right, own = refs[PARTS + n + 2 :]

    def store(rows, columns, value):
        high[rows, columns], low[rows, columns] = split3(value)

    assemble(pos_ref, g_a, g_b, store)
    assemble_roots(pos_ref, root_refs, left, right)

    rows = second_ref.shape[0]
    mine = place(pos_ref, 0, 0)
    parts_a = g_a[0].shape[0] // rows
    for refs_part, first, here in (
        (g_a, mine, mine < parts_a),
        (g_b, mine - parts_a, mine >= parts_a),
    ):

        @pl.when(here)
        def _():
            for m in range(n):
                k = place(pos_ref, m // YS, -(m % YS))
                own[:, pl.ds(pl.multiple_of(k * LANES, LANES), LANES)] = refs_part[m][
                    pl.ds(pl.multiple_of(first * rows, rows), rows), :
                ]

    moment = beta_two * second_ref[...] + (1.0 - beta_two) * own[...] * own[...]
    moment_ref[...] = moment
    adam = own[...] / (jnp.sqrt(moment) + adam_eps)
    adam_part = jnp.sum(adam * adam)

    mixed = dot3((high[...], low[...]), split3(right[...]), ((1,), (0,)))
    result = dot3(split3(left[...]), split3(mixed), ((1,), (0,)))
    shampoo_part = jnp.sum(result * result)

    shards, per, _ = out_ref.shape
    width = result.shape[1]
    row = lax.broadcasted_iota(jnp.int32, (per, LANES), 0)
    lane = lax.broadcasted_iota(jnp.int32, (per, LANES), 1)
    norms = jnp.where(row == 0, adam_part, jnp.where(row == 1, shampoo_part, 0.0))
    norms = jnp.where(lane == pos_ref[2], norms, 0.0)
    out_ref[:, :, :width] = result.reshape(shards, per, width)
    out_ref[:, :, width:] = jnp.broadcast_to(norms[None], (shards, per, LANES))


def shampoo(pos, g_parts, root_parts, second, shards):
    rows, size = second.shape
    half, per = size // XS, size // shards // YS
    outs = (
        jax.ShapeDtypeStruct((shards, per, half + LANES), jnp.float32),
        jax.ShapeDtypeStruct(second.shape, jnp.float32),
    )
    arrays = (*listed(g_parts), *root_parts, second)
    return pl.pallas_call(
        shampoo_kernel,
        grid=(1,),
        in_specs=smem(1) + blocks(arrays),
        out_specs=blocks(outs),
        out_shape=outs,
        scratch_shapes=[
            VMEM((size, size), jnp.bfloat16),
            VMEM((size, size), jnp.bfloat16),
            VMEM((size // YS, size), jnp.float32),
            VMEM((size, half), jnp.float32),
            VMEM((rows, size), jnp.float32),
        ],
        compiler_params=PARAMS,
    )(pos, *arrays)


def stats_kernel(pos_ref, *refs):
    left_ref, right_ref, left_out, right_out, g = refs[PARTS:]

    def store(rows, columns, value):
        g[rows, columns] = value

    assemble(pos_ref, *named(refs[:PARTS]), store)
    rows = left_ref.shape[0]
    first = pl.multiple_of(place(pos_ref, 0, 0) * rows, rows)
    every = split3(g[...])
    own_rows = split3(g[pl.ds(first, rows), :])
    own_cols = split3(g[:, pl.ds(first, rows)])
    left_out[...] = beta_two * left_ref[...] + (1.0 - beta_two) * dot3(
        own_rows, every, ((1,), (1,))
    )
    right_out[...] = beta_two * right_ref[...] + (1.0 - beta_two) * dot3(
        own_cols, every, ((0,), (0,))
    )


def statistics(pos, g_parts, left, right):
    size = left.shape[1]
    arrays = (*listed(g_parts), left, right)
    outs = (
        jax.ShapeDtypeStruct(left.shape, jnp.float32),
        jax.ShapeDtypeStruct(right.shape, jnp.float32),
    )
    return pl.pallas_call(
        stats_kernel,
        grid=(1,),
        in_specs=smem(1) + blocks(arrays),
        out_specs=blocks(outs),
        out_shape=outs,
        scratch_shapes=[VMEM((size, size), jnp.float32)],
        compiler_params=PARAMS,
        cost_estimate=pl.CostEstimate(
            flops=12 * left.shape[0] * size * size, bytes_accessed=24 * left.size, transcendentals=0
        ),
    )(pos, *arrays)


def order_kernel(pos_ref, owner_ref, *refs):
    n = XS * YS
    (a_refs, b_refs), out_ref = named(refs[:PARTS]), refs[PARTS]
    stripe, columns = out_ref.shape[1:]
    body, width = a_refs[0].shape
    per = b_refs[0].shape[0] - body
    block_cols = columns // (2 * XS * width)
    norms = b_refs[0][body:, :LANES]
    for m in range(1, n):
        norms = norms + b_refs[m][body:, :LANES]
    root = jnp.sqrt(norms)
    factors = root[0:1] / (root[1:2] + norm_eps)
    lane = lax.broadcasted_iota(jnp.int32, (1, LANES), 1)
    for j in range(block_cols):
        slot = owner_ref[pl.program_id(0) * block_cols + j]
        factor = jnp.sum(jnp.where(lane == slot, factors, 0.0))
        for m in range(n):
            x = lax.rem(pos_ref[0] + m // YS, XS)
            y = lax.rem(pos_ref[1] + YS - m % YS, YS)
            rows = pl.ds(pl.multiple_of(y * per, per), per)
            first = pl.multiple_of((j * XS + x) * 2 * width, 2 * width)
            source = pl.ds(pl.multiple_of(slot * per, per), per)
            out_ref[0, rows, pl.ds(first, width)] = a_refs[m][source] * factor
            out_ref[0, rows, pl.ds(pl.multiple_of(first + width, width), width)] = (
                b_refs[m][source] * factor
            )


def unpack_kernel(back_ref, *refs):
    part_a, part_b = refs[-2:]
    rows, width = part_a.shape
    part_a[...] = back_ref[:, :, :width].reshape(rows, width)
    part_b[:rows] = back_ref[:, :, width : 2 * width].reshape(rows, width)
    norms = jnp.sum(back_ref[:, :, 2 * width :], axis=0)
    for n in range(width // LANES):
        part_b[rows:, n * LANES : (n + 1) * LANES] = norms


def unpack(back, after):
    shards, per, size = back.shape
    width = (size - LANES) // 2
    outs = [
        jax.ShapeDtypeStruct((shards * per, width), jnp.float32),
        jax.ShapeDtypeStruct((shards * per + per, width), jnp.float32),
    ]
    return pl.pallas_call(
        unpack_kernel,
        grid=(1,),
        in_specs=blocks((back,)) + unread(len(after)),
        out_specs=blocks(outs),
        out_shape=outs,
        compiler_params=PARAMS,
    )(back, *after)


def order(pos, owner_slot, got, shape):
    block_rows, stripe, columns = shape
    fixed = lambda n: lambda i, *_: (0,) * n
    return pl.pallas_call(
        order_kernel,
        grid_spec=pltpu.PrefetchScalarGridSpec(
            num_scalar_prefetch=2,
            grid=(block_rows,),
            in_specs=[pl.BlockSpec(v.shape, fixed(v.ndim)) for v in listed(got)],
            out_specs=pl.BlockSpec((1, stripe, columns), lambda i, *_: (i, 0, 0)),
        ),
        out_shape=jax.ShapeDtypeStruct(shape, jnp.float32),
        compiler_params=PARAMS,
    )(pos, owner_slot, *listed(got))


def per_device(grads, owner_slot, left_stat, right_stat, left_root, right_root, second_moment):
    replicas = lax.axis_size("rep")
    shards = lax.axis_size("shard")
    own_rows = grads[0]
    size = own_rows.shape[1] * shards
    rep = lax.axis_index("rep")
    pos = jnp.stack([rep // YS, rep % YS, lax.axis_index("shard")]).astype(jnp.int32)

    a, b, under_way = reduce_scatter(cut(pos, owner_slot, own_rows, shards))
    root_parts, crossed = roots(pos, left_root[0], right_root[0], under_way)
    summed = total(1.0 / replicas, a, b, (crossed,))
    panel = lax.all_to_all(summed, "shard", 0, 0, tiled=True).reshape(size, LANES)

    split = size * 5 // 8
    g_parts = gather(panel[:split], panel[split:])
    message, moment_new = shampoo(pos, g_parts, root_parts, second_moment[0], shards)
    back = lax.all_to_all(message, "shard", 0, 0, tiled=True)
    left_new, right_new = statistics(pos, g_parts, left_stat[0], right_stat[0])

    parts = gather(*unpack(back, (left_new,)))
    direction = order(pos, owner_slot, parts, own_rows.shape)
    return (direction, left_new[None], right_new[None], moment_new[None])


def solution(mesh):
    return jax.shard_map(
        per_device,
        mesh=mesh,
        in_specs=(
            P("rep", None, "shard", None),
            P(),
            P("shard", "rep", None),
            P("shard", "rep", None),
            P("shard", "rep", None),
            P("shard", "rep", None),
            P("shard", "rep", None),
        ),
        out_specs=(
            P(None, "shard", None),
            P("shard", "rep", None),
            P("shard", "rep", None),
            P("shard", "rep", None),
        ),
        check_vma=False,
    )
```

```python
import functools

import jax
import jax.numpy as jnp
from jax import lax
from jax.experimental import pallas as pl
from jax.experimental.pallas import tpu as pltpu
from jax.sharding import PartitionSpec as P

beta_two = 0.99
adam_eps = 1e-08
norm_eps = 1e-06

XS, YS = 2, 4
LANES = 128
VMEM = pltpu.VMEM
PARAMS = pltpu.CompilerParams(vmem_limit_bytes=24 * 1024 * 1024)


def shift(value, dx, dy):
    pairs = [
        (r, ((r // YS + dx) % XS) * YS + (r % YS + dy) % YS) for r in range(XS * YS)
    ]
    return lax.ppermute(value, "rep", pairs)


def whole(n):
    return [pl.BlockSpec(memory_space=VMEM)] * n


def smem(n):
    return [pl.BlockSpec(memory_space=pltpu.SMEM)] * n


def place(pos_ref, x_rel, t):
    x = lax.rem(pos_ref[0] + x_rel, XS)
    y = lax.rem(pos_ref[1] + t + YS, YS)
    return x * YS + y


def split3(value):
    high = value.astype(jnp.bfloat16)
    low = (value - high.astype(jnp.float32)).astype(jnp.bfloat16)
    return high, low


def dot3(a, b, dims):
    dot = functools.partial(
        lax.dot_general, dimension_numbers=(dims, ((), ())), preferred_element_type=jnp.float32
    )
    return dot(a[0], b[0]) + (dot(a[0], b[1]) + dot(a[1], b[0]))


def cut_kernel(pos_ref, owner_ref, g_ref, *outs):
    keep_a, send_a, keep_b, send_b = outs[:4], outs[4:8], outs[8], outs[9:12]
    i = pl.program_id(0)
    split = keep_a[0].shape[0]
    block_cols = g_ref.shape[2] // (XS * YS * LANES)

    def piece(j, x_rel, t):
        column = (j * XS * YS + place(pos_ref, x_rel, t)) * LANES
        return g_ref[0, :, pl.ds(pl.multiple_of(column, LANES), LANES)]

    for j in range(block_cols):
        slot = owner_ref[i * block_cols + j]

        @pl.when(slot < split)
        def _():
            for t in range(YS):
                keep_a[t][slot] = piece(j, 0, t)
                send_a[t][slot] = piece(j, 1, t)

        @pl.when(slot >= split)
        def _():
            for x_rel in range(XS):
                keep_b[x_rel, slot - split] = piece(j, x_rel, 0)
                for t in range(1, YS):
                    send_b[t - 1][x_rel, slot - split] = piece(j, x_rel, t)


def cut(pos, owner_slot, own_rows, slots):
    block_rows, stripe, columns = own_rows.shape
    split = (slots * 19) // 32
    shapes = [(split, stripe, LANES)] * (2 * YS)
    shapes += [(XS, slots - split, stripe, LANES)] * YS
    fixed = lambda n: lambda i, *_: (0,) * n
    return pl.pallas_call(
        cut_kernel,
        grid_spec=pltpu.PrefetchScalarGridSpec(
            num_scalar_prefetch=2,
            grid=(block_rows,),
            in_specs=[pl.BlockSpec((1, stripe, columns), lambda i, *_: (i, 0, 0))],
            out_specs=[pl.BlockSpec(s, fixed(len(s))) for s in shapes],
        ),
        out_shape=[jax.ShapeDtypeStruct(s, jnp.float32) for s in shapes],
        compiler_params=PARAMS,
    )(pos, owner_slot, own_rows)


def unread(n):
    return [pl.BlockSpec(memory_space=pl.ANY)] * n


def add_kernel(keep, first, second, third, *refs):
    away, own = refs[-2:]
    for x, out in ((1, away), (0, own)):
        out[...] = keep[x] + first[x] + second[x] + third[x]


def add(keep, got, after):
    out = jax.ShapeDtypeStruct(keep.shape[1:], jnp.float32)
    arrays = (keep, *got)
    return pl.pallas_call(
        add_kernel,
        in_specs=whole(len(arrays)) + unread(len(after)),
        out_specs=whole(2),
        out_shape=(out, out),
        compiler_params=PARAMS,
    )(*arrays, *after)


def total_kernel(scale, a0, a1, a2, a3, b0, b1, *refs):
    out = refs[-1]
    split = a0.shape[0]
    out[:split] = (a0[...] + a1[...] + a2[...] + a3[...]) * scale
    out[split:] = (b0[...] + b1[...]) * scale


def total(scale, a, b, after):
    slots = a[0].shape[0] + b[0].shape[0]
    out = jax.ShapeDtypeStruct((slots, *a[0].shape[1:]), jnp.float32)
    arrays = (*a, *b)
    return pl.pallas_call(
        functools.partial(total_kernel, scale),
        in_specs=whole(len(arrays)) + unread(len(after)),
        out_specs=whole(1)[0],
        out_shape=out,
        compiler_params=PARAMS,
    )(*arrays, *after)


def reduce_scatter(parts):
    keep_a, send_a, keep_b, send_b = parts[:4], parts[4:8], parts[8], parts[9:12]
    got_a = {t: shift(send_a[t], 1, 0) for t in (2, 1, 3, 0)}
    got_b = [shift(send_b[t - 1], 0, t) for t in (1, 3, 2)]
    sum_a = {t: keep_a[t] + got_a[t] for t in (2, 1, 3, 0)}
    last_a = {t: shift(sum_a[t], 0, t) for t in (2, 1, 3)}
    away, own = add(keep_b, got_b, (sum_a[2], sum_a[1]))
    last_b = shift(away, 1, 0)
    return (sum_a[0], last_a[2], last_a[1], last_a[3]), (own, last_b), away


def gather(part_a, part_b):
    got = {("a", 0, 0): part_a, ("b", 0, 0): part_b}
    for t in (1, 3, 2):
        got["a", 0, t] = shift(part_a, 0, t)
    got["b", 1, 0] = shift(part_b, 1, 0)
    got["a", 1, 0] = shift(part_a, 1, 0)
    for t in (1, 3, 2):
        got["b", 0, t] = shift(part_b, 0, t)
    for t in (1, 3, 2):
        got["a", 1, t] = shift(got["a", 0, t], 1, 0)
        got["b", 1, t] = shift(got["b", 1, 0], 0, t)
    return got


LATEST_FIRST = (
    [(n, 1, t) for t in (2, 3, 1) for n in ("b", "a")]
    + [("b", 0, t) for t in (2, 3, 1)]
    + [("a", 1, 0), ("b", 1, 0)]
    + [("a", 0, t) for t in (2, 3, 1)]
    + [("b", 0, 0), ("a", 0, 0)]
)
PARTS = len(LATEST_FIRST)


def listed(got):
    return [got[key] for key in LATEST_FIRST]


def named(refs):
    got = dict(zip(LATEST_FIRST, refs))
    return tuple([got[n, x, t] for x in range(XS) for t in range(YS)] for n in ("a", "b"))


def roots_kernel(left_ref, right_ref, after_ref, left_out, right_cut):
    left_out[...] = left_ref[...]
    for k in range(XS * YS):
        right_cut[k] = right_ref[:, k * LANES : (k + 1) * LANES]


def roots(left_rows, right_rows, after):
    rows, size = left_rows.shape
    left, right = pl.pallas_call(
        roots_kernel,
        in_specs=whole(2) + unread(1),
        out_specs=whole(2),
        out_shape=(
            jax.ShapeDtypeStruct((rows, size), jnp.float32),
            jax.ShapeDtypeStruct((XS * YS, rows, LANES), jnp.float32),
        ),
        compiler_params=PARAMS,
    )(left_rows, right_rows, after)
    left = lax.all_gather(left, "rep", axis=0, tiled=True)
    return left, lax.all_to_all(right, "rep", 0, 0, tiled=True).reshape(size, LANES)


def halves_kernel(whole_ref, *refs):
    part_a, part_b = refs[-2:]
    slots = part_a.shape[0] // whole_ref.shape[1]
    part_a[...] = whole_ref[:slots].reshape(part_a.shape)
    part_b[...] = whole_ref[slots:].reshape(part_b.shape)


def halves(panel, split, after):
    shards, stripe, _ = panel.shape
    outs = [
        jax.ShapeDtypeStruct((rows, LANES), jnp.float32)
        for rows in (split, shards * stripe - split)
    ]
    return pl.pallas_call(
        halves_kernel,
        in_specs=whole(1) + unread(len(after)),
        out_specs=whole(2),
        out_shape=outs,
        compiler_params=PARAMS,
    )(panel, *after)


def assemble(pos_ref, a_refs, b_refs, store):
    split = a_refs[0].shape[0]
    for n in range(XS * YS):
        k = place(pos_ref, n // YS, -(n % YS))
        columns = pl.ds(pl.multiple_of(k * LANES, LANES), LANES)
        store(slice(0, split), columns, a_refs[n][...])
        store(slice(split, None), columns, b_refs[n][...])


def shampoo_kernel(pos_ref, *refs):
    n = XS * YS
    g_a, g_b = named(refs[:PARTS])
    left, right, second_ref, out_ref, moment_ref, high, low, own = refs[PARTS:]

    def store(rows, columns, value):
        high[rows, columns], low[rows, columns] = split3(value)

    assemble(pos_ref, g_a, g_b, store)

    rows = second_ref.shape[0]
    mine = place(pos_ref, 0, 0)
    parts_a = g_a[0].shape[0] // rows
    for refs_part, first, here in (
        (g_a, mine, mine < parts_a),
        (g_b, mine - parts_a, mine >= parts_a),
    ):

        @pl.when(here)
        def _():
            for m in range(n):
                k = place(pos_ref, m // YS, -(m % YS))
                own[:, pl.ds(pl.multiple_of(k * LANES, LANES), LANES)] = refs_part[m][
                    pl.ds(pl.multiple_of(first * rows, rows), rows), :
                ]

    moment = beta_two * second_ref[...] + (1.0 - beta_two) * own[...] * own[...]
    moment_ref[...] = moment
    adam = own[...] / (jnp.sqrt(moment) + adam_eps)
    adam_part = jnp.sum(adam * adam)

    mixed = dot3((high[...], low[...]), split3(right[...]), ((1,), (0,)))
    result = dot3(split3(left[...]), split3(mixed), ((1,), (0,)))
    shampoo_part = jnp.sum(result * result)

    shards, message, _ = out_ref.shape
    stripe = result.shape[0] // shards
    row = lax.broadcasted_iota(jnp.int32, (message - stripe, LANES), 0)
    lane = lax.broadcasted_iota(jnp.int32, (message - stripe, LANES), 1)
    norms = jnp.where(row == 0, adam_part, jnp.where(row == 1, shampoo_part, 0.0))
    norms = jnp.where(lane == pos_ref[2], norms, 0.0)
    out_ref[:, :stripe] = result.reshape(shards, stripe, LANES)
    out_ref[:, stripe:] = jnp.broadcast_to(norms[None], (shards, *norms.shape))


def shampoo(pos, g_parts, left, right, second, shards):
    rows, size = second.shape
    outs = (
        jax.ShapeDtypeStruct((shards, size // shards + 8, LANES), jnp.float32),
        jax.ShapeDtypeStruct(second.shape, jnp.float32),
    )
    arrays = (*listed(g_parts), left, right, second)
    return pl.pallas_call(
        shampoo_kernel,
        in_specs=smem(1) + whole(len(arrays)),
        out_specs=whole(2),
        out_shape=outs,
        scratch_shapes=[
            VMEM((size, size), jnp.bfloat16),
            VMEM((size, size), jnp.bfloat16),
            VMEM((rows, size), jnp.float32),
        ],
        compiler_params=PARAMS,
    )(pos, *arrays)


def stats_kernel(pos_ref, *refs):
    left_ref, right_ref, left_out, right_out, g = refs[PARTS:]

    def store(rows, columns, value):
        g[rows, columns] = value

    assemble(pos_ref, *named(refs[:PARTS]), store)
    rows = left_ref.shape[0]
    first = pl.multiple_of(place(pos_ref, 0, 0) * rows, rows)
    every = split3(g[...])
    own_rows = split3(g[pl.ds(first, rows), :])
    own_cols = split3(g[:, pl.ds(first, rows)])
    left_out[...] = beta_two * left_ref[...] + (1.0 - beta_two) * dot3(
        own_rows, every, ((1,), (1,))
    )
    right_out[...] = beta_two * right_ref[...] + (1.0 - beta_two) * dot3(
        own_cols, every, ((0,), (0,))
    )


def statistics(pos, g_parts, left, right):
    size = left.shape[1]
    arrays = (*listed(g_parts), left, right)
    outs = (
        jax.ShapeDtypeStruct(left.shape, jnp.float32),
        jax.ShapeDtypeStruct(right.shape, jnp.float32),
    )
    return pl.pallas_call(
        stats_kernel,
        in_specs=smem(1) + whole(len(arrays)),
        out_specs=whole(2),
        out_shape=outs,
        scratch_shapes=[VMEM((size, size), jnp.float32)],
        compiler_params=PARAMS,
        cost_estimate=pl.CostEstimate(
            flops=12 * left.shape[0] * size * size, bytes_accessed=24 * left.size, transcendentals=0
        ),
    )(pos, *arrays)


def order_kernel(pos_ref, owner_ref, *refs):
    n = XS * YS
    (a_refs, b_refs), out_ref = named(refs[:PARTS]), refs[PARTS]
    stripe, columns = out_ref.shape[1:]
    half = stripe // 2
    block_cols = columns // (n * LANES)
    body = a_refs[0].shape[0]
    norms = b_refs[0][body:]
    for m in range(1, n):
        norms = norms + b_refs[m][body:]
    root = jnp.sqrt(norms)
    factors = root[0:1] / (root[1:2] + norm_eps)
    lane = lax.broadcasted_iota(jnp.int32, (1, LANES), 1)
    for j in range(block_cols):
        slot = owner_ref[pl.program_id(0) * block_cols + j]
        factor = jnp.sum(jnp.where(lane == slot, factors, 0.0))
        rows = pl.ds(pl.multiple_of(slot * half, half), half)
        for m in range(n):
            column = (j * n + place(pos_ref, m // YS, -(m % YS))) * LANES
            columns_m = pl.ds(pl.multiple_of(column, LANES), LANES)
            out_ref[0, :half, columns_m] = a_refs[m][rows] * factor
            out_ref[0, half:, columns_m] = b_refs[m][rows] * factor


def unpack_kernel(back_ref, *refs):
    part_a, part_b = refs[-2:]
    rows = part_a.shape[0]
    half = rows // back_ref.shape[0]
    part_a[...] = back_ref[:, :half].reshape(rows, LANES)
    part_b[:rows] = back_ref[:, half : 2 * half].reshape(rows, LANES)
    part_b[rows:] = jnp.sum(back_ref[:, 2 * half :], axis=0)


def unpack(back, after):
    shards, message, _ = back.shape
    rows = shards * (message - 8) // 2
    outs = [
        jax.ShapeDtypeStruct((rows, LANES), jnp.float32),
        jax.ShapeDtypeStruct((rows + 8, LANES), jnp.float32),
    ]
    return pl.pallas_call(
        unpack_kernel,
        in_specs=whole(1) + unread(len(after)),
        out_specs=whole(2),
        out_shape=outs,
        compiler_params=PARAMS,
    )(back, *after)


def order(pos, owner_slot, got, shape):
    block_rows, stripe, columns = shape
    fixed = lambda n: lambda i, *_: (0,) * n
    return pl.pallas_call(
        order_kernel,
        grid_spec=pltpu.PrefetchScalarGridSpec(
            num_scalar_prefetch=2,
            grid=(block_rows,),
            in_specs=[pl.BlockSpec(v.shape, fixed(v.ndim)) for v in listed(got)],
            out_specs=pl.BlockSpec((1, stripe, columns), lambda i, *_: (i, 0, 0)),
        ),
        out_shape=jax.ShapeDtypeStruct(shape, jnp.float32),
        compiler_params=PARAMS,
    )(pos, owner_slot, *listed(got))


def per_device(grads, owner_slot, left_stat, right_stat, left_root, right_root, second_moment):
    replicas = lax.axis_size("rep")
    shards = lax.axis_size("shard")
    own_rows = grads[0]
    size = own_rows.shape[1] * shards
    rep = lax.axis_index("rep")
    pos = jnp.stack([rep // YS, rep % YS, lax.axis_index("shard")]).astype(jnp.int32)

    a, b, under_way = reduce_scatter(cut(pos, owner_slot, own_rows, shards))
    left, right = roots(left_root[0], right_root[0], under_way)
    summed = total(1.0 / replicas, a, b, ())
    panel = lax.all_to_all(summed, "shard", 0, 0, tiled=True)
    g_parts = gather(*halves(panel, size * 5 // 8, (right,)))
    message, moment_new = shampoo(pos, g_parts, left, right, second_moment[0], shards)
    back = lax.all_to_all(message, "shard", 0, 0, tiled=True)
    left_new, right_new = statistics(pos, g_parts, left_stat[0], right_stat[0])

    parts = gather(*unpack(back, (left_new,)))
    direction = order(pos, owner_slot, parts, own_rows.shape)
    return (direction, left_new[None], right_new[None], moment_new[None])


def solution(mesh):
    return jax.shard_map(
        per_device,
        mesh=mesh,
        in_specs=(
            P("rep", None, "shard", None),
            P(),
            P("shard", "rep", None),
            P("shard", "rep", None),
            P("shard", "rep", None),
            P("shard", "rep", None),
            P("shard", "rep", None),
        ),
        out_specs=(
            P(None, "shard", None),
            P("shard", "rep", None),
            P("shard", "rep", None),
            P("shard", "rep", None),
        ),
        check_vma=False,
    )
```

```python
import functools

import jax
import jax.numpy as jnp
from jax import lax
from jax.experimental import pallas as pl
from jax.experimental.pallas import tpu as pltpu
from jax.sharding import PartitionSpec as P

beta_two = 0.99
adam_eps = 1e-08
norm_eps = 1e-06

XS, YS = 2, 4
LANES = 128
VMEM = pltpu.VMEM
PARAMS = pltpu.CompilerParams(vmem_limit_bytes=48 * 1024 * 1024)


def shift(value, dx, dy):
    pairs = [
        (r, ((r // YS + dx) % XS) * YS + (r % YS + dy) % YS) for r in range(XS * YS)
    ]
    return lax.ppermute(value, "rep", pairs)


def whole(n):
    return [pl.BlockSpec(memory_space=VMEM)] * n


def smem(n):
    return [pl.BlockSpec(memory_space=pltpu.SMEM)] * n


def place(pos_ref, x_rel, t):
    x = lax.rem(pos_ref[0] + x_rel, XS)
    y = lax.rem(pos_ref[1] + t + YS, YS)
    return x * YS + y


def split3(value):
    high = value.astype(jnp.bfloat16)
    low = (value - high.astype(jnp.float32)).astype(jnp.bfloat16)
    return high, low


def dot3(a, b, dims):
    dot = functools.partial(
        lax.dot_general, dimension_numbers=(dims, ((), ())), preferred_element_type=jnp.float32
    )
    return dot(a[0], b[0]) + (dot(a[0], b[1]) + dot(a[1], b[0]))


def cut_kernel(pos_ref, owner_ref, g_ref, *outs):
    keep_a, send_a, keep_b, send_b = outs[:4], outs[4:8], outs[8], outs[9:12]
    i = pl.program_id(0)
    split = keep_a[0].shape[0]
    block_cols = g_ref.shape[2] // (XS * YS * LANES)

    def piece(j, x_rel, t):
        column = (j * XS * YS + place(pos_ref, x_rel, t)) * LANES
        return g_ref[0, :, pl.ds(pl.multiple_of(column, LANES), LANES)]

    for j in range(block_cols):
        slot = owner_ref[i * block_cols + j]

        @pl.when(slot < split)
        def _():
            for t in range(YS):
                keep_a[t][slot] = piece(j, 0, t)
                send_a[t][slot] = piece(j, 1, t)

        @pl.when(slot >= split)
        def _():
            for x_rel in range(XS):
                keep_b[x_rel, slot - split] = piece(j, x_rel, 0)
                for t in range(1, YS):
                    send_b[t - 1][x_rel, slot - split] = piece(j, x_rel, t)


def cut(pos, owner_slot, own_rows, slots):
    block_rows, stripe, columns = own_rows.shape
    split = (slots * 19) // 32
    shapes = [(split, stripe, LANES)] * (2 * YS)
    shapes += [(XS, slots - split, stripe, LANES)] * YS
    fixed = lambda n: lambda i, *_: (0,) * n
    return pl.pallas_call(
        cut_kernel,
        grid_spec=pltpu.PrefetchScalarGridSpec(
            num_scalar_prefetch=2,
            grid=(block_rows,),
            in_specs=[pl.BlockSpec((1, stripe, columns), lambda i, *_: (i, 0, 0))],
            out_specs=[pl.BlockSpec(s, fixed(len(s))) for s in shapes],
        ),
        out_shape=[jax.ShapeDtypeStruct(s, jnp.float32) for s in shapes],
        compiler_params=PARAMS,
    )(pos, owner_slot, own_rows)


def blocks(arrays):
    return [pl.BlockSpec(v.shape, lambda i, n=v.ndim: (0,) * n) for v in arrays]


def unread(n):
    return [pl.BlockSpec(memory_space=pl.ANY)] * n


def add_kernel(keep, first, second, third, *refs):
    away, own = refs[-2:]
    for x, out in ((1, away), (0, own)):
        out[...] = keep[x] + first[x] + second[x] + third[x]


def add(keep, got, after):
    out = jax.ShapeDtypeStruct(keep.shape[1:], jnp.float32)
    arrays = (keep, *got)
    return pl.pallas_call(
        add_kernel,
        grid=(1,),
        in_specs=blocks(arrays) + unread(len(after)),
        out_specs=blocks((out, out)),
        out_shape=(out, out),
        compiler_params=PARAMS,
    )(*arrays, *after)


def total_kernel(scale, a0, a1, a2, a3, b0, b1, *refs):
    out = refs[-1]
    split = a0.shape[0]
    out[:split] = (a0[...] + a1[...] + a2[...] + a3[...]) * scale
    out[split:] = (b0[...] + b1[...]) * scale


def total(scale, a, b, after):
    slots = a[0].shape[0] + b[0].shape[0]
    out = jax.ShapeDtypeStruct((slots, *a[0].shape[1:]), jnp.float32)
    arrays = (*a, *b)
    return pl.pallas_call(
        functools.partial(total_kernel, scale),
        grid=(1,),
        in_specs=blocks(arrays) + unread(len(after)),
        out_specs=blocks((out,))[0],
        out_shape=out,
        compiler_params=PARAMS,
    )(*arrays, *after)


def reduce_scatter(parts):
    keep_a, send_a, keep_b, send_b = parts[:4], parts[4:8], parts[8], parts[9:12]
    got_a = {t: shift(send_a[t], 1, 0) for t in (2, 1, 3, 0)}
    got_b = [shift(send_b[t - 1], 0, t) for t in (1, 3, 2)]
    sum_a = {t: keep_a[t] + got_a[t] for t in (2, 1, 3, 0)}
    last_a = {t: shift(sum_a[t], 0, t) for t in (2, 1, 3)}
    away, own = add(keep_b, got_b, (sum_a[2], sum_a[1]))
    last_b = shift(away, 1, 0)
    return (sum_a[0], last_a[2], last_a[1], last_a[3]), (own, last_b), own


def gather(part_a, part_b):
    got = {("a", 0, 0): part_a, ("b", 0, 0): part_b}
    for t in (1, 3, 2):
        got["a", 0, t] = shift(part_a, 0, t)
    got["b", 1, 0] = shift(part_b, 1, 0)
    got["a", 1, 0] = shift(part_a, 1, 0)
    for t in (1, 3, 2):
        got["b", 0, t] = shift(part_b, 0, t)
    for t in (1, 3, 2):
        got["a", 1, t] = shift(got["a", 0, t], 1, 0)
        got["b", 1, t] = shift(got["b", 1, 0], 0, t)
    return got


LATEST_FIRST = (
    [(n, 1, t) for t in (2, 3, 1) for n in ("b", "a")]
    + [("b", 0, t) for t in (2, 3, 1)]
    + [("a", 1, 0), ("b", 1, 0)]
    + [("a", 0, t) for t in (2, 3, 1)]
    + [("b", 0, 0), ("a", 0, 0)]
)
PARTS = len(LATEST_FIRST)


def listed(got):
    return [got[key] for key in LATEST_FIRST]


def named(refs):
    got = dict(zip(LATEST_FIRST, refs))
    return tuple([got[n, x, t] for x in range(XS) for t in range(YS)] for n in ("a", "b"))


def roots_kernel(left_ref, right_ref, after_ref, out):
    rows, size = left_ref.shape
    half, per = size // XS, rows // YS
    for k in range(XS * YS):
        x, y = k // YS, k % YS
        for n in range(per // 8):
            first = (n * YS + y) * 8
            for h in range(XS):
                out[k, h * per + n * 8 : h * per + n * 8 + 8] = left_ref[
                    first : first + 8, h * half : (h + 1) * half
                ]
        out[k, XS * per :] = right_ref[:, x * half : (x + 1) * half]


def roots(left_rows, right_rows, after):
    rows, size = left_rows.shape
    cut = pl.pallas_call(
        roots_kernel,
        in_specs=whole(2) + unread(1),
        out_specs=whole(1)[0],
        out_shape=jax.ShapeDtypeStruct((XS * YS, rows // YS * XS + rows, size // XS), jnp.float32),
        compiler_params=PARAMS,
    )(left_rows, right_rows, after)
    return lax.all_to_all(cut, "rep", 0, 0, tiled=True)


def halves_kernel(whole_ref, *refs):
    part_a, part_b = refs[-2:]
    slots = part_a.shape[0] // whole_ref.shape[1]
    part_a[...] = whole_ref[:slots].reshape(part_a.shape)
    part_b[...] = whole_ref[slots:].reshape(part_b.shape)


def halves(panel, split, after):
    shards, stripe, _ = panel.shape
    outs = [
        jax.ShapeDtypeStruct((rows, LANES), jnp.float32)
        for rows in (split, shards * stripe - split)
    ]
    return pl.pallas_call(
        halves_kernel,
        in_specs=whole(1) + unread(len(after)),
        out_specs=whole(2),
        out_shape=outs,
        compiler_params=PARAMS,
    )(panel, *after)


def assemble(pos_ref, a_refs, b_refs, store):
    split = a_refs[0].shape[0]
    for n in range(XS * YS):
        k = place(pos_ref, n // YS, -(n % YS))
        columns = pl.ds(pl.multiple_of(k * LANES, LANES), LANES)
        store(slice(0, split), columns, a_refs[n][...])
        store(slice(split, None), columns, b_refs[n][...])


def assemble_roots(parts, left, right):
    n, rows, half = parts.shape
    r_rows = right.shape[0] // n
    per = left.shape[0] // n
    for k in range(n):
        for h in range(XS):
            left[k * per : (k + 1) * per, h * half : (h + 1) * half] = parts[
                k, h * per : (h + 1) * per
            ]
        right[k * r_rows : (k + 1) * r_rows] = parts[k, rows - r_rows :]


def shampoo_kernel(pos_ref, *refs):
    n = XS * YS
    g_a, g_b = named(refs[:PARTS])
    root_ref, second_ref, out_ref, moment_ref, high, low, left, right, own = refs[PARTS:]

    def store(rows, columns, value):
        high[rows, columns], low[rows, columns] = split3(value)

    assemble(pos_ref, g_a, g_b, store)
    assemble_roots(root_ref, left, right)

    rows = second_ref.shape[0]
    mine = place(pos_ref, 0, 0)
    parts_a = g_a[0].shape[0] // rows
    for refs_part, first, here in (
        (g_a, mine, mine < parts_a),
        (g_b, mine - parts_a, mine >= parts_a),
    ):

        @pl.when(here)
        def _():
            for m in range(n):
                k = place(pos_ref, m // YS, -(m % YS))
                own[:, pl.ds(pl.multiple_of(k * LANES, LANES), LANES)] = refs_part[m][
                    pl.ds(pl.multiple_of(first * rows, rows), rows), :
                ]

    moment = beta_two * second_ref[...] + (1.0 - beta_two) * own[...] * own[...]
    moment_ref[...] = moment
    adam = own[...] / (jnp.sqrt(moment) + adam_eps)
    adam_part = jnp.sum(adam * adam)

    mixed = dot3((high[...], low[...]), split3(right[...]), ((1,), (0,)))
    result = dot3(split3(left[...]), split3(mixed), ((1,), (0,)))
    shampoo_part = jnp.sum(result * result)

    shards, per, _ = out_ref.shape
    width = result.shape[1]
    row = lax.broadcasted_iota(jnp.int32, (per, LANES), 0)
    lane = lax.broadcasted_iota(jnp.int32, (per, LANES), 1)
    norms = jnp.where(row == 0, adam_part, jnp.where(row == 1, shampoo_part, 0.0))
    norms = jnp.where(lane == pos_ref[2], norms, 0.0)
    out_ref[:, :, :width] = result.reshape(shards, per, width)
    out_ref[:, :, width:] = jnp.broadcast_to(norms[None], (shards, per, LANES))


def shampoo(pos, g_parts, root_parts, second, shards):
    rows, size = second.shape
    half, per = size // XS, size // shards // YS
    outs = (
        jax.ShapeDtypeStruct((shards, per, half + LANES), jnp.float32),
        jax.ShapeDtypeStruct(second.shape, jnp.float32),
    )
    arrays = (*listed(g_parts), root_parts, second)
    return pl.pallas_call(
        shampoo_kernel,
        grid=(1,),
        in_specs=smem(1) + blocks(arrays),
        out_specs=blocks(outs),
        out_shape=outs,
        scratch_shapes=[
            VMEM((size, size), jnp.bfloat16),
            VMEM((size, size), jnp.bfloat16),
            VMEM((size // YS, size), jnp.float32),
            VMEM((size, half), jnp.float32),
            VMEM((rows, size), jnp.float32),
        ],
        compiler_params=PARAMS,
    )(pos, *arrays)


def stats_kernel(pos_ref, *refs):
    left_ref, right_ref, left_out, right_out, g = refs[PARTS:]

    def store(rows, columns, value):
        g[rows, columns] = value

    assemble(pos_ref, *named(refs[:PARTS]), store)
    rows = left_ref.shape[0]
    first = pl.multiple_of(place(pos_ref, 0, 0) * rows, rows)
    every = split3(g[...])
    own_rows = split3(g[pl.ds(first, rows), :])
    own_cols = split3(g[:, pl.ds(first, rows)])
    left_out[...] = beta_two * left_ref[...] + (1.0 - beta_two) * dot3(
        own_rows, every, ((1,), (1,))
    )
    right_out[...] = beta_two * right_ref[...] + (1.0 - beta_two) * dot3(
        own_cols, every, ((0,), (0,))
    )


def statistics(pos, g_parts, left, right):
    size = left.shape[1]
    arrays = (*listed(g_parts), left, right)
    outs = (
        jax.ShapeDtypeStruct(left.shape, jnp.float32),
        jax.ShapeDtypeStruct(right.shape, jnp.float32),
    )
    return pl.pallas_call(
        stats_kernel,
        grid=(1,),
        in_specs=smem(1) + blocks(arrays),
        out_specs=blocks(outs),
        out_shape=outs,
        scratch_shapes=[VMEM((size, size), jnp.float32)],
        compiler_params=PARAMS,
        cost_estimate=pl.CostEstimate(
            flops=12 * left.shape[0] * size * size, bytes_accessed=24 * left.size, transcendentals=0
        ),
    )(pos, *arrays)


def order_kernel(pos_ref, owner_ref, *refs):
    n = XS * YS
    (a_refs, b_refs), out_ref = named(refs[:PARTS]), refs[PARTS]
    stripe, columns = out_ref.shape[1:]
    body, width = a_refs[0].shape
    per = b_refs[0].shape[0] - body
    block_cols = columns // (2 * XS * width)
    norms = b_refs[0][body:, :LANES]
    for m in range(1, n):
        norms = norms + b_refs[m][body:, :LANES]
    root = jnp.sqrt(norms)
    factors = root[0:1] / (root[1:2] + norm_eps)
    lane = lax.broadcasted_iota(jnp.int32, (1, LANES), 1)
    for j in range(block_cols):
        slot = owner_ref[pl.program_id(0) * block_cols + j]
        factor = jnp.sum(jnp.where(lane == slot, factors, 0.0))
        for m in range(n):
            x = lax.rem(pos_ref[0] + m // YS, XS)
            y = lax.rem(pos_ref[1] + YS - m % YS, YS)
            rows = pl.ds(pl.multiple_of(y * per, per), per)
            first = pl.multiple_of((j * XS + x) * 2 * width, 2 * width)
            source = pl.ds(pl.multiple_of(slot * per, per), per)
            out_ref[0, rows, pl.ds(first, width)] = a_refs[m][source] * factor
            out_ref[0, rows, pl.ds(pl.multiple_of(first + width, width), width)] = (
                b_refs[m][source] * factor
            )


def unpack_kernel(back_ref, *refs):
    part_a, part_b = refs[-2:]
    rows, width = part_a.shape
    part_a[...] = back_ref[:, :, :width].reshape(rows, width)
    part_b[:rows] = back_ref[:, :, width : 2 * width].reshape(rows, width)
    norms = jnp.sum(back_ref[:, :, 2 * width :], axis=0)
    for n in range(width // LANES):
        part_b[rows:, n * LANES : (n + 1) * LANES] = norms


def unpack(back, after):
    shards, per, size = back.shape
    width = (size - LANES) // 2
    outs = [
        jax.ShapeDtypeStruct((shards * per, width), jnp.float32),
        jax.ShapeDtypeStruct((shards * per + per, width), jnp.float32),
    ]
    return pl.pallas_call(
        unpack_kernel,
        grid=(1,),
        in_specs=blocks((back,)) + unread(len(after)),
        out_specs=blocks(outs),
        out_shape=outs,
        compiler_params=PARAMS,
    )(back, *after)


def order(pos, owner_slot, got, shape):
    block_rows, stripe, columns = shape
    fixed = lambda n: lambda i, *_: (0,) * n
    return pl.pallas_call(
        order_kernel,
        grid_spec=pltpu.PrefetchScalarGridSpec(
            num_scalar_prefetch=2,
            grid=(block_rows,),
            in_specs=[pl.BlockSpec(v.shape, fixed(v.ndim)) for v in listed(got)],
            out_specs=pl.BlockSpec((1, stripe, columns), lambda i, *_: (i, 0, 0)),
        ),
        out_shape=jax.ShapeDtypeStruct(shape, jnp.float32),
        compiler_params=PARAMS,
    )(pos, owner_slot, *listed(got))


def per_device(grads, owner_slot, left_stat, right_stat, left_root, right_root, second_moment):
    replicas = lax.axis_size("rep")
    shards = lax.axis_size("shard")
    own_rows = grads[0]
    size = own_rows.shape[1] * shards
    rep = lax.axis_index("rep")
    pos = jnp.stack([rep // YS, rep % YS, lax.axis_index("shard")]).astype(jnp.int32)

    a, b, under_way = reduce_scatter(cut(pos, owner_slot, own_rows, shards))
    root_parts = roots(left_root[0], right_root[0], under_way)
    summed = total(1.0 / replicas, a, b, ())
    panel = lax.all_to_all(summed, "shard", 0, 0, tiled=True)

    g_parts = gather(*halves(panel, size * 5 // 8, (root_parts,)))
    message, moment_new = shampoo(pos, g_parts, root_parts, second_moment[0], shards)
    back = lax.all_to_all(message, "shard", 0, 0, tiled=True)
    left_new, right_new = statistics(pos, g_parts, left_stat[0], right_stat[0])

    parts = gather(*unpack(back, (left_new,)))
    direction = order(pos, owner_slot, parts, own_rows.shape)
    return (direction, left_new[None], right_new[None], moment_new[None])


def solution(mesh):
    return jax.shard_map(
        per_device,
        mesh=mesh,
        in_specs=(
            P("rep", None, "shard", None),
            P(),
            P("shard", "rep", None),
            P("shard", "rep", None),
            P("shard", "rep", None),
            P("shard", "rep", None),
            P("shard", "rep", None),
        ),
        out_specs=(
            P(None, "shard", None),
            P("shard", "rep", None),
            P("shard", "rep", None),
            P("shard", "rep", None),
        ),
        check_vma=False,
    )
```

```python
import functools

import jax
import jax.numpy as jnp
from jax import lax
from jax.experimental import pallas as pl
from jax.experimental.pallas import tpu as pltpu
from jax.sharding import PartitionSpec as P

beta_two = 0.99
adam_eps = 1e-08
norm_eps = 1e-06

XS, YS = 2, 4
LANES = 128
VMEM = pltpu.VMEM
PARAMS = pltpu.CompilerParams(vmem_limit_bytes=48 * 1024 * 1024)


def shift(value, dx, dy):
    pairs = [
        (r, ((r // YS + dx) % XS) * YS + (r % YS + dy) % YS) for r in range(XS * YS)
    ]
    return lax.ppermute(value, "rep", pairs)


def whole(n):
    return [pl.BlockSpec(memory_space=VMEM)] * n


def smem(n):
    return [pl.BlockSpec(memory_space=pltpu.SMEM)] * n


def place(pos_ref, x_rel, t):
    x = lax.rem(pos_ref[0] + x_rel, XS)
    y = lax.rem(pos_ref[1] + t + YS, YS)
    return x * YS + y


def split3(value):
    high = value.astype(jnp.bfloat16)
    low = (value - high.astype(jnp.float32)).astype(jnp.bfloat16)
    return high, low


def dot3(a, b, dims):
    dot = functools.partial(
        lax.dot_general, dimension_numbers=(dims, ((), ())), preferred_element_type=jnp.float32
    )
    return dot(a[0], b[0]) + (dot(a[0], b[1]) + dot(a[1], b[0]))


def cut_kernel(pos_ref, owner_ref, g_ref, *outs):
    keep_a, send_a, keep_b, send_b = outs[:4], outs[4:8], outs[8], outs[9:12]
    i = pl.program_id(0)
    split = keep_a[0].shape[0]
    block_cols = g_ref.shape[2] // (XS * YS * LANES)

    def piece(j, x_rel, t):
        column = (j * XS * YS + place(pos_ref, x_rel, t)) * LANES
        return g_ref[0, :, pl.ds(pl.multiple_of(column, LANES), LANES)]

    for j in range(block_cols):
        slot = owner_ref[i * block_cols + j]

        @pl.when(slot < split)
        def _():
            for t in range(YS):
                keep_a[t][slot] = piece(j, 0, t)
                send_a[t][slot] = piece(j, 1, t)

        @pl.when(slot >= split)
        def _():
            for x_rel in range(XS):
                keep_b[x_rel, slot - split] = piece(j, x_rel, 0)
                for t in range(1, YS):
                    send_b[t - 1][x_rel, slot - split] = piece(j, x_rel, t)


def cut(pos, owner_slot, own_rows, slots):
    block_rows, stripe, columns = own_rows.shape
    split = (slots * 19) // 32
    shapes = [(split, stripe, LANES)] * (2 * YS)
    shapes += [(XS, slots - split, stripe, LANES)] * YS
    fixed = lambda n: lambda i, *_: (0,) * n
    return pl.pallas_call(
        cut_kernel,
        grid_spec=pltpu.PrefetchScalarGridSpec(
            num_scalar_prefetch=2,
            grid=(block_rows,),
            in_specs=[pl.BlockSpec((1, stripe, columns), lambda i, *_: (i, 0, 0))],
            out_specs=[pl.BlockSpec(s, fixed(len(s))) for s in shapes],
        ),
        out_shape=[jax.ShapeDtypeStruct(s, jnp.float32) for s in shapes],
        compiler_params=PARAMS,
    )(pos, owner_slot, own_rows)


def blocks(arrays):
    return [pl.BlockSpec(v.shape, lambda i, n=v.ndim: (0,) * n) for v in arrays]


def unread(n):
    return [pl.BlockSpec(memory_space=pl.ANY)] * n


def add_kernel(keep, first, second, third, *refs):
    away, own = refs[-2:]
    for x, out in ((1, away), (0, own)):
        out[...] = keep[x] + first[x] + second[x] + third[x]


def add(keep, got, after):
    out = jax.ShapeDtypeStruct(keep.shape[1:], jnp.float32)
    arrays = (keep, *got)
    return pl.pallas_call(
        add_kernel,
        grid=(1,),
        in_specs=blocks(arrays) + unread(len(after)),
        out_specs=blocks((out, out)),
        out_shape=(out, out),
        compiler_params=PARAMS,
    )(*arrays, *after)


def total_kernel(scale, a0, a1, a2, a3, b0, b1, *refs):
    out = refs[-1]
    split = a0.shape[0]
    out[:split] = (a0[...] + a1[...] + a2[...] + a3[...]) * scale
    out[split:] = (b0[...] + b1[...]) * scale


def total(scale, a, b, after):
    slots = a[0].shape[0] + b[0].shape[0]
    out = jax.ShapeDtypeStruct((slots, *a[0].shape[1:]), jnp.float32)
    arrays = (*a, *b)
    return pl.pallas_call(
        functools.partial(total_kernel, scale),
        grid=(1,),
        in_specs=blocks(arrays) + unread(len(after)),
        out_specs=blocks((out,))[0],
        out_shape=out,
        compiler_params=PARAMS,
    )(*arrays, *after)


def reduce_scatter(parts):
    keep_a, send_a, keep_b, send_b = parts[:4], parts[4:8], parts[8], parts[9:12]
    got_a = {t: shift(send_a[t], 1, 0) for t in (2, 1, 3, 0)}
    got_b = [shift(send_b[t - 1], 0, t) for t in (1, 3, 2)]
    sum_a = {t: keep_a[t] + got_a[t] for t in (2, 1, 3, 0)}
    last_a = {t: shift(sum_a[t], 0, t) for t in (2, 1, 3)}
    away, own = add(keep_b, got_b, (sum_a[2], sum_a[1]))
    last_b = shift(away, 1, 0)
    return (sum_a[0], last_a[2], last_a[1], last_a[3]), (own, last_b), sum_a[3]


def gather(part_a, part_b):
    got = {("a", 0, 0): part_a, ("b", 0, 0): part_b}
    for t in (1, 3, 2):
        got["a", 0, t] = shift(part_a, 0, t)
    got["b", 1, 0] = shift(part_b, 1, 0)
    got["a", 1, 0] = shift(part_a, 1, 0)
    for t in (1, 3, 2):
        got["b", 0, t] = shift(part_b, 0, t)
    for t in (1, 3, 2):
        got["a", 1, t] = shift(got["a", 0, t], 1, 0)
        got["b", 1, t] = shift(got["b", 1, 0], 0, t)
    return got


LATEST_FIRST = (
    [(n, 1, t) for t in (2, 3, 1) for n in ("b", "a")]
    + [("b", 0, t) for t in (2, 3, 1)]
    + [("a", 1, 0), ("b", 1, 0)]
    + [("a", 0, t) for t in (2, 3, 1)]
    + [("b", 0, 0), ("a", 0, 0)]
)
PARTS = len(LATEST_FIRST)


def listed(got):
    return [got[key] for key in LATEST_FIRST]


def named(refs):
    got = dict(zip(LATEST_FIRST, refs))
    return tuple([got[n, x, t] for x in range(XS) for t in range(YS)] for n in ("a", "b"))


DIRECT = [(1, t) for t in (2, 3, 1)] + [(0, t) for t in (2, 3, 1)] + [(1, 0), (0, 0)]


def roots_kernel(pos_ref, left_ref, right_ref, after_ref, *outs):
    rows, size = left_ref.shape
    half, per = size // XS, rows // YS
    for (x_rel, t), out in zip(DIRECT, outs):
        x = lax.rem(pos_ref[0] + x_rel, XS)
        y = lax.rem(pos_ref[1] + t, YS)
        for n in range(per // 8):
            first = pl.ds(pl.multiple_of((n * YS + y) * 8, 8), 8)
            for h in range(XS):
                out[h * per + n * 8 : h * per + n * 8 + 8] = left_ref[
                    first, h * half : (h + 1) * half
                ]
        out[XS * per :] = right_ref[:, pl.ds(pl.multiple_of(x * half, half), half)]


def roots(pos, left_rows, right_rows, after):
    rows, size = left_rows.shape
    chunk = jax.ShapeDtypeStruct((rows // YS * XS + rows, size // XS), jnp.float32)
    cuts = pl.pallas_call(
        roots_kernel,
        in_specs=smem(1) + whole(2) + unread(1),
        out_specs=whole(len(DIRECT)),
        out_shape=[chunk] * len(DIRECT),
        compiler_params=PARAMS,
    )(pos, left_rows, right_rows, after)
    return [
        cut if (x_rel, t) == (0, 0) else shift(cut, x_rel, t)
        for (x_rel, t), cut in zip(DIRECT, cuts)
    ]


def halves_kernel(whole_ref, *refs):
    part_a, part_b = refs[-2:]
    slots = part_a.shape[0] // whole_ref.shape[1]
    part_a[...] = whole_ref[:slots].reshape(part_a.shape)
    part_b[...] = whole_ref[slots:].reshape(part_b.shape)


def halves(panel, split, after):
    shards, stripe, _ = panel.shape
    outs = [
        jax.ShapeDtypeStruct((rows, LANES), jnp.float32)
        for rows in (split, shards * stripe - split)
    ]
    return pl.pallas_call(
        halves_kernel,
        in_specs=whole(1) + unread(len(after)),
        out_specs=whole(2),
        out_shape=outs,
        compiler_params=PARAMS,
    )(panel, *after)


def assemble(pos_ref, a_refs, b_refs, store):
    split = a_refs[0].shape[0]
    for n in range(XS * YS):
        k = place(pos_ref, n // YS, -(n % YS))
        columns = pl.ds(pl.multiple_of(k * LANES, LANES), LANES)
        store(slice(0, split), columns, a_refs[n][...])
        store(slice(split, None), columns, b_refs[n][...])


def assemble_roots(pos_ref, parts, left, right):
    n = len(parts)
    rows, half = parts[0].shape
    r_rows, per = right.shape[0] // n, left.shape[0] // n
    for (x_rel, t), part in zip(DIRECT, parts):
        k = place(pos_ref, x_rel, -t)
        for h in range(XS):
            left[pl.ds(pl.multiple_of(k * per, per), per), h * half : (h + 1) * half] = part[
                h * per : (h + 1) * per
            ]
        right[pl.ds(pl.multiple_of(k * r_rows, r_rows), r_rows), :] = part[rows - r_rows :]


def shampoo_kernel(pos_ref, *refs):
    n = XS * YS
    g_a, g_b = named(refs[:PARTS])
    second_ref, out_ref, moment_ref, high, low, left, right, own = refs[PARTS + n :]

    def store(rows, columns, value):
        high[rows, columns], low[rows, columns] = split3(value)

    assemble(pos_ref, g_a, g_b, store)
    assemble_roots(pos_ref, refs[PARTS : PARTS + n], left, right)

    rows = second_ref.shape[0]
    mine = place(pos_ref, 0, 0)
    parts_a = g_a[0].shape[0] // rows
    for refs_part, first, here in (
        (g_a, mine, mine < parts_a),
        (g_b, mine - parts_a, mine >= parts_a),
    ):

        @pl.when(here)
        def _():
            for m in range(n):
                k = place(pos_ref, m // YS, -(m % YS))
                own[:, pl.ds(pl.multiple_of(k * LANES, LANES), LANES)] = refs_part[m][
                    pl.ds(pl.multiple_of(first * rows, rows), rows), :
                ]

    moment = beta_two * second_ref[...] + (1.0 - beta_two) * own[...] * own[...]
    moment_ref[...] = moment
    adam = own[...] / (jnp.sqrt(moment) + adam_eps)
    adam_part = jnp.sum(adam * adam)

    mixed = dot3((high[...], low[...]), split3(right[...]), ((1,), (0,)))
    result = dot3(split3(left[...]), split3(mixed), ((1,), (0,)))
    shampoo_part = jnp.sum(result * result)

    shards, per, _ = out_ref.shape
    width = result.shape[1]
    row = lax.broadcasted_iota(jnp.int32, (per, LANES), 0)
    lane = lax.broadcasted_iota(jnp.int32, (per, LANES), 1)
    norms = jnp.where(row == 0, adam_part, jnp.where(row == 1, shampoo_part, 0.0))
    norms = jnp.where(lane == pos_ref[2], norms, 0.0)
    out_ref[:, :, :width] = result.reshape(shards, per, width)
    out_ref[:, :, width:] = jnp.broadcast_to(norms[None], (shards, per, LANES))


def shampoo(pos, g_parts, root_parts, second, shards):
    rows, size = second.shape
    half, per = size // XS, size // shards // YS
    outs = (
        jax.ShapeDtypeStruct((shards, per, half + LANES), jnp.float32),
        jax.ShapeDtypeStruct(second.shape, jnp.float32),
    )
    arrays = (*listed(g_parts), *root_parts, second)
    return pl.pallas_call(
        shampoo_kernel,
        grid=(1,),
        in_specs=smem(1) + blocks(arrays),
        out_specs=blocks(outs),
        out_shape=outs,
        scratch_shapes=[
            VMEM((size, size), jnp.bfloat16),
            VMEM((size, size), jnp.bfloat16),
            VMEM((size // YS, size), jnp.float32),
            VMEM((size, half), jnp.float32),
            VMEM((rows, size), jnp.float32),
        ],
        compiler_params=PARAMS,
    )(pos, *arrays)


def stats_kernel(pos_ref, *refs):
    left_ref, right_ref, left_out, right_out, g = refs[PARTS:]

    def store(rows, columns, value):
        g[rows, columns] = value

    assemble(pos_ref, *named(refs[:PARTS]), store)
    rows = left_ref.shape[0]
    first = pl.multiple_of(place(pos_ref, 0, 0) * rows, rows)
    every = split3(g[...])
    own_rows = split3(g[pl.ds(first, rows), :])
    own_cols = split3(g[:, pl.ds(first, rows)])
    left_out[...] = beta_two * left_ref[...] + (1.0 - beta_two) * dot3(
        own_rows, every, ((1,), (1,))
    )
    right_out[...] = beta_two * right_ref[...] + (1.0 - beta_two) * dot3(
        own_cols, every, ((0,), (0,))
    )


def statistics(pos, g_parts, left, right):
    size = left.shape[1]
    arrays = (*listed(g_parts), left, right)
    outs = (
        jax.ShapeDtypeStruct(left.shape, jnp.float32),
        jax.ShapeDtypeStruct(right.shape, jnp.float32),
    )
    return pl.pallas_call(
        stats_kernel,
        grid=(1,),
        in_specs=smem(1) + blocks(arrays),
        out_specs=blocks(outs),
        out_shape=outs,
        scratch_shapes=[VMEM((size, size), jnp.float32)],
        compiler_params=PARAMS,
        cost_estimate=pl.CostEstimate(
            flops=12 * left.shape[0] * size * size, bytes_accessed=24 * left.size, transcendentals=0
        ),
    )(pos, *arrays)


def order_kernel(pos_ref, owner_ref, *refs):
    n = XS * YS
    (a_refs, b_refs), out_ref = named(refs[:PARTS]), refs[PARTS]
    stripe, columns = out_ref.shape[1:]
    body, width = a_refs[0].shape
    per = b_refs[0].shape[0] - body
    block_cols = columns // (2 * XS * width)
    norms = b_refs[0][body:, :LANES]
    for m in range(1, n):
        norms = norms + b_refs[m][body:, :LANES]
    root = jnp.sqrt(norms)
    factors = root[0:1] / (root[1:2] + norm_eps)
    lane = lax.broadcasted_iota(jnp.int32, (1, LANES), 1)
    for j in range(block_cols):
        slot = owner_ref[pl.program_id(0) * block_cols + j]
        factor = jnp.sum(jnp.where(lane == slot, factors, 0.0))
        for m in range(n):
            x = lax.rem(pos_ref[0] + m // YS, XS)
            y = lax.rem(pos_ref[1] + YS - m % YS, YS)
            rows = pl.ds(pl.multiple_of(y * per, per), per)
            first = pl.multiple_of((j * XS + x) * 2 * width, 2 * width)
            source = pl.ds(pl.multiple_of(slot * per, per), per)
            out_ref[0, rows, pl.ds(first, width)] = a_refs[m][source] * factor
            out_ref[0, rows, pl.ds(pl.multiple_of(first + width, width), width)] = (
                b_refs[m][source] * factor
            )


def unpack_kernel(back_ref, *refs):
    part_a, part_b = refs[-2:]
    rows, width = part_a.shape
    part_a[...] = back_ref[:, :, :width].reshape(rows, width)
    part_b[:rows] = back_ref[:, :, width : 2 * width].reshape(rows, width)
    norms = jnp.sum(back_ref[:, :, 2 * width :], axis=0)
    for n in range(width // LANES):
        part_b[rows:, n * LANES : (n + 1) * LANES] = norms


def unpack(back, after):
    shards, per, size = back.shape
    width = (size - LANES) // 2
    outs = [
        jax.ShapeDtypeStruct((shards * per, width), jnp.float32),
        jax.ShapeDtypeStruct((shards * per + per, width), jnp.float32),
    ]
    return pl.pallas_call(
        unpack_kernel,
        grid=(1,),
        in_specs=blocks((back,)) + unread(len(after)),
        out_specs=blocks(outs),
        out_shape=outs,
        compiler_params=PARAMS,
    )(back, *after)


def order(pos, owner_slot, got, shape):
    block_rows, stripe, columns = shape
    fixed = lambda n: lambda i, *_: (0,) * n
    return pl.pallas_call(
        order_kernel,
        grid_spec=pltpu.PrefetchScalarGridSpec(
            num_scalar_prefetch=2,
            grid=(block_rows,),
            in_specs=[pl.BlockSpec(v.shape, fixed(v.ndim)) for v in listed(got)],
            out_specs=pl.BlockSpec((1, stripe, columns), lambda i, *_: (i, 0, 0)),
        ),
        out_shape=jax.ShapeDtypeStruct(shape, jnp.float32),
        compiler_params=PARAMS,
    )(pos, owner_slot, *listed(got))


def per_device(grads, owner_slot, left_stat, right_stat, left_root, right_root, second_moment):
    replicas = lax.axis_size("rep")
    shards = lax.axis_size("shard")
    own_rows = grads[0]
    size = own_rows.shape[1] * shards
    rep = lax.axis_index("rep")
    pos = jnp.stack([rep // YS, rep % YS, lax.axis_index("shard")]).astype(jnp.int32)

    a, b, under_way = reduce_scatter(cut(pos, owner_slot, own_rows, shards))
    root_parts = roots(pos, left_root[0], right_root[0], under_way)
    summed = total(1.0 / replicas, a, b, (root_parts[DIRECT.index((1, 0))],))
    panel = lax.all_to_all(summed, "shard", 0, 0, tiled=True)

    g_parts = gather(*halves(panel, size * 5 // 8, ()))
    message, moment_new = shampoo(pos, g_parts, root_parts, second_moment[0], shards)
    back = lax.all_to_all(message, "shard", 0, 0, tiled=True)
    left_new, right_new = statistics(pos, g_parts, left_stat[0], right_stat[0])

    parts = gather(*unpack(back, (left_new,)))
    direction = order(pos, owner_slot, parts, own_rows.shape)
    return (direction, left_new[None], right_new[None], moment_new[None])


def solution(mesh):
    return jax.shard_map(
        per_device,
        mesh=mesh,
        in_specs=(
            P("rep", None, "shard", None),
            P(),
            P("shard", "rep", None),
            P("shard", "rep", None),
            P("shard", "rep", None),
            P("shard", "rep", None),
            P("shard", "rep", None),
        ),
        out_specs=(
            P(None, "shard", None),
            P("shard", "rep", None),
            P("shard", "rep", None),
            P("shard", "rep", None),
        ),
        check_vma=False,
    )
```

```python
import functools

import jax
import jax.numpy as jnp
from jax import lax
from jax.experimental import pallas as pl
from jax.experimental.pallas import tpu as pltpu
from jax.sharding import PartitionSpec as P

beta_two = 0.99
adam_eps = 1e-08
norm_eps = 1e-06

XS, YS = 2, 4
LANES = 128
VMEM = pltpu.VMEM
PARAMS = pltpu.CompilerParams(vmem_limit_bytes=48 * 1024 * 1024)


def shift(value, dx, dy):
    pairs = [
        (r, ((r // YS + dx) % XS) * YS + (r % YS + dy) % YS) for r in range(XS * YS)
    ]
    return lax.ppermute(value, "rep", pairs)


def whole(n):
    return [pl.BlockSpec(memory_space=VMEM)] * n


def smem(n):
    return [pl.BlockSpec(memory_space=pltpu.SMEM)] * n


def place(pos_ref, x_rel, t):
    x = lax.rem(pos_ref[0] + x_rel, XS)
    y = lax.rem(pos_ref[1] + t + YS, YS)
    return x * YS + y


def split3(value):
    high = value.astype(jnp.bfloat16)
    low = (value - high.astype(jnp.float32)).astype(jnp.bfloat16)
    return high, low


def dot3(a, b, dims):
    dot = functools.partial(
        lax.dot_general, dimension_numbers=(dims, ((), ())), preferred_element_type=jnp.float32
    )
    return dot(a[0], b[0]) + (dot(a[0], b[1]) + dot(a[1], b[0]))


def cut_kernel(pos_ref, owner_ref, g_ref, *outs):
    keep_a, send_a, keep_b, send_b = outs[:4], outs[4:8], outs[8], outs[9:12]
    i = pl.program_id(0)
    split = keep_a[0].shape[0]
    block_cols = g_ref.shape[2] // (XS * YS * LANES)

    def piece(j, x_rel, t):
        column = (j * XS * YS + place(pos_ref, x_rel, t)) * LANES
        return g_ref[0, :, pl.ds(pl.multiple_of(column, LANES), LANES)]

    for j in range(block_cols):
        slot = owner_ref[i * block_cols + j]

        @pl.when(slot < split)
        def _():
            for t in range(YS):
                keep_a[t][slot] = piece(j, 0, t)
                send_a[t][slot] = piece(j, 1, t)

        @pl.when(slot >= split)
        def _():
            for x_rel in range(XS):
                keep_b[x_rel, slot - split] = piece(j, x_rel, 0)
                for t in range(1, YS):
                    send_b[t - 1][x_rel, slot - split] = piece(j, x_rel, t)


def cut(pos, owner_slot, own_rows, slots):
    block_rows, stripe, columns = own_rows.shape
    split = (slots * 19) // 32
    shapes = [(split, stripe, LANES)] * (2 * YS)
    shapes += [(XS, slots - split, stripe, LANES)] * YS
    fixed = lambda n: lambda i, *_: (0,) * n
    return pl.pallas_call(
        cut_kernel,
        grid_spec=pltpu.PrefetchScalarGridSpec(
            num_scalar_prefetch=2,
            grid=(block_rows,),
            in_specs=[pl.BlockSpec((1, stripe, columns), lambda i, *_: (i, 0, 0))],
            out_specs=[pl.BlockSpec(s, fixed(len(s))) for s in shapes],
        ),
        out_shape=[jax.ShapeDtypeStruct(s, jnp.float32) for s in shapes],
        compiler_params=PARAMS,
    )(pos, owner_slot, own_rows)


def blocks(arrays):
    return [pl.BlockSpec(v.shape, lambda i, n=v.ndim: (0,) * n) for v in arrays]


def unread(n):
    return [pl.BlockSpec(memory_space=pl.ANY)] * n


def plus_kernel(one, other, *refs):
    refs[-1][...] = one[...] + other[...]


def plus(one, other, after):
    return pl.pallas_call(
        plus_kernel,
        in_specs=whole(2) + unread(len(after)),
        out_specs=whole(1)[0],
        out_shape=jax.ShapeDtypeStruct(one.shape, jnp.float32),
        compiler_params=PARAMS,
    )(one, other, *after)


def add_kernel(keep, first, second, third, *refs):
    away, own = refs[-2:]
    for x, out in ((1, away), (0, own)):
        out[...] = keep[x] + first[x] + second[x] + third[x]


def add(keep, got, after):
    out = jax.ShapeDtypeStruct(keep.shape[1:], jnp.float32)
    arrays = (keep, *got)
    return pl.pallas_call(
        add_kernel,
        grid=(1,),
        in_specs=blocks(arrays) + unread(len(after)),
        out_specs=blocks((out, out)),
        out_shape=(out, out),
        compiler_params=PARAMS,
    )(*arrays, *after)


def total_kernel(scale, a0, a1, a2, a3, b0, b1, *refs):
    out = refs[-1]
    split = a0.shape[0]
    out[:split] = (a0[...] + a1[...] + a2[...] + a3[...]) * scale
    out[split:] = (b0[...] + b1[...]) * scale


def total(scale, a, b, after):
    slots = a[0].shape[0] + b[0].shape[0]
    out = jax.ShapeDtypeStruct((slots, *a[0].shape[1:]), jnp.float32)
    arrays = (*a, *b)
    return pl.pallas_call(
        functools.partial(total_kernel, scale),
        grid=(1,),
        in_specs=blocks(arrays) + unread(len(after)),
        out_specs=blocks((out,))[0],
        out_shape=out,
        compiler_params=PARAMS,
    )(*arrays, *after)


def reduce_scatter(parts):
    keep_a, send_a, keep_b, send_b = parts[:4], parts[4:8], parts[8], parts[9:12]
    got_a = {t: shift(send_a[t], 1, 0) for t in (2, 1, 3, 0)}
    got_b = [shift(send_b[t - 1], 0, t) for t in (1, 3, 2)]
    sum_a, last_a = {}, {}
    for t in (2, 1, 3, 0):
        sum_a[t] = plus(keep_a[t], got_a[t], (last_a[2],) if t in (1, 3) else ())
        if t:
            last_a[t] = shift(sum_a[t], 0, t)
    away, own = add(keep_b, got_b, (sum_a[2],))
    last_b = shift(away, 1, 0)
    return (sum_a[0], last_a[2], last_a[1], last_a[3]), (own, last_b), sum_a[3]


def gather(part_a, part_b):
    got = {("a", 0, 0): part_a, ("b", 0, 0): part_b}
    for t in (1, 3, 2):
        got["a", 0, t] = shift(part_a, 0, t)
    got["b", 1, 0] = shift(part_b, 1, 0)
    got["a", 1, 0] = shift(part_a, 1, 0)
    for t in (1, 3, 2):
        got["b", 0, t] = shift(part_b, 0, t)
    for t in (1, 3, 2):
        got["a", 1, t] = shift(got["a", 0, t], 1, 0)
        got["b", 1, t] = shift(got["b", 1, 0], 0, t)
    return got


LATEST_FIRST = (
    [("b", 0, t) for t in (2, 3, 1)]
    + [(n, 1, t) for t in (2, 3, 1) for n in ("b", "a")]
    + [("a", 1, 0), ("b", 1, 0)]
    + [("a", 0, t) for t in (2, 3, 1)]
    + [("b", 0, 0), ("a", 0, 0)]
)
PARTS = len(LATEST_FIRST)


def listed(got):
    return [got[key] for key in LATEST_FIRST]


def named(refs):
    got = dict(zip(LATEST_FIRST, refs))
    return tuple([got[n, x, t] for x in range(XS) for t in range(YS)] for n in ("a", "b"))


def crossing_kernel(pos_ref, right_ref, after_ref, out):
    half = out.shape[1]
    first = lax.rem(pos_ref[0] + 1, XS) * half
    out[...] = right_ref[:, pl.ds(pl.multiple_of(first, half), half)]


def crossing(pos, right_rows, after):
    rows, size = right_rows.shape
    other = pl.pallas_call(
        crossing_kernel,
        in_specs=smem(1) + whole(1) + unread(1),
        out_specs=whole(1)[0],
        out_shape=jax.ShapeDtypeStruct((rows, size // XS), jnp.float32),
        compiler_params=PARAMS,
    )(pos, right_rows, after)
    return shift(other, 1, 0)


def roots_kernel(pos_ref, left_ref, right_ref, crossed_ref, *outs):
    rows, size = left_ref.shape
    half, per = size // XS, rows // YS
    first_column = pl.ds(pl.multiple_of(pos_ref[0] * half, half), half)
    for t, out in enumerate(outs):
        y = lax.rem(pos_ref[1] + t, YS)
        for n in range(per // 8):
            first = pl.ds(pl.multiple_of((n * YS + y) * 8, 8), 8)
            for h in range(XS):
                out[h * per + n * 8 : h * per + n * 8 + 8] = left_ref[
                    first, h * half : (h + 1) * half
                ]
        out[XS * per : XS * per + rows] = right_ref[:, first_column]
        out[XS * per + rows :] = crossed_ref[...]


def roots(pos, left_rows, right_rows, crossed):
    rows, size = left_rows.shape
    part = jax.ShapeDtypeStruct((rows // YS * XS + 2 * rows, size // XS), jnp.float32)
    return pl.pallas_call(
        roots_kernel,
        in_specs=smem(1) + whole(3),
        out_specs=whole(YS),
        out_shape=[part] * YS,
        compiler_params=PARAMS,
    )(pos, left_rows, right_rows, crossed)


def join_kernel(a, b, c, d, *refs):
    out = refs[-1]
    rows = out.shape[0] // YS
    for t, ref in enumerate((a, b, c, d)):
        out[t * rows : (t + 1) * rows] = ref[:rows]


def join(parts, rows, after):
    return pl.pallas_call(
        join_kernel,
        in_specs=whole(YS) + unread(len(after)),
        out_specs=whole(1)[0],
        out_shape=jax.ShapeDtypeStruct((YS * rows, parts[0].shape[1]), jnp.float32),
        compiler_params=PARAMS,
    )(*parts, *after)


def halves_kernel(whole_ref, *refs):
    part_a, part_b = refs[-2:]
    slots = part_a.shape[0] // whole_ref.shape[1]
    part_a[...] = whole_ref[:slots].reshape(part_a.shape)
    part_b[...] = whole_ref[slots:].reshape(part_b.shape)


def halves(panel, split, after):
    shards, stripe, _ = panel.shape
    outs = [
        jax.ShapeDtypeStruct((rows, LANES), jnp.float32)
        for rows in (split, shards * stripe - split)
    ]
    return pl.pallas_call(
        halves_kernel,
        in_specs=whole(1) + unread(len(after)),
        out_specs=whole(2),
        out_shape=outs,
        compiler_params=PARAMS,
    )(panel, *after)


def assemble(pos_ref, a_refs, b_refs, store):
    split = a_refs[0].shape[0]
    for n in range(XS * YS):
        k = place(pos_ref, n // YS, -(n % YS))
        columns = pl.ds(pl.multiple_of(k * LANES, LANES), LANES)
        store(slice(0, split), columns, a_refs[n][...])
        store(slice(split, None), columns, b_refs[n][...])


def assemble_roots(pos_ref, refs, left, right):
    left_x, parts = refs[0], refs[1:]
    half = left_x.shape[1]
    per, r_rows = left_x.shape[0] // (XS * YS), right.shape[0] // (XS * YS)
    for x in range(XS):
        for t in range(YS):
            k = place(pos_ref, x, -t)
            for h in range(XS):
                source = left_x[(t * XS + h) * per : (t * XS + h + 1) * per] if x else parts[t][
                    h * per : (h + 1) * per
                ]
                left[pl.ds(pl.multiple_of(k * per, per), per), h * half : (h + 1) * half] = source
            first = XS * per + x * r_rows
            right[pl.ds(pl.multiple_of(k * r_rows, r_rows), r_rows), :] = parts[t][
                first : first + r_rows
            ]


def shampoo_kernel(pos_ref, *refs):
    n = XS * YS
    g_a, g_b = named(refs[:PARTS])
    root_refs = refs[PARTS : PARTS + YS + 1]
    second_ref, out_ref, moment_ref, high, low, left, right, own = refs[PARTS + YS + 1 :]

    def store(rows, columns, value):
        high[rows, columns], low[rows, columns] = split3(value)

    assemble(pos_ref, g_a, g_b, store)
    assemble_roots(pos_ref, root_refs, left, right)

    rows = second_ref.shape[0]
    mine = place(pos_ref, 0, 0)
    parts_a = g_a[0].shape[0] // rows
    for refs_part, first, here in (
        (g_a, mine, mine < parts_a),
        (g_b, mine - parts_a, mine >= parts_a),
    ):

        @pl.when(here)
        def _():
            for m in range(n):
                k = place(pos_ref, m // YS, -(m % YS))
                own[:, pl.ds(pl.multiple_of(k * LANES, LANES), LANES)] = refs_part[m][
                    pl.ds(pl.multiple_of(first * rows, rows), rows), :
                ]

    moment = beta_two * second_ref[...] + (1.0 - beta_two) * own[...] * own[...]
    moment_ref[...] = moment
    adam = own[...] / (jnp.sqrt(moment) + adam_eps)
    adam_part = jnp.sum(adam * adam)

    mixed = dot3((high[...], low[...]), split3(right[...]), ((1,), (0,)))
    result = dot3(split3(left[...]), split3(mixed), ((1,), (0,)))
    shampoo_part = jnp.sum(result * result)

    shards, per, _ = out_ref.shape
    width = result.shape[1]
    row = lax.broadcasted_iota(jnp.int32, (per, LANES), 0)
    lane = lax.broadcasted_iota(jnp.int32, (per, LANES), 1)
    norms = jnp.where(row == 0, adam_part, jnp.where(row == 1, shampoo_part, 0.0))
    norms = jnp.where(lane == pos_ref[2], norms, 0.0)
    out_ref[:, :, :width] = result.reshape(shards, per, width)
    out_ref[:, :, width:] = jnp.broadcast_to(norms[None], (shards, per, LANES))


def shampoo(pos, g_parts, root_parts, second, shards):
    rows, size = second.shape
    half, per = size // XS, size // shards // YS
    outs = (
        jax.ShapeDtypeStruct((shards, per, half + LANES), jnp.float32),
        jax.ShapeDtypeStruct(second.shape, jnp.float32),
    )
    arrays = (*listed(g_parts), *root_parts, second)
    return pl.pallas_call(
        shampoo_kernel,
        grid=(1,),
        in_specs=smem(1) + blocks(arrays),
        out_specs=blocks(outs),
        out_shape=outs,
        scratch_shapes=[
            VMEM((size, size), jnp.bfloat16),
            VMEM((size, size), jnp.bfloat16),
            VMEM((size // YS, size), jnp.float32),
            VMEM((size, half), jnp.float32),
            VMEM((rows, size), jnp.float32),
        ],
        compiler_params=PARAMS,
    )(pos, *arrays)


def stats_kernel(pos_ref, *refs):
    left_ref, right_ref, left_out, right_out, g = refs[PARTS:]

    def store(rows, columns, value):
        g[rows, columns] = value

    assemble(pos_ref, *named(refs[:PARTS]), store)
    rows = left_ref.shape[0]
    first = pl.multiple_of(place(pos_ref, 0, 0) * rows, rows)
    every = split3(g[...])
    own_rows = split3(g[pl.ds(first, rows), :])
    own_cols = split3(g[:, pl.ds(first, rows)])
    left_out[...] = beta_two * left_ref[...] + (1.0 - beta_two) * dot3(
        own_rows, every, ((1,), (1,))
    )
    right_out[...] = beta_two * right_ref[...] + (1.0 - beta_two) * dot3(
        own_cols, every, ((0,), (0,))
    )


def statistics(pos, g_parts, left, right):
    size = left.shape[1]
    arrays = (*listed(g_parts), left, right)
    outs = (
        jax.ShapeDtypeStruct(left.shape, jnp.float32),
        jax.ShapeDtypeStruct(right.shape, jnp.float32),
    )
    return pl.pallas_call(
        stats_kernel,
        grid=(1,),
        in_specs=smem(1) + blocks(arrays),
        out_specs=blocks(outs),
        out_shape=outs,
        scratch_shapes=[VMEM((size, size), jnp.float32)],
        compiler_params=PARAMS,
        cost_estimate=pl.CostEstimate(
            flops=12 * left.shape[0] * size * size, bytes_accessed=24 * left.size, transcendentals=0
        ),
    )(pos, *arrays)


def order_kernel(pos_ref, owner_ref, *refs):
    n = XS * YS
    (a_refs, b_refs), out_ref = named(refs[:PARTS]), refs[PARTS]
    stripe, columns = out_ref.shape[1:]
    body, width = a_refs[0].shape
    per = b_refs[0].shape[0] - body
    block_cols = columns // (2 * XS * width)
    norms = b_refs[0][body:, :LANES]
    for m in range(1, n):
        norms = norms + b_refs[m][body:, :LANES]
    root = jnp.sqrt(norms)
    factors = root[0:1] / (root[1:2] + norm_eps)
    lane = lax.broadcasted_iota(jnp.int32, (1, LANES), 1)
    for j in range(block_cols):
        slot = owner_ref[pl.program_id(0) * block_cols + j]
        factor = jnp.sum(jnp.where(lane == slot, factors, 0.0))
        for m in range(n):
            x = lax.rem(pos_ref[0] + m // YS, XS)
            y = lax.rem(pos_ref[1] + YS - m % YS, YS)
            rows = pl.ds(pl.multiple_of(y * per, per), per)
            first = pl.multiple_of((j * XS + x) * 2 * width, 2 * width)
            source = pl.ds(pl.multiple_of(slot * per, per), per)
            out_ref[0, rows, pl.ds(first, width)] = a_refs[m][source] * factor
            out_ref[0, rows, pl.ds(pl.multiple_of(first + width, width), width)] = (
                b_refs[m][source] * factor
            )


def unpack_kernel(back_ref, *refs):
    part_a, part_b = refs[-2:]
    rows, width = part_a.shape
    part_a[...] = back_ref[:, :, :width].reshape(rows, width)
    part_b[:rows] = back_ref[:, :, width : 2 * width].reshape(rows, width)
    norms = jnp.sum(back_ref[:, :, 2 * width :], axis=0)
    for n in range(width // LANES):
        part_b[rows:, n * LANES : (n + 1) * LANES] = norms


def unpack(back, after):
    shards, per, size = back.shape
    width = (size - LANES) // 2
    outs = [
        jax.ShapeDtypeStruct((shards * per, width), jnp.float32),
        jax.ShapeDtypeStruct((shards * per + per, width), jnp.float32),
    ]
    return pl.pallas_call(
        unpack_kernel,
        grid=(1,),
        in_specs=blocks((back,)) + unread(len(after)),
        out_specs=blocks(outs),
        out_shape=outs,
        compiler_params=PARAMS,
    )(back, *after)


def order(pos, owner_slot, got, shape):
    block_rows, stripe, columns = shape
    fixed = lambda n: lambda i, *_: (0,) * n
    return pl.pallas_call(
        order_kernel,
        grid_spec=pltpu.PrefetchScalarGridSpec(
            num_scalar_prefetch=2,
            grid=(block_rows,),
            in_specs=[pl.BlockSpec(v.shape, fixed(v.ndim)) for v in listed(got)],
            out_specs=pl.BlockSpec((1, stripe, columns), lambda i, *_: (i, 0, 0)),
        ),
        out_shape=jax.ShapeDtypeStruct(shape, jnp.float32),
        compiler_params=PARAMS,
    )(pos, owner_slot, *listed(got))


def per_device(grads, owner_slot, left_stat, right_stat, left_root, right_root, second_moment):
    replicas = lax.axis_size("rep")
    shards = lax.axis_size("shard")
    own_rows = grads[0]
    size = own_rows.shape[1] * shards
    rep = lax.axis_index("rep")
    pos = jnp.stack([rep // YS, rep % YS, lax.axis_index("shard")]).astype(jnp.int32)

    a, b, under_way = reduce_scatter(cut(pos, owner_slot, own_rows, shards))
    crossed = crossing(pos, right_root[0], under_way)
    root_parts = roots(pos, left_root[0], right_root[0], crossed)
    summed = total(1.0 / replicas, a, b, (root_parts[0],))
    panel = lax.all_to_all(summed, "shard", 0, 0, tiled=True)
    root_parts = [root_parts[0]] + [shift(root_parts[t], 0, t) for t in (1, 2, 3)]

    g_parts = gather(*halves(panel, size * 5 // 8, ()))
    left_rows = left_root.shape[1] // YS * XS
    joined = join(root_parts, left_rows, (g_parts["b", 1, 0],))
    root_parts = [shift(joined, 1, 0)] + root_parts
    message, moment_new = shampoo(pos, g_parts, root_parts, second_moment[0], shards)
    back = lax.all_to_all(message, "shard", 0, 0, tiled=True)
    left_new, right_new = statistics(pos, g_parts, left_stat[0], right_stat[0])

    parts = gather(*unpack(back, (left_new,)))
    direction = order(pos, owner_slot, parts, own_rows.shape)
    return (direction, left_new[None], right_new[None], moment_new[None])


def solution(mesh):
    return jax.shard_map(
        per_device,
        mesh=mesh,
        in_specs=(
            P("rep", None, "shard", None),
            P(),
            P("shard", "rep", None),
            P("shard", "rep", None),
            P("shard", "rep", None),
            P("shard", "rep", None),
            P("shard", "rep", None),
        ),
        out_specs=(
            P(None, "shard", None),
            P("shard", "rep", None),
            P("shard", "rep", None),
            P("shard", "rep", None),
        ),
        check_vma=False,
    )
```

```python
import functools

import jax
import jax.numpy as jnp
from jax import lax
from jax.experimental import pallas as pl
from jax.experimental.pallas import tpu as pltpu
from jax.sharding import PartitionSpec as P

beta_two = 0.99
adam_eps = 1e-08
norm_eps = 1e-06

XS, YS = 2, 4
LANES = 128
VMEM = pltpu.VMEM
PARAMS = pltpu.CompilerParams(vmem_limit_bytes=48 * 1024 * 1024)


def shift(value, dx, dy):
    pairs = [
        (r, ((r // YS + dx) % XS) * YS + (r % YS + dy) % YS) for r in range(XS * YS)
    ]
    return lax.ppermute(value, "rep", pairs)


def whole(n):
    return [pl.BlockSpec(memory_space=VMEM)] * n


def smem(n):
    return [pl.BlockSpec(memory_space=pltpu.SMEM)] * n


def place(pos_ref, x_rel, t):
    x = lax.rem(pos_ref[0] + x_rel, XS)
    y = lax.rem(pos_ref[1] + t + YS, YS)
    return x * YS + y


def split3(value):
    high = value.astype(jnp.bfloat16)
    low = (value - high.astype(jnp.float32)).astype(jnp.bfloat16)
    return high, low


def dot3(a, b, dims):
    dot = functools.partial(
        lax.dot_general, dimension_numbers=(dims, ((), ())), preferred_element_type=jnp.float32
    )
    return dot(a[0], b[0]) + (dot(a[0], b[1]) + dot(a[1], b[0]))


def cut_kernel(pos_ref, owner_ref, g_ref, *outs):
    keep_a, send_a, keep_b, send_b = outs[:4], outs[4:8], outs[8], outs[9:12]
    i = pl.program_id(0)
    split = keep_a[0].shape[0]
    block_cols = g_ref.shape[2] // (XS * YS * LANES)

    def piece(j, x_rel, t):
        column = (j * XS * YS + place(pos_ref, x_rel, t)) * LANES
        return g_ref[0, :, pl.ds(pl.multiple_of(column, LANES), LANES)]

    for j in range(block_cols):
        slot = owner_ref[i * block_cols + j]

        @pl.when(slot < split)
        def _():
            for t in range(YS):
                keep_a[t][slot] = piece(j, 0, t)
                send_a[t][slot] = piece(j, 1, t)

        @pl.when(slot >= split)
        def _():
            for x_rel in range(XS):
                keep_b[x_rel, slot - split] = piece(j, x_rel, 0)
                for t in range(1, YS):
                    send_b[t - 1][x_rel, slot - split] = piece(j, x_rel, t)


def cut(pos, owner_slot, own_rows, slots):
    block_rows, stripe, columns = own_rows.shape
    split = (slots * 19) // 32
    shapes = [(split, stripe, LANES)] * (2 * YS)
    shapes += [(XS, slots - split, stripe, LANES)] * YS
    fixed = lambda n: lambda i, *_: (0,) * n
    return pl.pallas_call(
        cut_kernel,
        grid_spec=pltpu.PrefetchScalarGridSpec(
            num_scalar_prefetch=2,
            grid=(block_rows,),
            in_specs=[pl.BlockSpec((1, stripe, columns), lambda i, *_: (i, 0, 0))],
            out_specs=[pl.BlockSpec(s, fixed(len(s))) for s in shapes],
        ),
        out_shape=[jax.ShapeDtypeStruct(s, jnp.float32) for s in shapes],
        compiler_params=PARAMS,
    )(pos, owner_slot, own_rows)


def blocks(arrays):
    return [pl.BlockSpec(v.shape, lambda i, n=v.ndim: (0,) * n) for v in arrays]


def unread(n):
    return [pl.BlockSpec(memory_space=pl.ANY)] * n


def add_kernel(keep, first, second, third, *refs):
    away, own = refs[-2:]
    for x, out in ((1, away), (0, own)):
        out[...] = keep[x] + first[x] + second[x] + third[x]


def add(keep, got, after):
    out = jax.ShapeDtypeStruct(keep.shape[1:], jnp.float32)
    arrays = (keep, *got)
    return pl.pallas_call(
        add_kernel,
        grid=(1,),
        in_specs=blocks(arrays) + unread(len(after)),
        out_specs=blocks((out, out)),
        out_shape=(out, out),
        compiler_params=PARAMS,
    )(*arrays, *after)


def total_kernel(scale, a0, a1, a2, a3, b0, b1, *refs):
    out = refs[-1]
    split = a0.shape[0]
    out[:split] = (a0[...] + a1[...] + a2[...] + a3[...]) * scale
    out[split:] = (b0[...] + b1[...]) * scale


def total(scale, a, b, after):
    slots = a[0].shape[0] + b[0].shape[0]
    out = jax.ShapeDtypeStruct((slots, *a[0].shape[1:]), jnp.float32)
    arrays = (*a, *b)
    return pl.pallas_call(
        functools.partial(total_kernel, scale),
        grid=(1,),
        in_specs=blocks(arrays) + unread(len(after)),
        out_specs=blocks((out,))[0],
        out_shape=out,
        compiler_params=PARAMS,
    )(*arrays, *after)


def reduce_scatter(parts):
    keep_a, send_a, keep_b, send_b = parts[:4], parts[4:8], parts[8], parts[9:12]
    got_a = {t: shift(send_a[t], 1, 0) for t in (2, 1, 3, 0)}
    got_b = [shift(send_b[t - 1], 0, t) for t in (1, 3, 2)]
    sum_a = {t: keep_a[t] + got_a[t] for t in (2, 1, 3, 0)}
    last_a = {t: shift(sum_a[t], 0, t) for t in (2, 1, 3)}
    away, own = add(keep_b, got_b, (sum_a[2], sum_a[1]))
    last_b = shift(away, 1, 0)
    return (sum_a[0], last_a[2], last_a[1], last_a[3]), (own, last_b), sum_a[3]


def gather(part_a, part_b):
    got = {("a", 0, 0): part_a, ("b", 0, 0): part_b}
    for t in (1, 3, 2):
        got["a", 0, t] = shift(part_a, 0, t)
    got["b", 1, 0] = shift(part_b, 1, 0)
    got["a", 1, 0] = shift(part_a, 1, 0)
    for t in (1, 3, 2):
        got["b", 0, t] = shift(part_b, 0, t)
    for t in (1, 3, 2):
        got["a", 1, t] = shift(got["a", 0, t], 1, 0)
        got["b", 1, t] = shift(got["b", 1, 0], 0, t)
    return got


LATEST_FIRST = (
    [("b", 0, t) for t in (2, 3, 1)]
    + [(n, 1, t) for t in (2, 3, 1) for n in ("b", "a")]
    + [("a", 1, 0), ("b", 1, 0)]
    + [("a", 0, t) for t in (2, 3, 1)]
    + [("b", 0, 0), ("a", 0, 0)]
)
PARTS = len(LATEST_FIRST)


def listed(got):
    return [got[key] for key in LATEST_FIRST]


def named(refs):
    got = dict(zip(LATEST_FIRST, refs))
    return tuple([got[n, x, t] for x in range(XS) for t in range(YS)] for n in ("a", "b"))


def columns_kernel(right_ref, after_ref, out):
    for k in range(XS * YS):
        out[k] = right_ref[:, k * LANES : (k + 1) * LANES]


def columns(right_rows, after):
    rows, size = right_rows.shape
    cut = pl.pallas_call(
        columns_kernel,
        in_specs=whole(1) + unread(1),
        out_specs=whole(1)[0],
        out_shape=jax.ShapeDtypeStruct((XS * YS, rows, LANES), jnp.float32),
        compiler_params=PARAMS,
    )(right_rows, after)
    return lax.all_to_all(cut, "rep", 0, 0, tiled=True).reshape(size, LANES)


def halves_kernel(whole_ref, *refs):
    part_a, part_b = refs[-2:]
    slots = part_a.shape[0] // whole_ref.shape[1]
    part_a[...] = whole_ref[:slots].reshape(part_a.shape)
    part_b[...] = whole_ref[slots:].reshape(part_b.shape)


def halves(panel, split, after):
    shards, stripe, _ = panel.shape
    outs = [
        jax.ShapeDtypeStruct((rows, LANES), jnp.float32)
        for rows in (split, shards * stripe - split)
    ]
    return pl.pallas_call(
        halves_kernel,
        in_specs=whole(1) + unread(len(after)),
        out_specs=whole(2),
        out_shape=outs,
        compiler_params=PARAMS,
    )(panel, *after)


def assemble(pos_ref, a_refs, b_refs, store):
    split = a_refs[0].shape[0]
    for n in range(XS * YS):
        k = place(pos_ref, n // YS, -(n % YS))
        columns = pl.ds(pl.multiple_of(k * LANES, LANES), LANES)
        store(slice(0, split), columns, a_refs[n][...])
        store(slice(split, None), columns, b_refs[n][...])


def shampoo_kernel(pos_ref, *refs):
    n = XS * YS
    g_a, g_b = named(refs[:PARTS])
    left, right, second_ref, out_ref, moment_ref, high, low, own = refs[PARTS:]

    def store(rows, columns, value):
        high[rows, columns], low[rows, columns] = split3(value)

    assemble(pos_ref, g_a, g_b, store)

    rows = second_ref.shape[0]
    mine = place(pos_ref, 0, 0)
    parts_a = g_a[0].shape[0] // rows
    for refs_part, first, here in (
        (g_a, mine, mine < parts_a),
        (g_b, mine - parts_a, mine >= parts_a),
    ):

        @pl.when(here)
        def _():
            for m in range(n):
                k = place(pos_ref, m // YS, -(m % YS))
                own[:, pl.ds(pl.multiple_of(k * LANES, LANES), LANES)] = refs_part[m][
                    pl.ds(pl.multiple_of(first * rows, rows), rows), :
                ]

    moment = beta_two * second_ref[...] + (1.0 - beta_two) * own[...] * own[...]
    moment_ref[...] = moment
    adam = own[...] / (jnp.sqrt(moment) + adam_eps)
    adam_part = jnp.sum(adam * adam)

    mixed = dot3((high[...], low[...]), split3(right[...]), ((1,), (0,)))
    result = dot3(split3(left[...]), split3(mixed), ((1,), (0,)))
    shampoo_part = jnp.sum(result * result)

    shards, message, _ = out_ref.shape
    stripe = result.shape[0] // shards
    row = lax.broadcasted_iota(jnp.int32, (message - stripe, LANES), 0)
    lane = lax.broadcasted_iota(jnp.int32, (message - stripe, LANES), 1)
    norms = jnp.where(row == 0, adam_part, jnp.where(row == 1, shampoo_part, 0.0))
    norms = jnp.where(lane == pos_ref[2], norms, 0.0)
    out_ref[:, :stripe] = result.reshape(shards, stripe, LANES)
    out_ref[:, stripe:] = jnp.broadcast_to(norms[None], (shards, *norms.shape))


def shampoo(pos, g_parts, left, right, second, shards):
    rows, size = second.shape
    outs = (
        jax.ShapeDtypeStruct((shards, size // shards + 8, LANES), jnp.float32),
        jax.ShapeDtypeStruct(second.shape, jnp.float32),
    )
    arrays = (*listed(g_parts), left, right, second)
    return pl.pallas_call(
        shampoo_kernel,
        grid=(1,),
        in_specs=smem(1) + blocks(arrays),
        out_specs=blocks(outs),
        out_shape=outs,
        scratch_shapes=[
            VMEM((size, size), jnp.bfloat16),
            VMEM((size, size), jnp.bfloat16),
            VMEM((rows, size), jnp.float32),
        ],
        compiler_params=PARAMS,
    )(pos, *arrays)


def stats_kernel(pos_ref, *refs):
    left_ref, right_ref, left_out, right_out, g = refs[PARTS:]

    def store(rows, columns, value):
        g[rows, columns] = value

    assemble(pos_ref, *named(refs[:PARTS]), store)
    rows = left_ref.shape[0]
    first = pl.multiple_of(place(pos_ref, 0, 0) * rows, rows)
    every = split3(g[...])
    own_rows = split3(g[pl.ds(first, rows), :])
    own_cols = split3(g[:, pl.ds(first, rows)])
    left_out[...] = beta_two * left_ref[...] + (1.0 - beta_two) * dot3(
        own_rows, every, ((1,), (1,))
    )
    right_out[...] = beta_two * right_ref[...] + (1.0 - beta_two) * dot3(
        own_cols, every, ((0,), (0,))
    )


def statistics(pos, g_parts, left, right):
    size = left.shape[1]
    arrays = (*listed(g_parts), left, right)
    outs = (
        jax.ShapeDtypeStruct(left.shape, jnp.float32),
        jax.ShapeDtypeStruct(right.shape, jnp.float32),
    )
    return pl.pallas_call(
        stats_kernel,
        grid=(1,),
        in_specs=smem(1) + blocks(arrays),
        out_specs=blocks(outs),
        out_shape=outs,
        scratch_shapes=[VMEM((size, size), jnp.float32)],
        compiler_params=PARAMS,
        cost_estimate=pl.CostEstimate(
            flops=12 * left.shape[0] * size * size, bytes_accessed=24 * left.size, transcendentals=0
        ),
    )(pos, *arrays)


def order_kernel(pos_ref, owner_ref, *refs):
    n = XS * YS
    (a_refs, b_refs), out_ref = named(refs[:PARTS]), refs[PARTS]
    stripe, columns = out_ref.shape[1:]
    half = stripe // 2
    block_cols = columns // (n * LANES)
    body = a_refs[0].shape[0]
    norms = b_refs[0][body:]
    for m in range(1, n):
        norms = norms + b_refs[m][body:]
    root = jnp.sqrt(norms)
    factors = root[0:1] / (root[1:2] + norm_eps)
    lane = lax.broadcasted_iota(jnp.int32, (1, LANES), 1)
    for j in range(block_cols):
        slot = owner_ref[pl.program_id(0) * block_cols + j]
        factor = jnp.sum(jnp.where(lane == slot, factors, 0.0))
        rows = pl.ds(pl.multiple_of(slot * half, half), half)
        for m in range(n):
            column = (j * n + place(pos_ref, m // YS, -(m % YS))) * LANES
            columns_m = pl.ds(pl.multiple_of(column, LANES), LANES)
            out_ref[0, :half, columns_m] = a_refs[m][rows] * factor
            out_ref[0, half:, columns_m] = b_refs[m][rows] * factor


def unpack_kernel(back_ref, *refs):
    part_a, part_b = refs[-2:]
    rows = part_a.shape[0]
    half = rows // back_ref.shape[0]
    part_a[...] = back_ref[:, :half].reshape(rows, LANES)
    part_b[:rows] = back_ref[:, half : 2 * half].reshape(rows, LANES)
    part_b[rows:] = jnp.sum(back_ref[:, 2 * half :], axis=0)


def unpack(back, after):
    shards, message, _ = back.shape
    rows = shards * (message - 8) // 2
    outs = [
        jax.ShapeDtypeStruct((rows, LANES), jnp.float32),
        jax.ShapeDtypeStruct((rows + 8, LANES), jnp.float32),
    ]
    return pl.pallas_call(
        unpack_kernel,
        grid=(1,),
        in_specs=blocks((back,)) + unread(len(after)),
        out_specs=blocks(outs),
        out_shape=outs,
        compiler_params=PARAMS,
    )(back, *after)


def order(pos, owner_slot, got, shape):
    block_rows, stripe, columns = shape
    fixed = lambda n: lambda i, *_: (0,) * n
    return pl.pallas_call(
        order_kernel,
        grid_spec=pltpu.PrefetchScalarGridSpec(
            num_scalar_prefetch=2,
            grid=(block_rows,),
            in_specs=[pl.BlockSpec(v.shape, fixed(v.ndim)) for v in listed(got)],
            out_specs=pl.BlockSpec((1, stripe, columns), lambda i, *_: (i, 0, 0)),
        ),
        out_shape=jax.ShapeDtypeStruct(shape, jnp.float32),
        compiler_params=PARAMS,
    )(pos, owner_slot, *listed(got))


def per_device(grads, owner_slot, left_stat, right_stat, left_root, right_root, second_moment):
    replicas = lax.axis_size("rep")
    shards = lax.axis_size("shard")
    own_rows = grads[0]
    size = own_rows.shape[1] * shards
    rep = lax.axis_index("rep")
    pos = jnp.stack([rep // YS, rep % YS, lax.axis_index("shard")]).astype(jnp.int32)

    a, b, under_way = reduce_scatter(cut(pos, owner_slot, own_rows, shards))
    left = lax.all_gather(left_root[0], "rep", axis=0, tiled=True)
    right = columns(right_root[0], under_way)
    summed = total(1.0 / replicas, a, b, ())
    panel = lax.all_to_all(summed, "shard", 0, 0, tiled=True)
    g_parts = gather(*halves(panel, size // 2, (right,)))
    message, moment_new = shampoo(pos, g_parts, left, right, second_moment[0], shards)
    back = lax.all_to_all(message, "shard", 0, 0, tiled=True)
    left_new, right_new = statistics(pos, g_parts, left_stat[0], right_stat[0])

    parts = gather(*unpack(back, (left_new,)))
    direction = order(pos, owner_slot, parts, own_rows.shape)
    return (direction, left_new[None], right_new[None], moment_new[None])


def solution(mesh):
    return jax.shard_map(
        per_device,
        mesh=mesh,
        in_specs=(
            P("rep", None, "shard", None),
            P(),
            P("shard", "rep", None),
            P("shard", "rep", None),
            P("shard", "rep", None),
            P("shard", "rep", None),
            P("shard", "rep", None),
        ),
        out_specs=(
            P(None, "shard", None),
            P("shard", "rep", None),
            P("shard", "rep", None),
            P("shard", "rep", None),
        ),
        check_vma=False,
    )
```

```python
import functools

import jax
import jax.numpy as jnp
from jax import lax
from jax.experimental import pallas as pl
from jax.experimental.pallas import tpu as pltpu
from jax.sharding import PartitionSpec as P

beta_two = 0.99
adam_eps = 1e-08
norm_eps = 1e-06

XS, YS = 2, 4
LANES = 128
VMEM = pltpu.VMEM
PARAMS = pltpu.CompilerParams(vmem_limit_bytes=48 * 1024 * 1024)
SMALL = pltpu.CompilerParams(vmem_limit_bytes=32 * 1024 * 1024)


def shift(value, dx, dy):
    pairs = [
        (r, ((r // YS + dx) % XS) * YS + (r % YS + dy) % YS) for r in range(XS * YS)
    ]
    return lax.ppermute(value, "rep", pairs)


def whole(n):
    return [pl.BlockSpec(memory_space=VMEM)] * n


def smem(n):
    return [pl.BlockSpec(memory_space=pltpu.SMEM)] * n


def place(pos_ref, x_rel, t):
    x = lax.rem(pos_ref[0] + x_rel, XS)
    y = lax.rem(pos_ref[1] + t + YS, YS)
    return x * YS + y


def split3(value):
    high = value.astype(jnp.bfloat16)
    low = (value - high.astype(jnp.float32)).astype(jnp.bfloat16)
    return high, low


def dot3(a, b, dims):
    dot = functools.partial(
        lax.dot_general, dimension_numbers=(dims, ((), ())), preferred_element_type=jnp.float32
    )
    return dot(a[0], b[0]) + (dot(a[0], b[1]) + dot(a[1], b[0]))


def cut_kernel(pos_ref, owner_ref, g_ref, *outs):
    keep_a, send_a, keep_b, send_b = outs[:4], outs[4:8], outs[8], outs[9:12]
    i = pl.program_id(0)
    split = keep_a[0].shape[0]
    block_cols = g_ref.shape[2] // (XS * YS * LANES)

    def piece(j, x_rel, t):
        column = (j * XS * YS + place(pos_ref, x_rel, t)) * LANES
        return g_ref[0, :, pl.ds(pl.multiple_of(column, LANES), LANES)]

    for j in range(block_cols):
        slot = owner_ref[i * block_cols + j]

        @pl.when(slot < split)
        def _():
            for t in range(YS):
                keep_a[t][slot] = piece(j, 0, t)
                send_a[t][slot] = piece(j, 1, t)

        @pl.when(slot >= split)
        def _():
            for x_rel in range(XS):
                keep_b[x_rel, slot - split] = piece(j, x_rel, 0)
                for t in range(1, YS):
                    send_b[t - 1][x_rel, slot - split] = piece(j, x_rel, t)


def cut(pos, owner_slot, own_rows, slots):
    block_rows, stripe, columns = own_rows.shape
    split = (slots * 19) // 32
    shapes = [(split, stripe, LANES)] * (2 * YS)
    shapes += [(XS, slots - split, stripe, LANES)] * YS
    fixed = lambda n: lambda i, *_: (0,) * n
    return pl.pallas_call(
        cut_kernel,
        grid_spec=pltpu.PrefetchScalarGridSpec(
            num_scalar_prefetch=2,
            grid=(block_rows,),
            in_specs=[pl.BlockSpec((1, stripe, columns), lambda i, *_: (i, 0, 0))],
            out_specs=[pl.BlockSpec(s, fixed(len(s))) for s in shapes],
        ),
        out_shape=[jax.ShapeDtypeStruct(s, jnp.float32) for s in shapes],
        compiler_params=PARAMS,
    )(pos, owner_slot, own_rows)


def blocks(arrays):
    return [pl.BlockSpec(v.shape, lambda i, n=v.ndim: (0,) * n) for v in arrays]


def unread(n):
    return [pl.BlockSpec(memory_space=pl.ANY)] * n


def add_kernel(keep, first, second, third, *refs):
    away, own = refs[-2:]
    for x, out in ((1, away), (0, own)):
        out[...] = keep[x] + first[x] + second[x] + third[x]


def add(keep, got, after):
    out = jax.ShapeDtypeStruct(keep.shape[1:], jnp.float32)
    arrays = (keep, *got)
    return pl.pallas_call(
        add_kernel,
        grid=(1,),
        in_specs=blocks(arrays) + unread(len(after)),
        out_specs=blocks((out, out)),
        out_shape=(out, out),
        compiler_params=PARAMS,
    )(*arrays, *after)


def total_kernel(scale, a0, a1, a2, a3, b0, b1, *refs):
    out = refs[-1]
    split = a0.shape[0]
    out[:split] = (a0[...] + a1[...] + a2[...] + a3[...]) * scale
    out[split:] = (b0[...] + b1[...]) * scale


def total(scale, a, b, after):
    slots = a[0].shape[0] + b[0].shape[0]
    out = jax.ShapeDtypeStruct((slots, *a[0].shape[1:]), jnp.float32)
    arrays = (*a, *b)
    return pl.pallas_call(
        functools.partial(total_kernel, scale),
        grid=(1,),
        in_specs=blocks(arrays) + unread(len(after)),
        out_specs=blocks((out,))[0],
        out_shape=out,
        compiler_params=PARAMS,
    )(*arrays, *after)


def reduce_scatter(parts):
    keep_a, send_a, keep_b, send_b = parts[:4], parts[4:8], parts[8], parts[9:12]
    got_a = {t: shift(send_a[t], 1, 0) for t in (2, 1, 3, 0)}
    got_b = [shift(send_b[t - 1], 0, t) for t in (1, 3, 2)]
    sum_a = {t: keep_a[t] + got_a[t] for t in (2, 1, 3, 0)}
    last_a = {t: shift(sum_a[t], 0, t) for t in (2, 1, 3)}
    away, own = add(keep_b, got_b, (sum_a[2], sum_a[1]))
    last_b = shift(away, 1, 0)
    return (sum_a[0], last_a[2], last_a[1], last_a[3]), (own, last_b), sum_a[3]


def gather(part_a, part_b):
    got = {("a", 0, 0): part_a, ("b", 0, 0): part_b}
    for t in (1, 3, 2):
        got["a", 0, t] = shift(part_a, 0, t)
    got["b", 1, 0] = shift(part_b, 1, 0)
    got["a", 1, 0] = shift(part_a, 1, 0)
    for t in (1, 3, 2):
        got["b", 0, t] = shift(part_b, 0, t)
    for t in (1, 3, 2):
        got["a", 1, t] = shift(got["a", 0, t], 1, 0)
        got["b", 1, t] = shift(got["b", 1, 0], 0, t)
    return got


LATEST_FIRST = (
    [("b", 0, t) for t in (2, 3, 1)]
    + [(n, 1, t) for t in (2, 3, 1) for n in ("b", "a")]
    + [("a", 1, 0), ("b", 1, 0)]
    + [("a", 0, t) for t in (2, 3, 1)]
    + [("b", 0, 0), ("a", 0, 0)]
)
PARTS = len(LATEST_FIRST)


def listed(got):
    return [got[key] for key in LATEST_FIRST]


def named(refs):
    got = dict(zip(LATEST_FIRST, refs))
    return tuple([got[n, x, t] for x in range(XS) for t in range(YS)] for n in ("a", "b"))


def columns_kernel(right_ref, after_ref, out):
    for k in range(XS * YS):
        out[k] = right_ref[:, k * LANES : (k + 1) * LANES]


def columns(right_rows, after):
    rows, size = right_rows.shape
    cut = pl.pallas_call(
        columns_kernel,
        in_specs=whole(1) + unread(1),
        out_specs=whole(1)[0],
        out_shape=jax.ShapeDtypeStruct((XS * YS, rows, LANES), jnp.float32),
        compiler_params=PARAMS,
    )(right_rows, after)
    return lax.all_to_all(cut, "rep", 0, 0, tiled=True).reshape(size, LANES)


def halves_kernel(whole_ref, *refs):
    part_a, part_b = refs[-2:]
    slots = part_a.shape[0] // whole_ref.shape[1]
    part_a[...] = whole_ref[:slots].reshape(part_a.shape)
    part_b[...] = whole_ref[slots:].reshape(part_b.shape)


def halves(panel, split, after):
    shards, stripe, _ = panel.shape
    outs = [
        jax.ShapeDtypeStruct((rows, LANES), jnp.float32)
        for rows in (split, shards * stripe - split)
    ]
    return pl.pallas_call(
        halves_kernel,
        in_specs=whole(1) + unread(len(after)),
        out_specs=whole(2),
        out_shape=outs,
        compiler_params=PARAMS,
    )(panel, *after)


def in_hbm(n):
    return [pl.BlockSpec(memory_space=pltpu.HBM)] * n


def panels(pos_ref, refs, g, sems):
    copies = []
    for key, ref in zip(LATEST_FIRST, refs):
        name, x, t = key
        k = place(pos_ref, x, -t)
        rows = ref.shape[0]
        first = 0 if name == "a" else g.shape[0] - rows
        target = g.at[pl.ds(first, rows), pl.ds(pl.multiple_of(k * LANES, LANES), LANES)]
        copies.append(pltpu.make_async_copy(ref, target, sems.at[len(copies)]))
    return copies


def shampoo_kernel(pos_ref, *refs):
    left_in, right_in, second_in, out_ref, moment_ref, g_out, *scratch = refs[PARTS:]
    g, left, right, second, sems = scratch
    others = [
        pltpu.make_async_copy(source, target, sems.at[PARTS + n])
        for n, (source, target) in enumerate(
            ((right_in, right), (second_in, second), (left_in, left))
        )
    ]
    copies = panels(pos_ref, refs[:PARTS], g, sems)
    for copy in copies + others:
        copy.start()
    for copy in copies + others[:2]:
        copy.wait()
    keep = pltpu.make_async_copy(g, g_out, sems.at[PARTS + 3])
    keep.start()

    mixed = dot3(split3(g[...]), split3(right[...]), ((1,), (0,)))

    rows = second.shape[0]
    own = g[pl.ds(pl.multiple_of(place(pos_ref, 0, 0) * rows, rows), rows), :]
    moment = beta_two * second[...] + (1.0 - beta_two) * own * own
    moment_ref[...] = moment
    adam = own / (jnp.sqrt(moment) + adam_eps)
    adam_part = jnp.sum(adam * adam)

    others[2].wait()
    result = dot3(split3(left[...]), split3(mixed), ((1,), (0,)))
    shampoo_part = jnp.sum(result * result)

    shards, message, _ = out_ref.shape
    stripe = result.shape[0] // shards
    row = lax.broadcasted_iota(jnp.int32, (message - stripe, LANES), 0)
    lane = lax.broadcasted_iota(jnp.int32, (message - stripe, LANES), 1)
    norms = jnp.where(row == 0, adam_part, jnp.where(row == 1, shampoo_part, 0.0))
    norms = jnp.where(lane == pos_ref[2], norms, 0.0)
    out_ref[:, :stripe] = result.reshape(shards, stripe, LANES)
    out_ref[:, stripe:] = jnp.broadcast_to(norms[None], (shards, *norms.shape))
    keep.wait()


def shampoo(pos, g_parts, left, right, second, shards):
    rows, size = second.shape
    outs = (
        jax.ShapeDtypeStruct((shards, size // shards + 8, LANES), jnp.float32),
        jax.ShapeDtypeStruct(second.shape, jnp.float32),
        jax.ShapeDtypeStruct((size, size), jnp.float32),
    )
    arrays = (*listed(g_parts), left, right, second)
    return pl.pallas_call(
        shampoo_kernel,
        in_specs=smem(1) + in_hbm(len(arrays)),
        out_specs=whole(2) + in_hbm(1),
        out_shape=outs,
        scratch_shapes=[
            VMEM((size, size), jnp.float32),
            VMEM((size, size), jnp.float32),
            VMEM(right.shape, jnp.float32),
            VMEM(second.shape, jnp.float32),
            pltpu.SemaphoreType.DMA((PARTS + 4,)),
        ],
        compiler_params=SMALL,
    )(pos, *arrays)


def stats_kernel(pos_ref, g, left_ref, right_ref, left_out, right_out):
    rows = left_ref.shape[0]
    first = pl.multiple_of(place(pos_ref, 0, 0) * rows, rows)
    every = split3(g[...])
    own_rows = split3(g[pl.ds(first, rows), :])
    own_cols = split3(g[:, pl.ds(first, rows)])
    left_out[...] = beta_two * left_ref[...] + (1.0 - beta_two) * dot3(
        own_rows, every, ((1,), (1,))
    )
    right_out[...] = beta_two * right_ref[...] + (1.0 - beta_two) * dot3(
        own_cols, every, ((0,), (0,))
    )


def statistics(pos, g, left, right):
    size = left.shape[1]
    arrays = (g, left, right)
    outs = (
        jax.ShapeDtypeStruct(left.shape, jnp.float32),
        jax.ShapeDtypeStruct(right.shape, jnp.float32),
    )
    return pl.pallas_call(
        stats_kernel,
        grid=(1,),
        in_specs=smem(1) + blocks(arrays),
        out_specs=blocks(outs),
        out_shape=outs,
        compiler_params=PARAMS,
        cost_estimate=pl.CostEstimate(
            flops=12 * left.shape[0] * size * size, bytes_accessed=24 * left.size, transcendentals=0
        ),
    )(pos, *arrays)


def order_kernel(pos_ref, owner_ref, *refs):
    n = XS * YS
    (a_refs, b_refs), out_ref = named(refs[:PARTS]), refs[PARTS]
    stripe, columns = out_ref.shape[1:]
    half = stripe // 2
    block_cols = columns // (n * LANES)
    body = a_refs[0].shape[0]
    norms = b_refs[0][body:]
    for m in range(1, n):
        norms = norms + b_refs[m][body:]
    root = jnp.sqrt(norms)
    factors = root[0:1] / (root[1:2] + norm_eps)
    lane = lax.broadcasted_iota(jnp.int32, (1, LANES), 1)
    for j in range(block_cols):
        slot = owner_ref[pl.program_id(0) * block_cols + j]
        factor = jnp.sum(jnp.where(lane == slot, factors, 0.0))
        rows = pl.ds(pl.multiple_of(slot * half, half), half)
        for m in range(n):
            column = (j * n + place(pos_ref, m // YS, -(m % YS))) * LANES
            columns_m = pl.ds(pl.multiple_of(column, LANES), LANES)
            out_ref[0, :half, columns_m] = a_refs[m][rows] * factor
            out_ref[0, half:, columns_m] = b_refs[m][rows] * factor


def unpack_kernel(back_ref, *refs):
    part_a, part_b = refs[-2:]
    rows = part_a.shape[0]
    half = rows // back_ref.shape[0]
    part_a[...] = back_ref[:, :half].reshape(rows, LANES)
    part_b[:rows] = back_ref[:, half : 2 * half].reshape(rows, LANES)
    part_b[rows:] = jnp.sum(back_ref[:, 2 * half :], axis=0)


def unpack(back, after):
    shards, message, _ = back.shape
    rows = shards * (message - 8) // 2
    outs = [
        jax.ShapeDtypeStruct((rows, LANES), jnp.float32),
        jax.ShapeDtypeStruct((rows + 8, LANES), jnp.float32),
    ]
    return pl.pallas_call(
        unpack_kernel,
        grid=(1,),
        in_specs=blocks((back,)) + unread(len(after)),
        out_specs=blocks(outs),
        out_shape=outs,
        compiler_params=PARAMS,
    )(back, *after)


def order(pos, owner_slot, got, shape):
    block_rows, stripe, columns = shape
    fixed = lambda n: lambda i, *_: (0,) * n
    return pl.pallas_call(
        order_kernel,
        grid_spec=pltpu.PrefetchScalarGridSpec(
            num_scalar_prefetch=2,
            grid=(block_rows,),
            in_specs=[pl.BlockSpec(v.shape, fixed(v.ndim)) for v in listed(got)],
            out_specs=pl.BlockSpec((1, stripe, columns), lambda i, *_: (i, 0, 0)),
        ),
        out_shape=jax.ShapeDtypeStruct(shape, jnp.float32),
        compiler_params=PARAMS,
    )(pos, owner_slot, *listed(got))


def per_device(grads, owner_slot, left_stat, right_stat, left_root, right_root, second_moment):
    replicas = lax.axis_size("rep")
    shards = lax.axis_size("shard")
    own_rows = grads[0]
    size = own_rows.shape[1] * shards
    rep = lax.axis_index("rep")
    pos = jnp.stack([rep // YS, rep % YS, lax.axis_index("shard")]).astype(jnp.int32)

    a, b, under_way = reduce_scatter(cut(pos, owner_slot, own_rows, shards))
    left = lax.all_gather(left_root[0], "rep", axis=0, tiled=True)
    right = columns(right_root[0], under_way)
    summed = total(1.0 / replicas, a, b, ())
    panel = lax.all_to_all(summed, "shard", 0, 0, tiled=True)
    g_parts = gather(*halves(panel, size // 2, (right,)))
    message, moment_new, gradient = shampoo(pos, g_parts, left, right, second_moment[0], shards)
    back = lax.all_to_all(message, "shard", 0, 0, tiled=True)
    left_new, right_new = statistics(pos, gradient, left_stat[0], right_stat[0])

    parts = gather(*unpack(back, (left_new,)))
    direction = order(pos, owner_slot, parts, own_rows.shape)
    return (direction, left_new[None], right_new[None], moment_new[None])


def solution(mesh):
    return jax.shard_map(
        per_device,
        mesh=mesh,
        in_specs=(
            P("rep", None, "shard", None),
            P(),
            P("shard", "rep", None),
            P("shard", "rep", None),
            P("shard", "rep", None),
            P("shard", "rep", None),
            P("shard", "rep", None),
        ),
        out_specs=(
            P(None, "shard", None),
            P("shard", "rep", None),
            P("shard", "rep", None),
            P("shard", "rep", None),
        ),
        check_vma=False,
    )
```

```python
import functools

import jax
import jax.numpy as jnp
from jax import lax
from jax.experimental import pallas as pl
from jax.experimental.pallas import tpu as pltpu
from jax.sharding import PartitionSpec as P

beta_two = 0.99
adam_eps = 1e-08
norm_eps = 1e-06

XS, YS = 2, 4
LANES = 128
VMEM = pltpu.VMEM
PARAMS = pltpu.CompilerParams(vmem_limit_bytes=48 * 1024 * 1024)
FULL = pltpu.CompilerParams(vmem_limit_bytes=62 * 1024 * 1024)


def shift(value, dx, dy):
    pairs = [
        (r, ((r // YS + dx) % XS) * YS + (r % YS + dy) % YS) for r in range(XS * YS)
    ]
    return lax.ppermute(value, "rep", pairs)


def whole(n):
    return [pl.BlockSpec(memory_space=VMEM)] * n


def smem(n):
    return [pl.BlockSpec(memory_space=pltpu.SMEM)] * n


def place(pos_ref, x_rel, t):
    x = lax.rem(pos_ref[0] + x_rel, XS)
    y = lax.rem(pos_ref[1] + t + YS, YS)
    return x * YS + y


def split3(value):
    high = value.astype(jnp.bfloat16)
    low = (value - high.astype(jnp.float32)).astype(jnp.bfloat16)
    return high, low


def dot3(a, b, dims):
    dot = functools.partial(
        lax.dot_general, dimension_numbers=(dims, ((), ())), preferred_element_type=jnp.float32
    )
    return dot(a[0], b[0]) + (dot(a[0], b[1]) + dot(a[1], b[0]))


def cut_kernel(pos_ref, owner_ref, g_ref, *outs):
    keep_a, send_a, keep_b, send_b = outs[:4], outs[4:8], outs[8], outs[9:12]
    i = pl.program_id(0)
    split = keep_a[0].shape[0]
    block_cols = g_ref.shape[2] // (XS * YS * LANES)

    def piece(j, x_rel, t):
        column = (j * XS * YS + place(pos_ref, x_rel, t)) * LANES
        return g_ref[0, :, pl.ds(pl.multiple_of(column, LANES), LANES)]

    for j in range(block_cols):
        slot = owner_ref[i * block_cols + j]

        @pl.when(slot < split)
        def _():
            for t in range(YS):
                keep_a[t][slot] = piece(j, 0, t)
                send_a[t][slot] = piece(j, 1, t)

        @pl.when(slot >= split)
        def _():
            for x_rel in range(XS):
                keep_b[x_rel, slot - split] = piece(j, x_rel, 0)
                for t in range(1, YS):
                    send_b[t - 1][x_rel, slot - split] = piece(j, x_rel, t)


def cut(pos, owner_slot, own_rows, slots):
    block_rows, stripe, columns = own_rows.shape
    split = (slots * 19) // 32
    shapes = [(split, stripe, LANES)] * (2 * YS)
    shapes += [(XS, slots - split, stripe, LANES)] * YS
    fixed = lambda n: lambda i, *_: (0,) * n
    return pl.pallas_call(
        cut_kernel,
        grid_spec=pltpu.PrefetchScalarGridSpec(
            num_scalar_prefetch=2,
            grid=(block_rows,),
            in_specs=[pl.BlockSpec((1, stripe, columns), lambda i, *_: (i, 0, 0))],
            out_specs=[pl.BlockSpec(s, fixed(len(s))) for s in shapes],
        ),
        out_shape=[jax.ShapeDtypeStruct(s, jnp.float32) for s in shapes],
        compiler_params=PARAMS,
    )(pos, owner_slot, own_rows)


def blocks(arrays):
    return [pl.BlockSpec(v.shape, lambda i, n=v.ndim: (0,) * n) for v in arrays]


def unread(n):
    return [pl.BlockSpec(memory_space=pl.ANY)] * n


def add_kernel(keep, first, second, third, *refs):
    away, own = refs[-2:]
    for x, out in ((1, away), (0, own)):
        out[...] = keep[x] + first[x] + second[x] + third[x]


def add(keep, got, after):
    out = jax.ShapeDtypeStruct(keep.shape[1:], jnp.float32)
    arrays = (keep, *got)
    return pl.pallas_call(
        add_kernel,
        grid=(1,),
        in_specs=blocks(arrays) + unread(len(after)),
        out_specs=blocks((out, out)),
        out_shape=(out, out),
        compiler_params=PARAMS,
    )(*arrays, *after)


def total_kernel(scale, a0, a1, a2, a3, b0, b1, *refs):
    out = refs[-1]
    split = a0.shape[0]
    out[:split] = (a0[...] + a1[...] + a2[...] + a3[...]) * scale
    out[split:] = (b0[...] + b1[...]) * scale


def total(scale, a, b, after):
    slots = a[0].shape[0] + b[0].shape[0]
    out = jax.ShapeDtypeStruct((slots, *a[0].shape[1:]), jnp.float32)
    arrays = (*a, *b)
    return pl.pallas_call(
        functools.partial(total_kernel, scale),
        grid=(1,),
        in_specs=blocks(arrays) + unread(len(after)),
        out_specs=blocks((out,))[0],
        out_shape=out,
        compiler_params=PARAMS,
    )(*arrays, *after)


def reduce_scatter(parts):
    keep_a, send_a, keep_b, send_b = parts[:4], parts[4:8], parts[8], parts[9:12]
    got_a = {t: shift(send_a[t], 1, 0) for t in (2, 1, 3, 0)}
    got_b = [shift(send_b[t - 1], 0, t) for t in (1, 3, 2)]
    sum_a = {t: keep_a[t] + got_a[t] for t in (2, 1, 3, 0)}
    last_a = {t: shift(sum_a[t], 0, t) for t in (2, 1, 3)}
    away, own = add(keep_b, got_b, (sum_a[2], sum_a[1]))
    last_b = shift(away, 1, 0)
    return (sum_a[0], last_a[2], last_a[1], last_a[3]), (own, last_b), sum_a[3]


def gather(part_a, part_b):
    got = {("a", 0, 0): part_a, ("b", 0, 0): part_b}
    for t in (1, 3, 2):
        got["a", 0, t] = shift(part_a, 0, t)
    got["b", 1, 0] = shift(part_b, 1, 0)
    got["a", 1, 0] = shift(part_a, 1, 0)
    for t in (1, 3, 2):
        got["b", 0, t] = shift(part_b, 0, t)
    for t in (1, 3, 2):
        got["a", 1, t] = shift(got["a", 0, t], 1, 0)
        got["b", 1, t] = shift(got["b", 1, 0], 0, t)
    return got


LATEST_FIRST = (
    [("b", 0, t) for t in (2, 3, 1)]
    + [(n, 1, t) for t in (2, 3, 1) for n in ("b", "a")]
    + [("a", 1, 0), ("b", 1, 0)]
    + [("a", 0, t) for t in (2, 3, 1)]
    + [("b", 0, 0), ("a", 0, 0)]
)
PARTS = len(LATEST_FIRST)


def listed(got):
    return [got[key] for key in LATEST_FIRST]


def named(refs):
    got = dict(zip(LATEST_FIRST, refs))
    return tuple([got[n, x, t] for x in range(XS) for t in range(YS)] for n in ("a", "b"))


def columns_kernel(right_ref, after_ref, out):
    for k in range(XS * YS):
        out[k] = right_ref[:, k * LANES : (k + 1) * LANES]


def columns(right_rows, after):
    rows, size = right_rows.shape
    cut = pl.pallas_call(
        columns_kernel,
        in_specs=whole(1) + unread(1),
        out_specs=whole(1)[0],
        out_shape=jax.ShapeDtypeStruct((XS * YS, rows, LANES), jnp.float32),
        compiler_params=PARAMS,
    )(right_rows, after)
    return lax.all_to_all(cut, "rep", 0, 0, tiled=True).reshape(size, LANES)


def halves_kernel(whole_ref, *refs):
    part_a, part_b = refs[-2:]
    slots = part_a.shape[0] // whole_ref.shape[1]
    part_a[...] = whole_ref[:slots].reshape(part_a.shape)
    part_b[...] = whole_ref[slots:].reshape(part_b.shape)


def halves(panel, split, after):
    shards, stripe, _ = panel.shape
    outs = [
        jax.ShapeDtypeStruct((rows, LANES), jnp.float32)
        for rows in (split, shards * stripe - split)
    ]
    return pl.pallas_call(
        halves_kernel,
        in_specs=whole(1) + unread(len(after)),
        out_specs=whole(2),
        out_shape=outs,
        compiler_params=PARAMS,
    )(panel, *after)


def in_hbm(n):
    return [pl.BlockSpec(memory_space=pltpu.HBM)] * n


def panels(pos_ref, refs, g, sems):
    copies = []
    for key, ref in zip(LATEST_FIRST, refs):
        name, x, t = key
        k = place(pos_ref, x, -t)
        rows = ref.shape[0]
        first = 0 if name == "a" else g.shape[0] - rows
        target = g.at[pl.ds(first, rows), pl.ds(pl.multiple_of(k * LANES, LANES), LANES)]
        copies.append(pltpu.make_async_copy(ref, target, sems.at[len(copies)]))
    return copies


def shampoo_kernel(pos_ref, *refs):
    left_in, right_in, second_in, out_ref, moment_ref, g_out, *scratch = refs[PARTS:]
    g, left, right, second, sems = scratch
    others = [
        pltpu.make_async_copy(source, target, sems.at[PARTS + n])
        for n, (source, target) in enumerate(
            ((right_in, right), (second_in, second), (left_in, left))
        )
    ]
    copies = panels(pos_ref, refs[:PARTS], g, sems)
    for copy in copies + others:
        copy.start()
    for copy in copies + others[:2]:
        copy.wait()
    keep = pltpu.make_async_copy(g, g_out, sems.at[PARTS + 3])
    keep.start()

    mixed = dot3(split3(g[...]), split3(right[...]), ((1,), (0,)))

    rows = second.shape[0]
    own = g[pl.ds(pl.multiple_of(place(pos_ref, 0, 0) * rows, rows), rows), :]
    moment = beta_two * second[...] + (1.0 - beta_two) * own * own
    moment_ref[...] = moment
    adam = own / (jnp.sqrt(moment) + adam_eps)
    adam_part = jnp.sum(adam * adam)

    others[2].wait()
    result = dot3(split3(left[...]), split3(mixed), ((1,), (0,)))
    shampoo_part = jnp.sum(result * result)

    shards, message, _ = out_ref.shape
    stripe = result.shape[0] // shards
    row = lax.broadcasted_iota(jnp.int32, (message - stripe, LANES), 0)
    lane = lax.broadcasted_iota(jnp.int32, (message - stripe, LANES), 1)
    norms = jnp.where(row == 0, adam_part, jnp.where(row == 1, shampoo_part, 0.0))
    norms = jnp.where(lane == pos_ref[2], norms, 0.0)
    out_ref[:, :stripe] = result.reshape(shards, stripe, LANES)
    out_ref[:, stripe:] = jnp.broadcast_to(norms[None], (shards, *norms.shape))
    keep.wait()


def shampoo(pos, g_parts, left, right, second, shards):
    rows, size = second.shape
    outs = (
        jax.ShapeDtypeStruct((shards, size // shards + 8, LANES), jnp.float32),
        jax.ShapeDtypeStruct(second.shape, jnp.float32),
        jax.ShapeDtypeStruct((size, size), jnp.float32),
    )
    arrays = (*listed(g_parts), left, right, second)
    return pl.pallas_call(
        shampoo_kernel,
        in_specs=smem(1) + in_hbm(len(arrays)),
        out_specs=whole(2) + in_hbm(1),
        out_shape=outs,
        scratch_shapes=[
            VMEM((size, size), jnp.float32),
            VMEM((size, size), jnp.float32),
            VMEM(right.shape, jnp.float32),
            VMEM(second.shape, jnp.float32),
            pltpu.SemaphoreType.DMA((PARTS + 4,)),
        ],
        compiler_params=FULL,
    )(pos, *arrays)


def stats_kernel(pos_ref, g, left_ref, right_ref, left_out, right_out):
    rows = left_ref.shape[0]
    first = pl.multiple_of(place(pos_ref, 0, 0) * rows, rows)
    every = split3(g[...])
    own_rows = split3(g[pl.ds(first, rows), :])
    own_cols = split3(g[:, pl.ds(first, rows)])
    left_out[...] = beta_two * left_ref[...] + (1.0 - beta_two) * dot3(
        own_rows, every, ((1,), (1,))
    )
    right_out[...] = beta_two * right_ref[...] + (1.0 - beta_two) * dot3(
        own_cols, every, ((0,), (0,))
    )


def statistics(pos, g, left, right):
    size = left.shape[1]
    arrays = (g, left, right)
    outs = (
        jax.ShapeDtypeStruct(left.shape, jnp.float32),
        jax.ShapeDtypeStruct(right.shape, jnp.float32),
    )
    return pl.pallas_call(
        stats_kernel,
        grid=(1,),
        in_specs=smem(1) + blocks(arrays),
        out_specs=blocks(outs),
        out_shape=outs,
        compiler_params=FULL,
        cost_estimate=pl.CostEstimate(
            flops=12 * left.shape[0] * size * size, bytes_accessed=24 * left.size, transcendentals=0
        ),
    )(pos, *arrays)


def order_kernel(pos_ref, owner_ref, *refs):
    n = XS * YS
    (a_refs, b_refs), out_ref = named(refs[:PARTS]), refs[PARTS]
    stripe, columns = out_ref.shape[1:]
    half = stripe // 2
    block_cols = columns // (n * LANES)
    body = a_refs[0].shape[0]
    norms = b_refs[0][body:]
    for m in range(1, n):
        norms = norms + b_refs[m][body:]
    root = jnp.sqrt(norms)
    factors = root[0:1] / (root[1:2] + norm_eps)
    lane = lax.broadcasted_iota(jnp.int32, (1, LANES), 1)
    for j in range(block_cols):
        slot = owner_ref[pl.program_id(0) * block_cols + j]
        factor = jnp.sum(jnp.where(lane == slot, factors, 0.0))
        rows = pl.ds(pl.multiple_of(slot * half, half), half)
        for m in range(n):
            column = (j * n + place(pos_ref, m // YS, -(m % YS))) * LANES
            columns_m = pl.ds(pl.multiple_of(column, LANES), LANES)
            out_ref[0, :half, columns_m] = a_refs[m][rows] * factor
            out_ref[0, half:, columns_m] = b_refs[m][rows] * factor


def unpack_kernel(back_ref, *refs):
    part_a, part_b = refs[-2:]
    rows = part_a.shape[0]
    half = rows // back_ref.shape[0]
    part_a[...] = back_ref[:, :half].reshape(rows, LANES)
    part_b[:rows] = back_ref[:, half : 2 * half].reshape(rows, LANES)
    part_b[rows:] = jnp.sum(back_ref[:, 2 * half :], axis=0)


def unpack(back, after):
    shards, message, _ = back.shape
    rows = shards * (message - 8) // 2
    outs = [
        jax.ShapeDtypeStruct((rows, LANES), jnp.float32),
        jax.ShapeDtypeStruct((rows + 8, LANES), jnp.float32),
    ]
    return pl.pallas_call(
        unpack_kernel,
        grid=(1,),
        in_specs=blocks((back,)) + unread(len(after)),
        out_specs=blocks(outs),
        out_shape=outs,
        compiler_params=PARAMS,
    )(back, *after)


def order(pos, owner_slot, got, shape):
    block_rows, stripe, columns = shape
    fixed = lambda n: lambda i, *_: (0,) * n
    return pl.pallas_call(
        order_kernel,
        grid_spec=pltpu.PrefetchScalarGridSpec(
            num_scalar_prefetch=2,
            grid=(block_rows,),
            in_specs=[pl.BlockSpec(v.shape, fixed(v.ndim)) for v in listed(got)],
            out_specs=pl.BlockSpec((1, stripe, columns), lambda i, *_: (i, 0, 0)),
        ),
        out_shape=jax.ShapeDtypeStruct(shape, jnp.float32),
        compiler_params=PARAMS,
    )(pos, owner_slot, *listed(got))


def per_device(grads, owner_slot, left_stat, right_stat, left_root, right_root, second_moment):
    replicas = lax.axis_size("rep")
    shards = lax.axis_size("shard")
    own_rows = grads[0]
    size = own_rows.shape[1] * shards
    rep = lax.axis_index("rep")
    pos = jnp.stack([rep // YS, rep % YS, lax.axis_index("shard")]).astype(jnp.int32)

    a, b, under_way = reduce_scatter(cut(pos, owner_slot, own_rows, shards))
    left = lax.all_gather(left_root[0], "rep", axis=0, tiled=True)
    right = columns(right_root[0], under_way)
    summed = total(1.0 / replicas, a, b, ())
    panel = lax.all_to_all(summed, "shard", 0, 0, tiled=True)
    g_parts = gather(*halves(panel, size * 15 // 32, (right,)))
    message, moment_new, gradient = shampoo(pos, g_parts, left, right, second_moment[0], shards)
    back = lax.all_to_all(message, "shard", 0, 0, tiled=True)
    left_new, right_new = statistics(pos, gradient, left_stat[0], right_stat[0])

    parts = gather(*unpack(back, (left_new,)))
    direction = order(pos, owner_slot, parts, own_rows.shape)
    return (direction, left_new[None], right_new[None], moment_new[None])


def solution(mesh):
    return jax.shard_map(
        per_device,
        mesh=mesh,
        in_specs=(
            P("rep", None, "shard", None),
            P(),
            P("shard", "rep", None),
            P("shard", "rep", None),
            P("shard", "rep", None),
            P("shard", "rep", None),
            P("shard", "rep", None),
        ),
        out_specs=(
            P(None, "shard", None),
            P("shard", "rep", None),
            P("shard", "rep", None),
            P("shard", "rep", None),
        ),
        check_vma=False,
    )
```

```python
import functools

import jax
import jax.numpy as jnp
from jax import lax
from jax.experimental import pallas as pl
from jax.experimental.pallas import tpu as pltpu
from jax.sharding import PartitionSpec as P

beta_two = 0.99
adam_eps = 1e-08
norm_eps = 1e-06

XS, YS = 2, 4
LANES = 128
VMEM = pltpu.VMEM
PARAMS = pltpu.CompilerParams(vmem_limit_bytes=48 * 1024 * 1024)
FULL = pltpu.CompilerParams(vmem_limit_bytes=62 * 1024 * 1024)


def shift(value, dx, dy):
    pairs = [
        (r, ((r // YS + dx) % XS) * YS + (r % YS + dy) % YS) for r in range(XS * YS)
    ]
    return lax.ppermute(value, "rep", pairs)


def whole(n):
    return [pl.BlockSpec(memory_space=VMEM)] * n


def smem(n):
    return [pl.BlockSpec(memory_space=pltpu.SMEM)] * n


def place(pos_ref, x_rel, t):
    x = lax.rem(pos_ref[0] + x_rel, XS)
    y = lax.rem(pos_ref[1] + t + YS, YS)
    return x * YS + y


def split3(value):
    high = value.astype(jnp.bfloat16)
    low = (value - high.astype(jnp.float32)).astype(jnp.bfloat16)
    return high, low


def dot3(a, b, dims):
    dot = functools.partial(
        lax.dot_general, dimension_numbers=(dims, ((), ())), preferred_element_type=jnp.float32
    )
    return dot(a[0], b[0]) + (dot(a[0], b[1]) + dot(a[1], b[0]))


def cut_kernel(pos_ref, owner_ref, g_ref, *outs):
    keep_a, send_a, keep_b, send_b = outs[:4], outs[4:8], outs[8], outs[9:12]
    i = pl.program_id(0)
    split = keep_a[0].shape[0]
    block_cols = g_ref.shape[2] // (XS * YS * LANES)

    def piece(j, x_rel, t):
        column = (j * XS * YS + place(pos_ref, x_rel, t)) * LANES
        return g_ref[0, :, pl.ds(pl.multiple_of(column, LANES), LANES)]

    for j in range(block_cols):
        slot = owner_ref[i * block_cols + j]

        @pl.when(slot < split)
        def _():
            for t in range(YS):
                keep_a[t][slot] = piece(j, 0, t)
                send_a[t][slot] = piece(j, 1, t)

        @pl.when(slot >= split)
        def _():
            for x_rel in range(XS):
                keep_b[x_rel, slot - split] = piece(j, x_rel, 0)
                for t in range(1, YS):
                    send_b[t - 1][x_rel, slot - split] = piece(j, x_rel, t)


def cut(pos, owner_slot, own_rows, slots):
    block_rows, stripe, columns = own_rows.shape
    split = (slots * 19) // 32
    shapes = [(split, stripe, LANES)] * (2 * YS)
    shapes += [(XS, slots - split, stripe, LANES)] * YS
    fixed = lambda n: lambda i, *_: (0,) * n
    return pl.pallas_call(
        cut_kernel,
        grid_spec=pltpu.PrefetchScalarGridSpec(
            num_scalar_prefetch=2,
            grid=(block_rows,),
            in_specs=[pl.BlockSpec((1, stripe, columns), lambda i, *_: (i, 0, 0))],
            out_specs=[pl.BlockSpec(s, fixed(len(s))) for s in shapes],
        ),
        out_shape=[jax.ShapeDtypeStruct(s, jnp.float32) for s in shapes],
        compiler_params=PARAMS,
    )(pos, owner_slot, own_rows)


def blocks(arrays):
    return [pl.BlockSpec(v.shape, lambda i, n=v.ndim: (0,) * n) for v in arrays]


def unread(n):
    return [pl.BlockSpec(memory_space=pl.ANY)] * n


def add_kernel(keep, first, second, third, *refs):
    away, own = refs[-2:]
    for x, out in ((1, away), (0, own)):
        out[...] = keep[x] + first[x] + second[x] + third[x]


def add(keep, got, after):
    out = jax.ShapeDtypeStruct(keep.shape[1:], jnp.float32)
    arrays = (keep, *got)
    return pl.pallas_call(
        add_kernel,
        grid=(1,),
        in_specs=blocks(arrays) + unread(len(after)),
        out_specs=blocks((out, out)),
        out_shape=(out, out),
        compiler_params=PARAMS,
    )(*arrays, *after)


def total_kernel(scale, a0, a1, a2, a3, b0, b1, *refs):
    out = refs[-1]
    split = a0.shape[0]
    out[:split] = (a0[...] + a1[...] + a2[...] + a3[...]) * scale
    out[split:] = (b0[...] + b1[...]) * scale


def total(scale, a, b, after):
    slots = a[0].shape[0] + b[0].shape[0]
    out = jax.ShapeDtypeStruct((slots, *a[0].shape[1:]), jnp.float32)
    arrays = (*a, *b)
    return pl.pallas_call(
        functools.partial(total_kernel, scale),
        grid=(1,),
        in_specs=blocks(arrays) + unread(len(after)),
        out_specs=blocks((out,))[0],
        out_shape=out,
        compiler_params=PARAMS,
    )(*arrays, *after)


def reduce_scatter(parts):
    keep_a, send_a, keep_b, send_b = parts[:4], parts[4:8], parts[8], parts[9:12]
    got_a = {t: shift(send_a[t], 1, 0) for t in (2, 1, 3, 0)}
    got_b = [shift(send_b[t - 1], 0, t) for t in (1, 3, 2)]
    sum_a = {t: keep_a[t] + got_a[t] for t in (2, 1, 3, 0)}
    last_a = {t: shift(sum_a[t], 0, t) for t in (2, 1, 3)}
    away, own = add(keep_b, got_b, (sum_a[2], sum_a[1]))
    last_b = shift(away, 1, 0)
    return (sum_a[0], last_a[2], last_a[1], last_a[3]), (own, last_b), sum_a[3]


def gather(part_a, part_b):
    got = {("a", 0, 0): part_a, ("b", 0, 0): part_b}
    for t in (1, 3, 2):
        got["a", 0, t] = shift(part_a, 0, t)
    got["b", 1, 0] = shift(part_b, 1, 0)
    got["a", 1, 0] = shift(part_a, 1, 0)
    for t in (1, 3, 2):
        got["b", 0, t] = shift(part_b, 0, t)
    for t in (1, 3, 2):
        got["a", 1, t] = shift(got["a", 0, t], 1, 0)
        got["b", 1, t] = shift(got["b", 1, 0], 0, t)
    return got


LATEST_FIRST = (
    [("b", 0, t) for t in (2, 3, 1)]
    + [(n, 1, t) for t in (2, 3, 1) for n in ("b", "a")]
    + [("a", 1, 0), ("b", 1, 0)]
    + [("a", 0, t) for t in (2, 3, 1)]
    + [("b", 0, 0), ("a", 0, 0)]
)
PARTS = len(LATEST_FIRST)


def listed(got):
    return [got[key] for key in LATEST_FIRST]


def named(refs):
    got = dict(zip(LATEST_FIRST, refs))
    return tuple([got[n, x, t] for x in range(XS) for t in range(YS)] for n in ("a", "b"))


def columns_kernel(right_ref, after_ref, out):
    for k in range(XS * YS):
        out[k] = right_ref[:, k * LANES : (k + 1) * LANES]


def columns(right_rows, after):
    rows, size = right_rows.shape
    cut = pl.pallas_call(
        columns_kernel,
        in_specs=whole(1) + unread(1),
        out_specs=whole(1)[0],
        out_shape=jax.ShapeDtypeStruct((XS * YS, rows, LANES), jnp.float32),
        compiler_params=PARAMS,
    )(right_rows, after)
    return lax.all_to_all(cut, "rep", 0, 0, tiled=True).reshape(size, LANES)


def halves_kernel(whole_ref, *refs):
    part_a, part_b = refs[-2:]
    slots = part_a.shape[0] // whole_ref.shape[1]
    part_a[...] = whole_ref[:slots].reshape(part_a.shape)
    part_b[...] = whole_ref[slots:].reshape(part_b.shape)


def halves(panel, split, after):
    shards, stripe, _ = panel.shape
    outs = [
        jax.ShapeDtypeStruct((rows, LANES), jnp.float32)
        for rows in (split, shards * stripe - split)
    ]
    return pl.pallas_call(
        halves_kernel,
        in_specs=whole(1) + unread(len(after)),
        out_specs=whole(2),
        out_shape=outs,
        compiler_params=PARAMS,
    )(panel, *after)


def in_hbm(n):
    return [pl.BlockSpec(memory_space=pltpu.HBM)] * n


def panels(pos_ref, refs, g, sems):
    copies = []
    for key, ref in zip(LATEST_FIRST, refs):
        name, x, t = key
        k = place(pos_ref, x, -t)
        rows = ref.shape[0]
        first = 0 if name == "a" else g.shape[0] - rows
        target = g.at[pl.ds(first, rows), pl.ds(pl.multiple_of(k * LANES, LANES), LANES)]
        copies.append(pltpu.make_async_copy(ref, target, sems.at[len(copies)]))
    return copies


def shampoo_kernel(pos_ref, *refs):
    left_in, right_in, second_in, out_ref, moment_ref, g_out, *scratch = refs[PARTS:]
    g, left, right, second, sems = scratch
    others = [
        pltpu.make_async_copy(source, target, sems.at[PARTS + n])
        for n, (source, target) in enumerate(
            ((right_in, right), (second_in, second), (left_in, left))
        )
    ]
    copies = panels(pos_ref, refs[:PARTS], g, sems)
    for copy in copies + others:
        copy.start()
    for copy in copies + others[:2]:
        copy.wait()
    keep = pltpu.make_async_copy(g, g_out, sems.at[PARTS + 3])
    keep.start()

    mixed = dot3(split3(g[...]), split3(right[...]), ((1,), (0,)))

    rows = second.shape[0]
    own = g[pl.ds(pl.multiple_of(place(pos_ref, 0, 0) * rows, rows), rows), :]
    moment = beta_two * second[...] + (1.0 - beta_two) * own * own
    moment_ref[...] = moment
    adam = own / (jnp.sqrt(moment) + adam_eps)
    adam_part = jnp.sum(adam * adam)

    others[2].wait()
    result = dot3(split3(left[...]), split3(mixed), ((1,), (0,)))
    shampoo_part = jnp.sum(result * result)

    shards, message, _ = out_ref.shape
    stripe = result.shape[0] // shards
    row = lax.broadcasted_iota(jnp.int32, (message - stripe, LANES), 0)
    lane = lax.broadcasted_iota(jnp.int32, (message - stripe, LANES), 1)
    norms = jnp.where(row == 0, adam_part, jnp.where(row == 1, shampoo_part, 0.0))
    norms = jnp.where(lane == pos_ref[2], norms, 0.0)
    out_ref[:, :stripe] = result.reshape(shards, stripe, LANES)
    out_ref[:, stripe:] = jnp.broadcast_to(norms[None], (shards, *norms.shape))
    keep.wait()


def shampoo(pos, g_parts, left, right, second, shards):
    rows, size = second.shape
    outs = (
        jax.ShapeDtypeStruct((shards, size // shards + 8, LANES), jnp.float32),
        jax.ShapeDtypeStruct(second.shape, jnp.float32),
        jax.ShapeDtypeStruct((size, size), jnp.float32),
    )
    arrays = (*listed(g_parts), left, right, second)
    return pl.pallas_call(
        shampoo_kernel,
        in_specs=smem(1) + in_hbm(len(arrays)),
        out_specs=whole(2) + in_hbm(1),
        out_shape=outs,
        scratch_shapes=[
            VMEM((size, size), jnp.float32),
            VMEM((size, size), jnp.float32),
            VMEM(right.shape, jnp.float32),
            VMEM(second.shape, jnp.float32),
            pltpu.SemaphoreType.DMA((PARTS + 4,)),
        ],
        compiler_params=FULL,
    )(pos, *arrays)


def stats_kernel(pos_ref, g, left_ref, right_ref, left_out, right_out):
    rows = left_ref.shape[0]
    first = pl.multiple_of(place(pos_ref, 0, 0) * rows, rows)
    every = split3(g[...])
    own_rows = split3(g[pl.ds(first, rows), :])
    own_cols = split3(g[:, pl.ds(first, rows)])
    left_out[...] = beta_two * left_ref[...] + (1.0 - beta_two) * dot3(
        own_rows, every, ((1,), (1,))
    )
    right_out[...] = beta_two * right_ref[...] + (1.0 - beta_two) * dot3(
        own_cols, every, ((0,), (0,))
    )


def statistics(pos, g, left, right):
    size = left.shape[1]
    arrays = (g, left, right)
    outs = (
        jax.ShapeDtypeStruct(left.shape, jnp.float32),
        jax.ShapeDtypeStruct(right.shape, jnp.float32),
    )
    return pl.pallas_call(
        stats_kernel,
        grid=(1,),
        in_specs=smem(1) + blocks(arrays),
        out_specs=blocks(outs),
        out_shape=outs,
        compiler_params=FULL,
        cost_estimate=pl.CostEstimate(
            flops=12 * left.shape[0] * size * size, bytes_accessed=24 * left.size, transcendentals=0
        ),
    )(pos, *arrays)


def order_kernel(pos_ref, owner_ref, *refs):
    n = XS * YS
    (a_refs, b_refs), out_ref = named(refs[:PARTS]), refs[PARTS]
    stripe, columns = out_ref.shape[1:]
    half = stripe // 2
    block_cols = columns // (n * LANES)
    body = a_refs[0].shape[0]
    norms = b_refs[0][body:]
    for m in range(1, n):
        norms = norms + b_refs[m][body:]
    root = jnp.sqrt(norms)
    factors = root[0:1] / (root[1:2] + norm_eps)
    lane = lax.broadcasted_iota(jnp.int32, (1, LANES), 1)
    for j in range(block_cols):
        slot = owner_ref[pl.program_id(0) * block_cols + j]
        factor = jnp.sum(jnp.where(lane == slot, factors, 0.0))
        rows = pl.ds(pl.multiple_of(slot * half, half), half)
        for m in range(n):
            column = (j * n + place(pos_ref, m // YS, -(m % YS))) * LANES
            columns_m = pl.ds(pl.multiple_of(column, LANES), LANES)
            out_ref[0, :half, columns_m] = a_refs[m][rows] * factor
            out_ref[0, half:, columns_m] = b_refs[m][rows] * factor


def unpack_kernel(back_ref, *refs):
    part_a, part_b = refs[-2:]
    rows = part_a.shape[0]
    half = rows // back_ref.shape[0]
    part_a[...] = back_ref[:, :half].reshape(rows, LANES)
    part_b[:rows] = back_ref[:, half : 2 * half].reshape(rows, LANES)
    part_b[rows:] = jnp.sum(back_ref[:, 2 * half :], axis=0)


def unpack(back, after):
    shards, message, _ = back.shape
    rows = shards * (message - 8) // 2
    outs = [
        jax.ShapeDtypeStruct((rows, LANES), jnp.float32),
        jax.ShapeDtypeStruct((rows + 8, LANES), jnp.float32),
    ]
    return pl.pallas_call(
        unpack_kernel,
        grid=(1,),
        in_specs=blocks((back,)) + unread(len(after)),
        out_specs=blocks(outs),
        out_shape=outs,
        compiler_params=PARAMS,
    )(back, *after)


def order(pos, owner_slot, got, shape):
    block_rows, stripe, columns = shape
    fixed = lambda n: lambda i, *_: (0,) * n
    return pl.pallas_call(
        order_kernel,
        grid_spec=pltpu.PrefetchScalarGridSpec(
            num_scalar_prefetch=2,
            grid=(block_rows,),
            in_specs=[pl.BlockSpec(v.shape, fixed(v.ndim)) for v in listed(got)],
            out_specs=pl.BlockSpec((1, stripe, columns), lambda i, *_: (i, 0, 0)),
        ),
        out_shape=jax.ShapeDtypeStruct(shape, jnp.float32),
        compiler_params=PARAMS,
    )(pos, owner_slot, *listed(got))


def per_device(grads, owner_slot, left_stat, right_stat, left_root, right_root, second_moment):
    replicas = lax.axis_size("rep")
    shards = lax.axis_size("shard")
    own_rows = grads[0]
    size = own_rows.shape[1] * shards
    rep = lax.axis_index("rep")
    pos = jnp.stack([rep // YS, rep % YS, lax.axis_index("shard")]).astype(jnp.int32)

    a, b, under_way = reduce_scatter(cut(pos, owner_slot, own_rows, shards))
    left = lax.all_gather(left_root[0], "rep", axis=0, tiled=True)
    right = columns(right_root[0], own_rows)
    summed = total(1.0 / replicas, a, b, ())
    panel = lax.all_to_all(summed, "shard", 0, 0, tiled=True)
    g_parts = gather(*halves(panel, size * 15 // 32, ()))
    message, moment_new, gradient = shampoo(pos, g_parts, left, right, second_moment[0], shards)
    back = lax.all_to_all(message, "shard", 0, 0, tiled=True)
    left_new, right_new = statistics(pos, gradient, left_stat[0], right_stat[0])

    parts = gather(*unpack(back, (left_new,)))
    direction = order(pos, owner_slot, parts, own_rows.shape)
    return (direction, left_new[None], right_new[None], moment_new[None])


def solution(mesh):
    return jax.shard_map(
        per_device,
        mesh=mesh,
        in_specs=(
            P("rep", None, "shard", None),
            P(),
            P("shard", "rep", None),
            P("shard", "rep", None),
            P("shard", "rep", None),
            P("shard", "rep", None),
            P("shard", "rep", None),
        ),
        out_specs=(
            P(None, "shard", None),
            P("shard", "rep", None),
            P("shard", "rep", None),
            P("shard", "rep", None),
        ),
        check_vma=False,
    )
```
